32 devices in a mesh: groups: 2 (over x), cols: 16 (over z, y, core).
Axes of the slice: x: 2, y: 2, z: 4, core: 2. Of those that a mesh axis runs over, the one named last changes fastest.
Arguments:
- image_feats: bfloat16 [64, 16384], P('groups', 'cols'), parts along dimension 0, may hold values from -6 to 6
- teacher: bfloat16 [64, 256, 512], P('groups', 'cols'), parts along dimension 0, may hold values from -40 to 40
- w_first: bfloat16 [128, 576], P('cols'), may hold values from -0.25 to 0.25
- w_middle: bfloat16 [128, 1152], P('cols'), may hold values from -0.1875 to 0.1875
- w_last: bfloat16 [512, 1152], P('cols'), may hold values from -0.1875 to 0.1875
Outputs:
- grad_first: float32 [256, 576], P(('groups', 'cols')), parts along dimension 0
- grad_middle: float32 [256, 1152], P(('groups', 'cols')), parts along dimension 0
- grad_last: float32 [1024, 1152], P(('groups', 'cols')), parts along dimension 0
The draws below stay inside these ranges and needn't reach their ends.
There are 2 independent parts, one for each index of `groups`. The reference program is written for one: setup_inputs(seed, part) draws one part's arguments, and reference() takes and returns one part's arrays. A program takes and returns all parts, laid end to end along the dimension named above; an argument that names none is the same for every part. Nothing has to cross between parts.
All inputs are finite; a program needn't handle non-finite values.
Results may differ from the reference program's by a relative error of at most 0.012.
Values may be sent and summed in bfloat16 or wider, within the bound.
No kernel may reach another device: no remote copies, remote signals or barrier semaphores. Data moves between devices by JAX's collectives and lax.ppermute only.
A program may use at most 64 MiB of HBM per device.

```python
import jax
import jax.numpy as jnp
from jax import lax

C_IN = 64
WIDTH = 128
TEACHER_CH = 512
ROWS = 32
COLS = 256


def draw_teacher(key, part):
    base_key = jax.random.fold_in(key, 7)
    value_key, order_key = jax.random.split(base_key, 2)
    ranking = jax.random.permutation(order_key, TEACHER_CH)
    channel_scale = jnp.power(10.0, ranking.astype(jnp.float32) / (TEACHER_CH - 1))
    values = jnp.clip(jax.random.normal(value_key, (ROWS, COLS, TEACHER_CH), jnp.float32), -4.0, 4.0)
    return (values * channel_scale).astype(jnp.bfloat16)


def block_levels(stream_key, shape, cuts, smallest, high):
    level, own = 1.0, jax.random.fold_in(stream_key, 6)
    for axis_at, blocks in cuts:
        steps = jnp.exp(jax.random.uniform(jax.random.fold_in(own, axis_at), (blocks,), jnp.float32, smallest / len(cuts), high / len(cuts)))
        level = level * jnp.repeat(steps, shape[axis_at] // blocks).reshape([-1 if axis == axis_at else 1 for axis in range(len(shape))])
    return level


def normal_values(own_key, dims, deviation, reach, pieces=(), kind=jnp.bfloat16):
    values = deviation * jax.random.normal(own_key, dims, jnp.float32)
    if pieces:
        values = values * block_levels(own_key, dims, pieces, -0.22, 0.18)
    return jnp.clip(values, -reach, reach).astype(kind)


def setup_inputs(seed: int = 0, part: int = 0) -> dict:
    keys = jax.random.split(jax.random.key(seed), 6)
    own_keys = jax.random.split(jax.random.fold_in(keys[5], part), 6)
    image_feats = normal_values(own_keys[0], (ROWS, COLS * C_IN), 1.0, 6.0, ((1, 16),))
    teacher = draw_teacher(jax.random.fold_in(jax.random.fold_in(keys[5], part), 71), part)
    w_first = normal_values(keys[2], (WIDTH, 9 * C_IN), (9 * C_IN) ** -0.5, 0.25, ((0, 16),))
    w_middle = normal_values(keys[3], (WIDTH, 9 * WIDTH), (9 * WIDTH) ** -0.5, 0.1875, ((0, 16),))
    w_last = normal_values(keys[4], (TEACHER_CH, 9 * WIDTH), (9 * WIDTH) ** -0.5, 0.1875, ((0, 16),))
    return dict(image_feats=image_feats, teacher=teacher, w_first=w_first, w_middle=w_middle, w_last=w_last)


epsilon = 1e-06

def to_kernel(weight, depth):
    outputs = weight.shape[0]
    return weight.astype(jnp.float32).reshape(outputs, 3, 3, depth).transpose(1, 2, 3, 0)

def from_kernel(kernel):
    return kernel.transpose(3, 0, 1, 2).reshape(kernel.shape[3], -1)

def conv_layer(inputs, kernel, spread):
    result = lax.conv_general_dilated(inputs[None], kernel, (1, 1), [(spread, spread), (spread, spread)], rhs_dilation=(spread, spread), dimension_numbers=('NHWC', 'HWIO', 'NHWC'), precision=lax.Precision.HIGHEST)
    return result[0]

def silu_slope(pre):
    sigma = jax.nn.sigmoid(pre)
    return sigma * (1.0 + pre * (1.0 - sigma))

def reference(image_feats, teacher, w_first, w_middle, w_last):
    stem = image_feats.reshape(ROWS, COLS, C_IN).astype(jnp.float32)
    kernel_first = to_kernel(w_first, C_IN)
    kernel_middle = to_kernel(w_middle, WIDTH)
    kernel_last = to_kernel(w_last, WIDTH)
    first_pre = conv_layer(stem, kernel_first, 2)
    first_act = jax.nn.silu(first_pre).astype(jnp.bfloat16)
    second_pre = conv_layer(first_act.astype(jnp.float32), kernel_middle, 4)
    second_act = jax.nn.silu(second_pre).astype(jnp.bfloat16)
    student = conv_layer(second_act.astype(jnp.float32), kernel_last, 8)
    s_norm = jnp.sqrt(lax.optimization_barrier(jnp.sum(student * student, -1, keepdims=True)) + epsilon)
    target = teacher.astype(jnp.float32)
    t_norm = jnp.sqrt(lax.optimization_barrier(jnp.sum(target * target, -1, keepdims=True)) + epsilon)
    s_unit = student / s_norm
    differ = s_unit - target / t_norm
    slope = ((differ - s_unit * lax.optimization_barrier(jnp.sum(s_unit * differ, -1, keepdims=True))) / s_norm).astype(jnp.bfloat16)
    unused, back_last = jax.vjp(lambda acts, kern: conv_layer(acts, kern, 8), second_act.astype(jnp.float32), kernel_last)
    back_second, kgrad_last = back_last(slope.astype(jnp.float32))
    slope_second = (back_second * silu_slope(second_pre)).astype(jnp.bfloat16)
    unused, back_middle = jax.vjp(lambda acts, kern: conv_layer(acts, kern, 4), first_act.astype(jnp.float32), kernel_middle)
    back_first, kgrad_middle = back_middle(slope_second.astype(jnp.float32))
    slope_first = (back_first * silu_slope(first_pre)).astype(jnp.bfloat16)
    unused, back_stem = jax.vjp(lambda kern: conv_layer(stem, kern, 2), kernel_first)
    kgrad_first = back_stem(slope_first.astype(jnp.float32))[0]
    return (from_kernel(kgrad_first), from_kernel(kgrad_middle), from_kernel(kgrad_last))
```

```python
import functools

import jax
import jax.numpy as jnp
from jax import lax
from jax.experimental import pallas as pl
from jax.experimental.pallas import tpu as pltpu
from jax.sharding import PartitionSpec as P

epsilon = 1e-06
bf16, f32 = jnp.bfloat16, jnp.float32
VMEM_LIMIT = 48 * 1024 * 1024
HALO_X, HALO_FIRST, HALO_SECOND, HALO_SLOPE, HALO_BACK = 13, 12, 10, 6, 2


def swap(array, mask):
    size = lax.axis_size("cols")
    return lax.ppermute(array, "cols", [(i, i ^ mask) for i in range(size)])


def shift(array, step):
    size = lax.axis_size("cols")
    return lax.ppermute(
        array, "cols", [(i, i + step) for i in range(size) if 0 <= i + step < size]
    )


def in_order(pieces, at):
    count = len(pieces)
    if count == 1:
        return pieces[0]
    half = count // 2
    low = in_order(pieces[:half], at % half)
    high = in_order(pieces[half:], at % half)
    return jnp.where(
        at < half, jnp.concatenate([low, high], 0), jnp.concatenate([high, low], 0)
    )


def pick(array, at):
    return lax.dynamic_index_in_dim(array, at, 0, keepdims=False)


def gather_rows(shard, me):
    size = lax.axis_size("cols")
    far = size // 4
    held = in_order([shard[None]] + [swap(shard, 4 * k)[None] for k in range(1, far)], me // 4)
    other = swap(held, 2)
    held = jnp.where(
        (me // 2) % 2 == 0, jnp.stack([held, other], 1), jnp.stack([other, held], 1)
    )
    other = swap(held, 1)
    held = jnp.where(me % 2 == 0, jnp.stack([held, other], 2), jnp.stack([other, held], 2))
    return held.reshape(size * shard.shape[0], shard.shape[1])


def scatter_rows(terms, me):
    size = lax.axis_size("cols")
    far = size // 4
    rows = terms.shape[0] // size
    held = terms.reshape(far, 2, 2, rows, terms.shape[1])
    core = me % 2
    mine = lax.dynamic_index_in_dim(held, core, 2, keepdims=False)
    theirs = lax.dynamic_index_in_dim(held, 1 - core, 2, keepdims=False)
    held = mine.astype(f32) + swap(theirs.astype(bf16), 1).astype(f32)
    row = (me // 2) % 2
    mine = lax.dynamic_index_in_dim(held, row, 1, keepdims=False)
    theirs = lax.dynamic_index_in_dim(held, 1 - row, 1, keepdims=False)
    held = mine + swap(theirs.astype(bf16), 2).astype(f32)
    place = me // 4
    sent = held.astype(bf16)
    total = pick(held, place)
    for k in range(1, far):
        total = total + swap(pick(sent, place ^ k), 4 * k).astype(f32)
    return total


def row_shifted(value, step, rows):
    count = value.shape[0]
    if step == 0:
        return value
    row = lax.broadcasted_iota(jnp.int32, (count, 1), 0) % rows + step
    rolled = pltpu.roll(value, (-step) % count, 0)
    return jnp.where((row >= 0) & (row < rows), rolled, 0.0)


def inside(count, rows, first, total):
    col = lax.broadcasted_iota(jnp.int32, (count, 1), 0) // rows + first
    return (col >= 0) & (col < total)


def dot(a, b, contract):
    return lax.dot_general(a, b, (contract, ((), ())), preferred_element_type=f32)


def put_patch(patch_ref, value, step, rows, out_cols):
    depth = value.shape[1]
    for ky in range(3):
        moved = row_shifted(value, (ky - 1) * step, rows).astype(bf16)
        for kx in range(3):
            tap = 3 * ky + kx
            start = kx * step * rows
            patch_ref[:, tap * depth : (tap + 1) * depth] = moved[start : start + out_cols * rows]


def front_kernel(
    own,
    rows,
    total,
    band_ref,
    xcol_ref,
    teacher_ref,
    w_first_ref,
    w_middle_ref,
    w_last_ref,
    grad_last_ref,
    slope_ref,
    tilt_first_ref,
    tilt_second_ref,
    patch_middle_ref,
    patch_last_ref,
    student_ref,
):
    first_col = band_ref[0] * own
    n_first, n_second, n_slope = (
        own + 2 * HALO_FIRST,
        own + 2 * HALO_SECOND,
        own + 2 * HALO_SLOPE,
    )
    pre = dot(xcol_ref[...], w_first_ref[...], ((1,), (1,)))
    sigma = 1.0 / (1.0 + jnp.exp(-pre))
    act = jnp.where(
        inside(n_first * rows, rows, first_col - HALO_FIRST, total), pre * sigma, 0.0
    )
    lo = HALO_FIRST * rows
    pre_own, sigma_own = pre[lo : lo + own * rows], sigma[lo : lo + own * rows]
    tilt_first_ref[...] = sigma_own * (1.0 + pre_own * (1.0 - sigma_own))
    put_patch(patch_middle_ref, act, 2, rows, n_second)

    pre = dot(patch_middle_ref[...], w_middle_ref[...], ((1,), (1,)))
    sigma = 1.0 / (1.0 + jnp.exp(-pre))
    act = jnp.where(
        inside(n_second * rows, rows, first_col - HALO_SECOND, total), pre * sigma, 0.0
    )
    lo, n_back = (HALO_SECOND - HALO_BACK) * rows, (own + 2 * HALO_BACK) * rows
    pre_back, sigma_back = pre[lo : lo + n_back], sigma[lo : lo + n_back]
    tilt_second_ref[...] = jnp.where(
        inside(n_back, rows, first_col - HALO_BACK, total),
        sigma_back * (1.0 + pre_back * (1.0 - sigma_back)),
        0.0,
    )
    put_patch(patch_last_ref, act, 4, rows, n_slope)

    student_ref[...] = dot(patch_last_ref[...], w_last_ref[...], ((1,), (1,)))
    block = 4 * rows

    def slopes(step, carry):
        at = pl.ds(pl.multiple_of(step * block, block), block)
        student = student_ref[at, :]
        s_inv = lax.rsqrt(jnp.sum(student * student, -1, keepdims=True) + epsilon)
        target = teacher_ref[at, :].astype(f32)
        t_inv = lax.rsqrt(jnp.sum(target * target, -1, keepdims=True) + epsilon)
        s_unit = student * s_inv
        differ = s_unit - target * t_inv
        slope = (differ - s_unit * jnp.sum(s_unit * differ, -1, keepdims=True)) * s_inv
        ok = inside(block, rows, first_col - HALO_SLOPE + step * (block // rows), total)
        slope_ref[at, :] = jnp.where(ok, slope, 0.0).astype(bf16)
        return carry

    lax.fori_loop(0, n_slope * rows // block, slopes, 0)
    lo, n_own = HALO_SLOPE * rows, own * rows
    grad_last_ref[...] = dot(
        slope_ref[lo : lo + n_own, :], patch_last_ref[lo : lo + n_own, :], ((0,), (0,))
    ).astype(bf16)


def spread_back(parts_ref, step, rows, out_cols):
    depth = parts_ref.shape[1] // 9
    total = None
    for ky in range(3):
        line = None
        for kx in range(3):
            tap = 3 * ky + kx
            start = (2 - kx) * step * rows
            piece = parts_ref[start : start + out_cols * rows, tap * depth : (tap + 1) * depth]
            line = piece if line is None else line + piece
        line = row_shifted(line, (1 - ky) * step, rows)
        total = line if total is None else total + line
    return total


def back_kernel(
    own,
    rows,
    xcol_ref,
    slope_ref,
    tilt_first_ref,
    tilt_second_ref,
    patch_middle_ref,
    w_middle_ref,
    w_last_ref,
    grad_first_ref,
    grad_middle_ref,
    parts_last_ref,
    parts_middle_ref,
):
    n_own, n_back = own * rows, (own + 2 * HALO_BACK) * rows
    parts_last_ref[...] = dot(slope_ref[...], w_last_ref[...], ((1,), (0,)))
    back_second = spread_back(parts_last_ref, 4, rows, own + 2 * HALO_BACK)
    slope_second = (back_second * tilt_second_ref[...]).astype(bf16)
    lo, hi = HALO_BACK * rows, HALO_SECOND * rows
    grad_middle_ref[...] = dot(
        slope_second[lo : lo + n_own], patch_middle_ref[hi : hi + n_own, :], ((0,), (0,))
    ).astype(bf16)
    parts_middle_ref[...] = dot(slope_second, w_middle_ref[...], ((1,), (0,)))
    back_first = spread_back(parts_middle_ref, 2, rows, own)
    slope_first = (back_first * tilt_first_ref[...]).astype(bf16)
    hi = HALO_FIRST * rows
    grad_first_ref[...] = dot(slope_first, xcol_ref[hi : hi + n_own, :], ((0,), (0,))).astype(bf16)


def on_device(image_feats, teacher, w_first, w_middle, w_last):
    size = lax.axis_size("cols")
    me = lax.axis_index("cols")
    height, breadth, channels = teacher.shape
    in_depth = w_first.shape[1] // 9
    hidden = w_middle.shape[1] // 9
    rows, piece = height // 2, breadth // 2
    own = 4 * piece
    total = own * (size // 4)

    small = gather_rows(jnp.concatenate([w_first, w_middle], 1), me)
    kernel_last = gather_rows(w_last, me)
    kernel_first, kernel_middle = small[:, : 9 * in_depth], small[:, 9 * in_depth :]

    cells = jnp.concatenate([teacher, image_feats.reshape(height, breadth, in_depth)], 2)
    classes = cells.reshape(rows, 2, piece, 2, -1).transpose(3, 1, 2, 0, 4)
    classes = classes.reshape(4, piece, rows, -1)
    low = me % 4
    band = in_order([pick(classes, low)] + [swap(pick(classes, low ^ k), k) for k in (1, 2, 3)], low)
    x_band, t_band = band[:, :, channels:], band[:, :, :channels]

    def widen(array, halo):
        before = shift(array[own - halo :], 4)
        after = shift(array[:halo], -4)
        return jnp.concatenate([before, array, after], 0)

    x_wide = jnp.pad(widen(x_band, HALO_X), ((0, 0), (1, 1), (0, 0)))
    t_wide = widen(t_band, HALO_SLOPE)
    n_first, n_slope, n_back = own + 2 * HALO_FIRST, own + 2 * HALO_SLOPE, own + 2 * HALO_BACK
    xcol = jnp.concatenate(
        [x_wide[kx : kx + n_first, ky : ky + rows] for ky in range(3) for kx in range(3)], 2
    ).reshape(n_first * rows, 9 * in_depth)
    t_wide = t_wide.reshape(n_slope * rows, channels)

    vmem = pl.BlockSpec(memory_space=pltpu.VMEM)
    n_second = own + 2 * HALO_SECOND
    grad_last, slope, tilt_first, tilt_second, patch_middle = pl.pallas_call(
        functools.partial(front_kernel, own, rows, total),
        in_specs=[pl.BlockSpec(memory_space=pltpu.SMEM)] + [vmem] * 5,
        out_specs=[vmem] * 5,
        out_shape=[
            jax.ShapeDtypeStruct((channels, 9 * hidden), bf16),
            jax.ShapeDtypeStruct((n_slope * rows, channels), bf16),
            jax.ShapeDtypeStruct((own * rows, hidden), f32),
            jax.ShapeDtypeStruct((n_back * rows, hidden), f32),
            jax.ShapeDtypeStruct((n_second * rows, 9 * hidden), bf16),
        ],
        scratch_shapes=[
            pltpu.VMEM((n_slope * rows, 9 * hidden), bf16),
            pltpu.VMEM((n_slope * rows, channels), f32),
        ],
        compiler_params=pltpu.CompilerParams(vmem_limit_bytes=VMEM_LIMIT),
        name="front",
    )((me // 4).astype(jnp.int32).reshape(1), xcol, t_wide, kernel_first, kernel_middle, kernel_last)
    out_last = scatter_rows(grad_last, me)
    grad_first, grad_middle = pl.pallas_call(
        functools.partial(back_kernel, own, rows),
        in_specs=[vmem] * 7,
        out_specs=[vmem] * 2,
        out_shape=[
            jax.ShapeDtypeStruct((hidden, 9 * in_depth), bf16),
            jax.ShapeDtypeStruct((hidden, 9 * hidden), bf16),
        ],
        scratch_shapes=[
            pltpu.VMEM((n_slope * rows, 9 * hidden), f32),
            pltpu.VMEM((n_back * rows, 9 * hidden), f32),
        ],
        compiler_params=pltpu.CompilerParams(vmem_limit_bytes=VMEM_LIMIT),
        name="back",
    )(xcol, slope, tilt_first, tilt_second, patch_middle, kernel_middle, kernel_last)
    out_small = scatter_rows(jnp.concatenate([grad_first, grad_middle], 1), me)
    return (out_small[:, : 9 * in_depth], out_small[:, 9 * in_depth :], out_last)


def solution(mesh):
    placed = (
        P("groups", "cols"),
        P("groups", "cols", None),
        P("cols", None),
        P("cols", None),
        P("cols", None),
    )
    return jax.shard_map(
        on_device,
        mesh=mesh,
        in_specs=placed,
        out_specs=(
            P(("groups", "cols"), None),
            P(("groups", "cols"), None),
            P(("groups", "cols"), None),
        ),
        check_vma=False,
    )
```

```python
import functools

import jax
import jax.numpy as jnp
from jax import lax
from jax.experimental import pallas as pl
from jax.experimental.pallas import tpu as pltpu
from jax.sharding import PartitionSpec as P

epsilon = 1e-06
bf16, f32 = jnp.bfloat16, jnp.float32
MIB = 1024 * 1024
HALO_X, HALO_FIRST, HALO_SECOND, HALO_SLOPE, HALO_BACK = 13, 12, 10, 6, 2
BLOCKS, FAR = 16, 4


def swap(array, mask):
    size = lax.axis_size("cols")
    return lax.ppermute(array, "cols", [(i, i ^ mask) for i in range(size)])


def shift(array, step):
    size = lax.axis_size("cols")
    return lax.ppermute(
        array, "cols", [(i, i + step) for i in range(size) if 0 <= i + step < size]
    )


def neighbours(fold):
    size = lax.axis_size("cols")
    return [list(range(i, i + fold)) for i in range(0, size, fold)]


def dot(a, b, contract):
    return lax.dot_general(a, b, (contract, ((), ())), preferred_element_type=f32)


def iota(shape, axis):
    return lax.broadcasted_iota(jnp.int32, shape, axis)


def row_shifted(value, step, rows):
    count = value.shape[0]
    if step == 0:
        return value
    row = iota((count, 1), 0) % rows + step
    rolled = pltpu.roll(value, (-step) % count, 0)
    return jnp.where((row >= 0) & (row < rows), rolled, 0.0)


def inside(count, rows, first, total):
    col = iota((count, 1), 0) // rows + first
    return (col >= 0) & (col < total)


def put_patch(patch_ref, value, step, rows, out_cols):
    depth = value.shape[1]
    for ky in range(3):
        moved = row_shifted(value, (ky - 1) * step, rows).astype(bf16)
        for kx in range(3):
            tap = 3 * ky + kx
            start = kx * step * rows
            patch_ref[:, tap * depth : (tap + 1) * depth] = moved[start : start + out_cols * rows]


def spread_back(parts_ref, step, rows, out_cols):
    depth = parts_ref.shape[1] // 9
    total = None
    for ky in range(3):
        line = None
        for kx in range(3):
            tap = 3 * ky + kx
            start = (2 - kx) * step * rows
            piece = parts_ref[start : start + out_cols * rows, tap * depth : (tap + 1) * depth]
            line = piece if line is None else line + piece
        line = row_shifted(line, (1 - ky) * step, rows)
        total = line if total is None else total + line
    return total


def deal_kernel(
    at_ref,
    x_hbm,
    teacher_hbm,
    w_first_hbm,
    w_middle_hbm,
    w_last_hbm,
    kept_ref,
    sent_ref,
    shard_ref,
    x_ref,
    teacher_ref,
    w_first_ref,
    w_middle_ref,
    w_last_ref,
    arrived,
):
    copies = [
        pltpu.make_async_copy(source, target, arrived.at[i])
        for i, (source, target) in enumerate(
            (
                (teacher_hbm, teacher_ref),
                (x_hbm, x_ref),
                (w_last_hbm, w_last_ref),
                (w_middle_hbm, w_middle_ref),
                (w_first_hbm, w_first_ref),
            )
        )
    ]
    for copy in copies:
        copy.start()
    height, breadth, channels = teacher_ref.shape
    depth = x_ref.shape[1] // breadth
    rows, piece = height // 2, breadth // 2
    cells = rows * piece
    core, row = at_ref[1] % 2, at_ref[1] // 2
    out = iota((cells, 1), 0)
    col, line = out // rows, out % rows
    for copy in copies:
        copy.wait()
    r_last, r_small, taps = w_last_ref.shape[0], w_middle_ref.shape[0], w_first_ref.shape[1]
    shard_ref[:r_last] = w_last_ref[...]
    shard_ref[r_last : r_last + r_small] = w_middle_ref[...]
    shard_ref[r_last + r_small :, :taps] = w_first_ref[...]
    shard_ref[r_last + r_small :, taps:] = jnp.zeros(
        (r_small, shard_ref.shape[1] - taps), shard_ref.dtype
    )
    field = teacher_ref[...].reshape(height * breadth, channels)
    pairs = jnp.concatenate(
        [x_ref[:, 2 * depth * i : 2 * depth * (i + 1)] for i in range(piece)], 0
    )
    for rc, out_ref in ((1, sent_ref), (0, kept_ref)):
        row_parity = core ^ rc
        source = col * height + 2 * line + row_parity
        pick = (iota((cells, piece * height), 1) == source).astype(f32).astype(bf16)
        both = dot(pick, pairs, ((1,), (0,)))
        low, high = both[:, :depth], both[:, depth:]
        for ry in range(2):
            col_parity = row ^ ry
            source = (2 * line + row_parity) * breadth + 2 * col + col_parity
            pick = (iota((cells, height * breadth), 1) == source).astype(f32).astype(bf16)
            out_ref[ry, :, :channels] = dot(pick, field, ((1,), (0,))).astype(bf16)
            out_ref[ry, :, channels:] = jnp.where(col_parity == 0, low, high).astype(bf16)


def collect_kernel(
    halo,
    at_ref,
    kept_ref,
    near_ref,
    far_ref,
    shard_ref,
    far1_ref,
    far2_ref,
    far3_ref,
    h_ref,
    band_ref,
    low_ref,
    high_ref,
):
    for far, ref in enumerate((shard_ref, far1_ref, far2_ref, far3_ref)):
        h_ref[far] = ref[...]
    cells = kept_ref.shape[1]
    low = at_ref[1]
    for k, piece in enumerate((kept_ref.at[0], near_ref.at[0], far_ref.at[0], far_ref.at[1])):
        band_ref[pl.ds(pl.multiple_of((low ^ k) * cells, cells), cells), :] = piece[...]
    low_ref[...] = band_ref[:halo]
    high_ref[...] = band_ref[band_ref.shape[0] - halo :]


def early_kernel(rows, channels, cols, before_ref, band_ref, after_ref, patch_ref):
    wide = jnp.concatenate([ref[:, channels:] for ref in (before_ref, band_ref, after_ref)], 0)
    put_patch(patch_ref, wide.astype(f32), 1, rows, cols)


def front_kernel(
    own,
    rows,
    total,
    at_ref,
    before_ref,
    band_ref,
    after_ref,
    patch_first_ref,
    h_ref,
    hy_ref,
    hc_ref,
    hyc_ref,
    keep_ref,
    send_ref,
    slope_ref,
    tilt_first_ref,
    tilt_second_ref,
    patch_middle_ref,
    w_middle_ref,
    w_last_ref,
    small_ref,
    patch_last_ref,
    student_ref,
    terms_ref,
):
    first_col, place = at_ref[0] * own, at_ref[2]
    r_last = w_last_ref.shape[1]
    r_small = small_ref.shape[1] // 2
    hidden = tilt_first_ref.shape[1]
    channels = slope_ref.shape[1]
    in_taps = patch_first_ref.shape[1]
    for near, ref in enumerate((h_ref, hc_ref, hy_ref, hyc_ref)):
        for far in range(FAR):
            at = place ^ (4 * far + near)
            w_last_ref[at] = ref[far, :r_last]
            small_ref[at] = ref[far, r_last:].astype(f32)
    small = small_ref[...]
    w_middle_ref[...] = small[:, :r_small].reshape(-1, 9 * hidden).astype(bf16)
    w_first = small[:, r_small:, :in_taps].reshape(-1, in_taps).astype(bf16)

    n_first, n_second, n_slope = (
        own + 2 * HALO_FIRST,
        own + 2 * HALO_SECOND,
        own + 2 * HALO_SLOPE,
    )
    pre = dot(patch_first_ref[...], w_first, ((1,), (1,)))
    sigma = 1.0 / (1.0 + jnp.exp(-pre))
    act = jnp.where(
        inside(n_first * rows, rows, first_col - HALO_FIRST, total), pre * sigma, 0.0
    )
    lo = HALO_FIRST * rows
    pre_own, sigma_own = pre[lo : lo + own * rows], sigma[lo : lo + own * rows]
    tilt_first_ref[...] = sigma_own * (1.0 + pre_own * (1.0 - sigma_own))
    put_patch(patch_middle_ref, act, 2, rows, n_second)

    pre = dot(patch_middle_ref[...], w_middle_ref[...], ((1,), (1,)))
    sigma = 1.0 / (1.0 + jnp.exp(-pre))
    act = jnp.where(
        inside(n_second * rows, rows, first_col - HALO_SECOND, total), pre * sigma, 0.0
    )
    lo, n_back = (HALO_SECOND - HALO_BACK) * rows, (own + 2 * HALO_BACK) * rows
    pre_back, sigma_back = pre[lo : lo + n_back], sigma[lo : lo + n_back]
    tilt_second_ref[...] = jnp.where(
        inside(n_back, rows, first_col - HALO_BACK, total),
        sigma_back * (1.0 + pre_back * (1.0 - sigma_back)),
        0.0,
    )
    put_patch(patch_last_ref, act, 4, rows, n_slope)

    w_last = w_last_ref[...].reshape(-1, 9 * hidden)
    student_ref[...] = dot(patch_last_ref[...], w_last, ((1,), (1,)))

    def slopes(start, count, target, col):
        at = pl.ds(start, count)
        student = student_ref[at, :]
        s_inv = lax.rsqrt(jnp.sum(student * student, -1, keepdims=True) + epsilon)
        target = target.astype(f32)
        t_inv = lax.rsqrt(jnp.sum(target * target, -1, keepdims=True) + epsilon)
        s_unit = student * s_inv
        differ = s_unit - target * t_inv
        slope = (differ - s_unit * jnp.sum(s_unit * differ, -1, keepdims=True)) * s_inv
        slope_ref[at, :] = jnp.where(inside(count, rows, col, total), slope, 0.0).astype(bf16)

    edge, block = HALO_SLOPE * rows, 4 * rows
    lo, n_own = edge, own * rows
    slopes(0, edge, before_ref[(HALO_X - HALO_SLOPE) * rows :, :channels], first_col - HALO_SLOPE)
    slopes(edge + n_own, edge, after_ref[:edge, :channels], first_col + own)

    def step(i, carry):
        at = pl.multiple_of(i * block, block)
        target = band_ref[pl.ds(at, block), :channels]
        slopes(pl.multiple_of(edge + at, rows), block, target, first_col + i * 4)
        return carry

    lax.fori_loop(0, own // 4, step, 0)
    terms = dot(
        slope_ref[lo : lo + n_own, :], patch_last_ref[lo : lo + n_own, :], ((0,), (0,))
    )
    terms_ref[...] = terms.reshape(terms_ref.shape)
    for ry in range(2):
        for far in range(FAR):
            at = place ^ (4 * far + 2 * ry)
            keep_ref[ry, far] = terms_ref[at]
            send_ref[ry, far] = terms_ref[at ^ 1].astype(bf16)


def back_kernel(
    own,
    rows,
    at_ref,
    slope_ref,
    tilt_second_ref,
    w_last_ref,
    tilt_first_ref,
    patch_first_ref,
    patch_middle_ref,
    w_middle_ref,
    keep_ref,
    send_ref,
    parts_last_ref,
    parts_ref,
    terms_ref,
):
    place = at_ref[2]
    n_own = own * rows
    w_last = w_last_ref[...].reshape(-1, w_last_ref.shape[2])
    parts_last_ref[...] = dot(slope_ref[...], w_last, ((1,), (0,)))
    back_second = spread_back(parts_last_ref, 4, rows, own + 2 * HALO_BACK)
    slope_second = (back_second * tilt_second_ref[...]).astype(bf16)
    lo, hi = HALO_BACK * rows, HALO_SECOND * rows
    r_small, middle = terms_ref.shape[1], patch_middle_ref.shape[1]
    grad_middle = dot(
        slope_second[lo : lo + n_own], patch_middle_ref[hi : hi + n_own, :], ((0,), (0,))
    )
    terms_ref[:, :, :middle] = grad_middle.reshape(-1, r_small, middle)
    parts_ref[...] = dot(slope_second, w_middle_ref[...], ((1,), (0,)))
    back_first = spread_back(parts_ref, 2, rows, own)
    slope_first = (back_first * tilt_first_ref[...]).astype(bf16)
    hi = HALO_FIRST * rows
    grad_first = dot(slope_first, patch_first_ref[hi : hi + n_own, :], ((0,), (0,)))
    terms_ref[:, :, middle:] = grad_first.reshape(-1, r_small, grad_first.shape[1])
    for ry in range(2):
        for far in range(FAR):
            at = place ^ (4 * far + 2 * ry)
            keep_ref[ry, far] = terms_ref[at]
            send_ref[ry, far] = terms_ref[at ^ 1].astype(bf16)


def merge_kernel(
    last_ref, last_got_ref, small_ref, small_got_ref, kept_ref, send1_ref, send2_ref, send3_ref
):
    r_last, middle = last_ref.shape[1], last_ref.shape[2]
    r_small = small_ref.shape[1]
    taps = small_ref.shape[2] - middle
    for far, ref in enumerate((kept_ref, send1_ref, send2_ref, send3_ref)):
        small = small_ref[far] + small_got_ref[far].astype(f32)
        ref[:r_last] = (last_ref[far] + last_got_ref[far].astype(f32)).astype(ref.dtype)
        pad = jnp.zeros((r_small, middle - taps), f32)
        tail = jnp.concatenate(
            [small[:, :middle], jnp.concatenate([small[:, middle:], pad], 1)], 0
        )
        ref[r_last:] = tail.astype(ref.dtype)


def finish_kernel(kept_ref, got1_ref, got2_ref, got3_ref, first_ref, middle_ref, last_ref):
    total = kept_ref[...]
    for ref in (got1_ref, got2_ref, got3_ref):
        total = total + ref[...].astype(f32)
    r_last, r_small, taps = last_ref.shape[0], middle_ref.shape[0], first_ref.shape[1]
    last_ref[...] = total[:r_last]
    middle_ref[...] = total[r_last : r_last + r_small]
    first_ref[...] = total[r_last + r_small :, :taps]


def call(kernel, name, inputs, outs, scratch, flops, spaces=None, semaphores=(), vmem_mib=24):
    vmem = pl.BlockSpec(memory_space=pltpu.VMEM)
    spaces = spaces or {}
    return pl.pallas_call(
        kernel,
        in_specs=[spaces.get(i, vmem) for i in range(len(inputs))],
        out_specs=[vmem] * len(outs),
        out_shape=[jax.ShapeDtypeStruct(shape, kind) for shape, kind in outs],
        scratch_shapes=[pltpu.VMEM(shape, kind) for shape, kind in scratch] + list(semaphores),
        compiler_params=pltpu.CompilerParams(vmem_limit_bytes=vmem_mib * MIB),
        cost_estimate=pl.CostEstimate(flops=flops, bytes_accessed=1_000_000, transcendentals=0),
        name=name,
    )(*inputs)


SMEM = {0: pl.BlockSpec(memory_space=pltpu.SMEM)}


def on_device(image_feats, teacher, w_first, w_middle, w_last):
    size = lax.axis_size("cols")
    me = lax.axis_index("cols")
    fold = size // BLOCKS
    height, breadth, channels = teacher.shape
    in_depth = w_first.shape[1] // 9
    hidden = w_middle.shape[1] // 9
    rows, piece = height // 2, breadth // 2
    own = 4 * piece
    total = own * (size // 4)
    at = jnp.stack([me // 4, me % 4, me // fold]).astype(jnp.int32)

    if fold > 1:
        w_first, w_middle, w_last = (
            lax.all_gather(w, "cols", axis_index_groups=neighbours(fold), axis=0, tiled=True)
            for w in (w_first, w_middle, w_last)
        )
    r_last, r_small = w_last.shape[0], w_first.shape[0]
    cells, deep = piece * rows, channels + in_depth
    hbm = pl.BlockSpec(memory_space=pltpu.HBM)
    kept, sent, shard = call(
        deal_kernel,
        "deal",
        (at, image_feats, teacher, w_first, w_middle, w_last),
        [
            ((2, cells, deep), bf16),
            ((2, cells, deep), bf16),
            ((r_last + 2 * r_small, 9 * hidden), bf16),
        ],
        [(a.shape, a.dtype) for a in (image_feats, teacher, w_first, w_middle, w_last)],
        600_000_000,
        SMEM | {i: hbm for i in range(1, 6)},
        [pltpu.SemaphoreType.DMA((5,))],
        60,
    )
    near = swap(sent, 1)
    pair = jnp.stack([kept[1], near[1]], 0)
    far = {k: swap(shard, 4 * k * fold) for k in (3, 2, 1)}
    pair = swap(pair, 2)
    halo = HALO_X * rows
    h, band, low_edge, high_edge = call(
        functools.partial(collect_kernel, halo),
        "collect",
        (at, kept, near, pair, shard, far[1], far[2], far[3]),
        [
            ((FAR,) + shard.shape, bf16),
            ((own * rows, deep), bf16),
            ((halo, deep), bf16),
            ((halo, deep), bf16),
        ],
        [],
        1_000_000,
        SMEM,
    )
    hy = swap(h, 2 * fold)
    hc = swap(h, fold)
    before = shift(high_edge, 4)
    after = shift(low_edge, -4)
    hyc = swap(hy, fold)

    n_first, n_second, n_slope, n_back = (
        (own + 2 * halo) * rows for halo in (HALO_FIRST, HALO_SECOND, HALO_SLOPE, HALO_BACK)
    )
    (patch_first,) = call(
        functools.partial(early_kernel, rows, channels, own + 2 * HALO_FIRST),
        "early",
        (before, band, after),
        [((n_first, 9 * in_depth), bf16)],
        [],
        6_000_000_000,
    )
    keep, send, slope, tilt_first, tilt_second, patch_middle, all_middle, all_last = call(
        functools.partial(front_kernel, own, rows, total),
        "front",
        (at, before, band, after, patch_first, h, hy, hc, hyc),
        [
            ((2, FAR, r_last, 9 * hidden), f32),
            ((2, FAR, r_last, 9 * hidden), bf16),
            ((n_slope, channels), bf16),
            ((own * rows, hidden), f32),
            ((n_back, hidden), f32),
            ((n_second, 9 * hidden), bf16),
            ((hidden, 9 * hidden), bf16),
            ((BLOCKS, r_last, 9 * hidden), bf16),
        ],
        [
            ((BLOCKS, 2 * r_small, 9 * hidden), f32),
            ((n_slope, 9 * hidden), bf16),
            ((n_slope, channels), f32),
            ((BLOCKS, r_last, 9 * hidden), f32),
        ],
        6_000_000_000,
        SMEM,
    )
    got = swap(send, fold)
    small_keep, small_send = call(
        functools.partial(back_kernel, own, rows),
        "back",
        (at, slope, tilt_second, all_last, tilt_first, patch_first, patch_middle, all_middle),
        [
            ((2, FAR, r_small, 9 * (hidden + in_depth)), f32),
            ((2, FAR, r_small, 9 * (hidden + in_depth)), bf16),
        ],
        [
            ((n_slope, 9 * hidden), f32),
            ((n_back, 9 * hidden), f32),
            ((BLOCKS, r_small, 9 * (hidden + in_depth)), f32),
        ],
        4_000_000_000,
        SMEM,
    )
    last_kept = keep[0] + got[0].astype(f32)
    last_sent = (keep[1] + got[1].astype(f32)).astype(bf16)
    last_got = swap(last_sent, 2 * fold)
    got = swap(small_send, fold)
    small_kept = small_keep[0] + got[0].astype(f32)
    small_sent = (small_keep[1] + got[1].astype(f32)).astype(bf16)
    small_got = swap(small_sent, 2 * fold)
    merged = call(
        merge_kernel,
        "merge",
        (last_kept, last_got, small_kept, small_got),
        [(shard.shape, f32)] + [(shard.shape, bf16)] * 3,
        [],
        1_000_000,
    )
    got = {k: swap(merged[k], 4 * k * fold) for k in (3, 2, 1)}
    out_first, out_middle, out_last = call(
        finish_kernel,
        "finish",
        (merged[0], got[1], got[2], got[3]),
        [(w.shape, f32) for w in (w_first, w_middle, w_last)],
        [],
        1_000_000,
    )
    if fold > 1:
        out_first, out_middle, out_last = (
            lax.psum_scatter(
                out, "cols", scatter_dimension=0, axis_index_groups=neighbours(fold), tiled=True
            )
            for out in (out_first, out_middle, out_last)
        )
    return (out_first, out_middle, out_last)


def solution(mesh):
    placed = (
        P("groups", "cols"),
        P("groups", "cols", None),
        P("cols", None),
        P("cols", None),
        P("cols", None),
    )
    return jax.shard_map(
        on_device,
        mesh=mesh,
        in_specs=placed,
        out_specs=(
            P(("groups", "cols"), None),
            P(("groups", "cols"), None),
            P(("groups", "cols"), None),
        ),
        check_vma=False,
    )
```

```python
import functools

import jax
import jax.numpy as jnp
from jax import lax
from jax.experimental import pallas as pl
from jax.experimental.pallas import tpu as pltpu
from jax.sharding import PartitionSpec as P

epsilon = 1e-06
bf16, f32 = jnp.bfloat16, jnp.float32
MIB = 1024 * 1024
HALO_X, HALO_FIRST, HALO_SECOND, HALO_SLOPE, HALO_BACK = 13, 12, 10, 6, 2
BLOCKS, FAR = 16, 4
STACK_COST = 3_000_000_000


def swap(array, mask):
    size = lax.axis_size("cols")
    return lax.ppermute(array, "cols", [(i, i ^ mask) for i in range(size)])


def shift(array, step):
    size = lax.axis_size("cols")
    return lax.ppermute(
        array, "cols", [(i, i + step) for i in range(size) if 0 <= i + step < size]
    )


def neighbours(fold):
    size = lax.axis_size("cols")
    return [list(range(i, i + fold)) for i in range(0, size, fold)]


def position(blocks):
    me = lax.axis_index("cols")
    return me // 4, me % 4, me // (lax.axis_size("cols") // blocks)


def dot(a, b, contract):
    return lax.dot_general(a, b, (contract, ((), ())), preferred_element_type=f32)


def iota(shape, axis):
    return lax.broadcasted_iota(jnp.int32, shape, axis)


def row_shifted(value, step, rows):
    count = value.shape[0]
    if step == 0:
        return value
    row = iota((count, 1), 0) % rows + step
    rolled = pltpu.roll(value, (-step) % count, 0)
    return jnp.where((row >= 0) & (row < rows), rolled, 0.0)


def inside(count, rows, first, total):
    col = iota((count, 1), 0) // rows + first
    return (col >= 0) & (col < total)


def put_patch(patch_ref, value, step, rows, out_cols):
    depth = value.shape[1]
    for ky in range(3):
        moved = row_shifted(value, (ky - 1) * step, rows).astype(bf16)
        for kx in range(3):
            tap = 3 * ky + kx
            start = kx * step * rows
            patch_ref[:, tap * depth : (tap + 1) * depth] = moved[start : start + out_cols * rows]


def spread_back(parts_ref, step, rows, out_cols):
    depth = parts_ref.shape[1] // 9
    total = None
    for ky in range(3):
        line = None
        for kx in range(3):
            tap = 3 * ky + kx
            start = (2 - kx) * step * rows
            piece = parts_ref[start : start + out_cols * rows, tap * depth : (tap + 1) * depth]
            line = piece if line is None else line + piece
        line = row_shifted(line, (1 - ky) * step, rows)
        total = line if total is None else total + line
    return total


def deal_kernel(
    x_hbm,
    teacher_hbm,
    w_first_hbm,
    w_middle_hbm,
    w_last_hbm,
    kept_ref,
    sent_ref,
    shard_ref,
    x_ref,
    teacher_ref,
    w_first_ref,
    w_middle_ref,
    w_last_ref,
    pick_x_ref,
    pick_t_ref,
    arrived,
):
    copies = [
        pltpu.make_async_copy(source, target, arrived.at[i])
        for i, (source, target) in enumerate(
            (
                (teacher_hbm, teacher_ref),
                (x_hbm, x_ref),
                (w_last_hbm, w_last_ref),
                (w_middle_hbm, w_middle_ref),
                (w_first_hbm, w_first_ref),
            )
        )
    ]
    for copy in copies:
        copy.start()
    height, breadth, channels = teacher_ref.shape
    depth = x_ref.shape[1] // breadth
    rows, piece = height // 2, breadth // 2
    cells = rows * piece
    low = position(BLOCKS)[1]
    core, row = low % 2, low // 2
    out = iota((cells, 1), 0)
    col, line = out // rows, out % rows
    for rc in range(2):
        line_of = 2 * line + (core ^ rc)
        pick_x_ref[rc] = (iota((cells, piece * height), 1) == col * height + line_of).astype(f32).astype(bf16)
        for ry in range(2):
            source = line_of * breadth + 2 * col + (row ^ ry)
            pick_t_ref[rc, ry] = (iota((cells, height * breadth), 1) == source).astype(f32).astype(bf16)
    for copy in copies:
        copy.wait()
    r_last, r_small, taps = w_last_ref.shape[0], w_middle_ref.shape[0], w_first_ref.shape[1]
    shard_ref[:r_last] = w_last_ref[...]
    shard_ref[r_last : r_last + r_small] = w_middle_ref[...]
    shard_ref[r_last + r_small :, :taps] = w_first_ref[...]
    shard_ref[r_last + r_small :, taps:] = jnp.zeros(
        (r_small, shard_ref.shape[1] - taps), shard_ref.dtype
    )
    field = teacher_ref[...].reshape(height * breadth, channels)
    pairs = jnp.concatenate(
        [x_ref[:, 2 * depth * i : 2 * depth * (i + 1)] for i in range(piece)], 0
    )
    for rc, out_ref in ((1, sent_ref), (0, kept_ref)):
        both = dot(pick_x_ref[rc], pairs, ((1,), (0,)))
        low, high = both[:, :depth], both[:, depth:]
        for ry in range(2):
            out_ref[ry, :, :channels] = dot(pick_t_ref[rc, ry], field, ((1,), (0,))).astype(bf16)
            out_ref[ry, :, channels:] = jnp.where((row ^ ry) == 0, low, high).astype(bf16)


def stack_kernel(*refs):
    for i, ref in enumerate(refs[:-1]):
        refs[-1][i] = ref[...]


def collect_kernel(halo, kept_ref, near_ref, far_ref, h_ref, band_ref, low_ref, high_ref, same_ref):
    cells = kept_ref.shape[1]
    low = position(BLOCKS)[1]
    for k, piece in enumerate((kept_ref.at[0], near_ref.at[0], far_ref.at[0], far_ref.at[1])):
        band_ref[pl.ds(pl.multiple_of((low ^ k) * cells, cells), cells), :] = piece[...]
    low_ref[...] = band_ref[:halo]
    high_ref[...] = band_ref[band_ref.shape[0] - halo :]


def early_kernel(rows, channels, cols, before_ref, band_ref, after_ref, patch_ref):
    wide = jnp.concatenate([ref[:, channels:] for ref in (before_ref, band_ref, after_ref)], 0)
    put_patch(patch_ref, wide.astype(f32), 1, rows, cols)


def front_kernel(
    own,
    rows,
    total,
    before_ref,
    band_ref,
    after_ref,
    patch_first_ref,
    h_ref,
    hy_ref,
    hc_ref,
    hyc_ref,
    keep_ref,
    send_ref,
    slope_ref,
    tilt_first_ref,
    tilt_second_ref,
    patch_middle_ref,
    w_middle_ref,
    w_last_ref,
    small_ref,
    patch_last_ref,
    student_ref,
    terms_ref,
):
    group, _, place = position(BLOCKS)
    first_col = group * own
    r_last = w_last_ref.shape[1]
    r_small = small_ref.shape[1] // 2
    hidden = tilt_first_ref.shape[1]
    channels = slope_ref.shape[1]
    in_taps = patch_first_ref.shape[1]
    for near, ref in enumerate((h_ref, hc_ref, hy_ref, hyc_ref)):
        for far in range(FAR):
            at = place ^ (4 * far + near)
            w_last_ref[at] = ref[far, :r_last]
            small_ref[at] = ref[far, r_last:].astype(f32)
    small = small_ref[...]
    w_middle_ref[...] = small[:, :r_small].reshape(-1, 9 * hidden).astype(bf16)
    w_first = small[:, r_small:, :in_taps].reshape(-1, in_taps).astype(bf16)

    n_first, n_second, n_slope = (
        own + 2 * HALO_FIRST,
        own + 2 * HALO_SECOND,
        own + 2 * HALO_SLOPE,
    )
    pre = dot(patch_first_ref[...], w_first, ((1,), (1,)))
    sigma = 1.0 / (1.0 + jnp.exp(-pre))
    act = jnp.where(
        inside(n_first * rows, rows, first_col - HALO_FIRST, total), pre * sigma, 0.0
    )
    lo = HALO_FIRST * rows
    pre_own, sigma_own = pre[lo : lo + own * rows], sigma[lo : lo + own * rows]
    tilt_first_ref[...] = sigma_own * (1.0 + pre_own * (1.0 - sigma_own))
    put_patch(patch_middle_ref, act, 2, rows, n_second)

    pre = dot(patch_middle_ref[...], w_middle_ref[...], ((1,), (1,)))
    sigma = 1.0 / (1.0 + jnp.exp(-pre))
    act = jnp.where(
        inside(n_second * rows, rows, first_col - HALO_SECOND, total), pre * sigma, 0.0
    )
    lo, n_back = (HALO_SECOND - HALO_BACK) * rows, (own + 2 * HALO_BACK) * rows
    pre_back, sigma_back = pre[lo : lo + n_back], sigma[lo : lo + n_back]
    tilt_second_ref[...] = jnp.where(
        inside(n_back, rows, first_col - HALO_BACK, total),
        sigma_back * (1.0 + pre_back * (1.0 - sigma_back)),
        0.0,
    )
    put_patch(patch_last_ref, act, 4, rows, n_slope)

    w_last = w_last_ref[...].reshape(-1, 9 * hidden)
    student_ref[...] = dot(patch_last_ref[...], w_last, ((1,), (1,)))

    def slopes(start, count, target, col):
        at = pl.ds(start, count)
        student = student_ref[at, :]
        s_inv = lax.rsqrt(jnp.sum(student * student, -1, keepdims=True) + epsilon)
        target = target.astype(f32)
        t_inv = lax.rsqrt(jnp.sum(target * target, -1, keepdims=True) + epsilon)
        s_unit = student * s_inv
        differ = s_unit - target * t_inv
        slope = (differ - s_unit * jnp.sum(s_unit * differ, -1, keepdims=True)) * s_inv
        slope_ref[at, :] = jnp.where(inside(count, rows, col, total), slope, 0.0).astype(bf16)

    edge, block = HALO_SLOPE * rows, 4 * rows
    lo, n_own = edge, own * rows
    slopes(0, edge, before_ref[(HALO_X - HALO_SLOPE) * rows :, :channels], first_col - HALO_SLOPE)
    slopes(edge + n_own, edge, after_ref[:edge, :channels], first_col + own)

    def step(i, carry):
        at = pl.multiple_of(i * block, block)
        target = band_ref[pl.ds(at, block), :channels]
        slopes(pl.multiple_of(edge + at, rows), block, target, first_col + i * 4)
        return carry

    lax.fori_loop(0, own // 4, step, 0)
    terms = dot(
        slope_ref[lo : lo + n_own, :], patch_last_ref[lo : lo + n_own, :], ((0,), (0,))
    )
    terms_ref[...] = terms.reshape(terms_ref.shape)
    for ry in range(2):
        for far in range(FAR):
            at = place ^ (4 * far + 2 * ry)
            keep_ref[ry, far] = terms_ref[at]
            send_ref[ry, far] = terms_ref[at ^ 1].astype(bf16)


def back_kernel(
    own,
    rows,
    slope_ref,
    tilt_second_ref,
    w_last_ref,
    tilt_first_ref,
    patch_first_ref,
    patch_middle_ref,
    w_middle_ref,
    keep_ref,
    send_ref,
    parts_last_ref,
    parts_ref,
    terms_ref,
):
    place = position(BLOCKS)[2]
    n_own = own * rows
    w_last = w_last_ref[...].reshape(-1, w_last_ref.shape[2])
    parts_last_ref[...] = dot(slope_ref[...], w_last, ((1,), (0,)))
    back_second = spread_back(parts_last_ref, 4, rows, own + 2 * HALO_BACK)
    slope_second = (back_second * tilt_second_ref[...]).astype(bf16)
    lo, hi = HALO_BACK * rows, HALO_SECOND * rows
    r_small, middle = terms_ref.shape[1], patch_middle_ref.shape[1]
    grad_middle = dot(
        slope_second[lo : lo + n_own], patch_middle_ref[hi : hi + n_own, :], ((0,), (0,))
    )
    terms_ref[:, :, :middle] = grad_middle.reshape(-1, r_small, middle)
    parts_ref[...] = dot(slope_second, w_middle_ref[...], ((1,), (0,)))
    back_first = spread_back(parts_ref, 2, rows, own)
    slope_first = (back_first * tilt_first_ref[...]).astype(bf16)
    hi = HALO_FIRST * rows
    grad_first = dot(slope_first, patch_first_ref[hi : hi + n_own, :], ((0,), (0,)))
    terms_ref[:, :, middle:] = grad_first.reshape(-1, r_small, grad_first.shape[1])
    for ry in range(2):
        for far in range(FAR):
            at = place ^ (4 * far + 2 * ry)
            keep_ref[far, ry] = terms_ref[at]
            send_ref[far, ry] = terms_ref[at ^ 1].astype(bf16)


def split_kernel(keep_ref, got_ref, kept_ref, *send_refs):
    for i, ref in enumerate((kept_ref,) + send_refs):
        ref[...] = (keep_ref[i] + got_ref[i].astype(f32)).astype(ref.dtype)


def add_kernel(keep_ref, got1_ref, got2_ref, got3_ref, kept_ref, send_ref):
    total = keep_ref[...]
    for ref in (got1_ref, got2_ref, got3_ref):
        total = total + ref[...].astype(f32)
    kept_ref[...] = total[0]
    send_ref[...] = total[1].astype(bf16)


def finish_kernel(
    last_ref, got1_ref, got2_ref, got3_ref, small_ref, got_ref, first_ref, middle_ref, out_ref
):
    total = last_ref[...]
    for ref in (got1_ref, got2_ref, got3_ref):
        total = total + ref[...].astype(f32)
    out_ref[...] = total
    small = small_ref[...] + got_ref[...].astype(f32)
    middle_ref[...] = small[:, : middle_ref.shape[1]]
    first_ref[...] = small[:, middle_ref.shape[1] :]


def call(kernel, name, inputs, outs, scratch, flops, spaces=None, semaphores=(), vmem_mib=24, out_spaces=None, aliases=None):
    vmem = pl.BlockSpec(memory_space=pltpu.VMEM)
    spaces = spaces or {}
    return pl.pallas_call(
        kernel,
        in_specs=[spaces.get(i, vmem) for i in range(len(inputs))],
        out_specs=[(out_spaces or {}).get(i, vmem) for i in range(len(outs))],
        input_output_aliases=aliases or {},
        out_shape=[jax.ShapeDtypeStruct(shape, kind) for shape, kind in outs],
        scratch_shapes=[pltpu.VMEM(shape, kind) for shape, kind in scratch] + list(semaphores),
        compiler_params=pltpu.CompilerParams(vmem_limit_bytes=vmem_mib * MIB),
        cost_estimate=pl.CostEstimate(flops=flops, bytes_accessed=1_000_000, transcendentals=0),
        name=name,
    )(*inputs)


def on_device(image_feats, teacher, w_first, w_middle, w_last):
    size = lax.axis_size("cols")
    fold = size // BLOCKS
    height, breadth, channels = teacher.shape
    in_depth = w_first.shape[1] // 9
    hidden = w_middle.shape[1] // 9
    rows, piece = height // 2, breadth // 2
    own = 4 * piece
    total = own * (size // 4)

    if fold > 1:
        w_first, w_middle, w_last = (
            lax.all_gather(w, "cols", axis_index_groups=neighbours(fold), axis=0, tiled=True)
            for w in (w_first, w_middle, w_last)
        )
    r_last, r_small = w_last.shape[0], w_first.shape[0]
    cells, deep = piece * rows, channels + in_depth
    hbm = pl.BlockSpec(memory_space=pltpu.HBM)
    kept, sent, shard = call(
        deal_kernel,
        "deal",
        (image_feats, teacher, w_first, w_middle, w_last),
        [
            ((2, cells, deep), bf16),
            ((2, cells, deep), bf16),
            ((r_last + 2 * r_small, 9 * hidden), bf16),
        ],
        [(a.shape, a.dtype) for a in (image_feats, teacher, w_first, w_middle, w_last)]
        + [((2, cells, piece * height), bf16), ((2, 2, cells, height * breadth), bf16)],
        600_000_000,
        {i: hbm for i in range(5)},
        [pltpu.SemaphoreType.DMA((5,))],
        60,
    )
    near = swap(sent, 1)
    pair = jnp.stack([kept[1], near[1]], 0)
    far = {k: swap(shard, 4 * k * fold) for k in (3, 2, 1)}
    pair = swap(pair, 2)
    halo = HALO_X * rows
    (h,) = call(
        stack_kernel,
        "stack",
        (shard, far[1], far[2], far[3]),
        [((FAR,) + shard.shape, bf16)],
        [],
        STACK_COST,
    )
    band, low_edge, high_edge, h = call(
        functools.partial(collect_kernel, halo),
        "collect",
        (kept, near, pair, h),
        [
            ((own * rows, deep), bf16),
            ((halo, deep), bf16),
            ((halo, deep), bf16),
            (h.shape, bf16),
        ],
        [],
        1_000_000,
        {3: pl.BlockSpec(memory_space=pl.ANY)},
        out_spaces={3: pl.BlockSpec(memory_space=pl.ANY)},
        aliases={3: 3},
    )
    hy = swap(h, 2 * fold)
    hc = swap(h, fold)
    before = shift(high_edge, 4)
    after = shift(low_edge, -4)
    hyc = swap(hy, fold)

    n_first, n_second, n_slope, n_back = (
        (own + 2 * halo) * rows for halo in (HALO_FIRST, HALO_SECOND, HALO_SLOPE, HALO_BACK)
    )
    (patch_first,) = call(
        functools.partial(early_kernel, rows, channels, own + 2 * HALO_FIRST),
        "early",
        (before, band, after),
        [((n_first, 9 * in_depth), bf16)],
        [],
        6_000_000_000,
    )
    keep, send, slope, tilt_first, tilt_second, patch_middle, all_middle, all_last = call(
        functools.partial(front_kernel, own, rows, total),
        "front",
        (before, band, after, patch_first, h, hy, hc, hyc),
        [
            ((2, FAR, r_last, 9 * hidden), f32),
            ((2, FAR, r_last, 9 * hidden), bf16),
            ((n_slope, channels), bf16),
            ((own * rows, hidden), f32),
            ((n_back, hidden), f32),
            ((n_second, 9 * hidden), bf16),
            ((hidden, 9 * hidden), bf16),
            ((BLOCKS, r_last, 9 * hidden), bf16),
        ],
        [
            ((BLOCKS, 2 * r_small, 9 * hidden), f32),
            ((n_slope, 9 * hidden), bf16),
            ((n_slope, channels), f32),
            ((BLOCKS, r_last, 9 * hidden), f32),
        ],
        6_000_000_000,
    )
    both = 9 * (hidden + in_depth)
    got = swap(send, fold)
    small_keep, small_send = call(
        functools.partial(back_kernel, own, rows),
        "back",
        (slope, tilt_second, all_last, tilt_first, patch_first, patch_middle, all_middle),
        [
            ((FAR, 2, r_small, both), f32),
            ((FAR, 2, r_small, both), bf16),
        ],
        [
            ((n_slope, 9 * hidden), f32),
            ((n_back, 9 * hidden), f32),
            ((BLOCKS, r_small, both), f32),
        ],
        4_000_000_000,
    )
    def split(keep, got, count):
        shape = keep.shape[1:]
        outs = [(shape, f32)] + [(shape, bf16)] * (count - 1)
        return call(split_kernel, "split", (keep, got), outs, [], 1_000_000)

    last_kept, last_sent = split(keep, got, 2)
    last_got = swap(last_sent, 2 * fold)
    parts = split(small_keep, swap(small_send, fold), FAR)
    small_got = {k: swap(parts[k], 4 * k * fold) for k in (3, 2, 1)}
    last = split(last_kept, last_got, FAR)
    last_got = {k: swap(last[k], 4 * k * fold) for k in (3, 2, 1)}
    small_kept, small_sent = call(
        add_kernel,
        "add",
        (parts[0], small_got[1], small_got[2], small_got[3]),
        [((r_small, both), f32), ((r_small, both), bf16)],
        [],
        1_000_000,
    )
    small_got = swap(small_sent, 2 * fold)
    out_first, out_middle, out_last = call(
        finish_kernel,
        "finish",
        (last[0], last_got[1], last_got[2], last_got[3], small_kept, small_got),
        [(w.shape, f32) for w in (w_first, w_middle, w_last)],
        [],
        1_000_000,
    )
    if fold > 1:
        out_first, out_middle, out_last = (
            lax.psum_scatter(
                out, "cols", scatter_dimension=0, axis_index_groups=neighbours(fold), tiled=True
            )
            for out in (out_first, out_middle, out_last)
        )
    return (out_first, out_middle, out_last)


def solution(mesh):
    placed = (
        P("groups", "cols"),
        P("groups", "cols", None),
        P("cols", None),
        P("cols", None),
        P("cols", None),
    )
    return jax.shard_map(
        on_device,
        mesh=mesh,
        in_specs=placed,
        out_specs=(
            P(("groups", "cols"), None),
            P(("groups", "cols"), None),
            P(("groups", "cols"), None),
        ),
        check_vma=False,
    )
```

```python
import functools

import jax
import jax.numpy as jnp
from jax import lax
from jax.experimental import pallas as pl
from jax.experimental.pallas import tpu as pltpu
from jax.sharding import PartitionSpec as P

epsilon = 1e-06
bf16, f32 = jnp.bfloat16, jnp.float32
MIB = 1024 * 1024
HALO_X, HALO_FIRST, HALO_SECOND, HALO_SLOPE, HALO_BACK = 13, 12, 10, 6, 2
BLOCKS, FAR = 16, 4
LANES = 128
STACK_COST = 3_000_000_000
EARLY_COST = 1_500_000_000


def swap(array, mask):
    size = lax.axis_size("cols")
    return lax.ppermute(array, "cols", [(i, i ^ mask) for i in range(size)])


def bands_beside(low_pairs, high_pairs):
    size = lax.axis_size("cols")
    pairs = [(i, i + 4) for i in range(4, size - 4) if (i // 4) % 2]
    across = lax.ppermute(high_pairs, "cols", pairs + [(j, i) for i, j in pairs])
    return swap(low_pairs, 4), across


def neighbours(fold):
    size = lax.axis_size("cols")
    return [list(range(i, i + fold)) for i in range(0, size, fold)]


def position(blocks):
    me = lax.axis_index("cols")
    return me // 4, me % 4, me // (lax.axis_size("cols") // blocks)


def dot(a, b, contract):
    return lax.dot_general(a, b, (contract, ((), ())), preferred_element_type=f32)


def iota(shape, axis):
    return lax.broadcasted_iota(jnp.int32, shape, axis)


def row_shifted(value, step, rows):
    count = value.shape[0]
    if step == 0:
        return value
    row = iota((count, 1), 0) % rows + step
    rolled = pltpu.roll(value, (-step) % count, 0)
    return jnp.where((row >= 0) & (row < rows), rolled, 0.0)


def inside(count, rows, first, total):
    col = iota((count, 1), 0) // rows + first
    return (col >= 0) & (col < total)


def put_patch(patch_ref, value, step, rows, out_cols):
    depth = value.shape[1]
    for ky in range(3):
        moved = row_shifted(value, (ky - 1) * step, rows).astype(bf16)
        for kx in range(3):
            tap = 3 * ky + kx
            start = kx * step * rows
            patch_ref[:, tap * depth : (tap + 1) * depth] = moved[start : start + out_cols * rows]


def spread_back(parts_ref, step, rows, out_cols):
    depth = parts_ref.shape[1] // 9
    total = None
    for ky in range(3):
        line = None
        for kx in range(3):
            tap = 3 * ky + kx
            start = (2 - kx) * step * rows
            piece = parts_ref[start : start + out_cols * rows, tap * depth : (tap + 1) * depth]
            line = piece if line is None else line + piece
        line = row_shifted(line, (1 - ky) * step, rows)
        total = line if total is None else total + line
    return total


def deal_kernel(
    x_hbm,
    teacher_hbm,
    w_first_hbm,
    w_middle_hbm,
    w_last_hbm,
    own_ref,
    near_ref,
    across_ref,
    shard_ref,
    x_ref,
    teacher_ref,
    w_first_ref,
    w_middle_ref,
    w_last_ref,
    pick_x_ref,
    pick_t_ref,
    arrived,
):
    copies = [
        pltpu.make_async_copy(source, target, arrived.at[i])
        for i, (source, target) in enumerate(
            (
                (teacher_hbm, teacher_ref),
                (x_hbm, x_ref),
                (w_last_hbm, w_last_ref),
                (w_middle_hbm, w_middle_ref),
                (w_first_hbm, w_first_ref),
            )
        )
    ]
    for copy in copies:
        copy.start()
    height, breadth, channels = teacher_ref.shape
    depth = x_ref.shape[1] // breadth
    rows, piece = height // 2, breadth // 2
    cells = rows * piece
    low = position(BLOCKS)[1]
    core, row = low % 2, low // 2
    out = iota((cells, 1), 0)
    col, line = out // rows, out % rows
    for rc in range(2):
        line_of = 2 * line + (core ^ rc)
        pick_x_ref[rc] = (iota((cells, piece * height), 1) == col * height + line_of).astype(f32).astype(bf16)
        for ry in range(2):
            source = line_of * breadth + 2 * col + (row ^ ry)
            pick_t_ref[rc, ry] = (iota((cells, height * breadth), 1) == source).astype(f32).astype(bf16)
    for copy in copies:
        copy.wait()
    at = put_tiles(shard_ref, 0, w_last_ref[...])
    at = put_tiles(shard_ref, at, w_middle_ref[...])
    put_tiles(shard_ref, at, w_first_ref[...])
    own_ref[: shard_ref.shape[0]] = shard_ref[...]
    field = teacher_ref[...].reshape(height * breadth, channels)
    pairs = jnp.concatenate(
        [x_ref[:, 2 * depth * i : 2 * depth * (i + 1)] for i in range(piece)], 0
    )
    x_parts = []
    for rc, out_ref in ((0, own_ref), (1, near_ref)):
        both = dot(pick_x_ref[rc], pairs, ((1,), (0,))).astype(bf16)
        low, high = both[:, :depth], both[:, depth:]
        x_parts.append(jnp.where(row == 0, high, low))
        across = dot(pick_t_ref[rc, 1], field, ((1,), (0,))).astype(bf16)
        put_tiles(across_ref, rc * cells * len(tiles(channels)), across)
        value = dot(pick_t_ref[rc, 0], field, ((1,), (0,))).astype(bf16)
        at = put_tiles(out_ref, out_ref.shape[0] - near_ref.shape[0], value)
        x = jnp.where(row == 0, low, high)
        out_ref[at:, :] = jnp.concatenate([x, jnp.zeros_like(x)], 1)
    across_ref[across_ref.shape[0] - cells :, :] = jnp.concatenate(x_parts, 1)


def tiles(width):
    return [(start, min(LANES, width - start)) for start in range(0, width, LANES)]


def put_tiles(ref, at, value):
    rows, width = value.shape
    for start, size in tiles(width):
        ref[at : at + rows, :size] = value[:, start : start + size]
        at += rows
    return at


def take_tiles(value, at, rows, width):
    return jnp.concatenate(
        [
            value[at + i * rows : at + (i + 1) * rows, :size]
            for i, (_, size) in enumerate(tiles(width))
        ],
        1,
    )


def hold_kernel(own_ref, across_ref, held_ref, same_ref):
    held_ref[...] = own_ref[...]


def stack_kernel(own_ref, far1_ref, far2_ref, far3_ref, last_ref, small_ref):
    cut, end = last_ref.shape[1], last_ref.shape[1] + small_ref.shape[1]
    for far, ref in enumerate((own_ref, far1_ref, far2_ref, far3_ref)):
        last_ref[far] = ref[:cut]
        small_ref[far] = ref[cut:end]


def after_kernel(value_ref, first_ref, same_ref):
    pass


def collect_kernel(
    cells,
    edge_t,
    edge_x,
    own_ref,
    near_ref,
    across_ref,
    diagonal_ref,
    last_ref,
    small_ref,
    x_ref,
    teacher_ref,
    edge_a_ref,
    edge_b_ref,
    same_last_ref,
    same_small_ref,
):
    depth, channels = x_ref.shape[1], teacher_ref.shape[1]
    low = position(BLOCKS)[1]
    part = cells * len(tiles(channels))
    skip = own_ref.shape[0] - near_ref.shape[0]
    pieces = ((own_ref, skip, 0), (near_ref, 0, 0), (across_ref, 0, 0), (diagonal_ref, part, depth))
    for k, (ref, row, lane) in enumerate(pieces):
        at = pl.ds(pl.multiple_of((low ^ k) * cells, cells), cells)
        x_ref[at, :] = ref[ref.shape[0] - cells :, lane : lane + depth]
        for lanes, size in tiles(channels):
            teacher_ref[at, lanes : lanes + size] = ref[row : row + cells, :]
            row += cells
    own = teacher_ref.shape[0]
    half = edge_x - edge_t
    odd = position(BLOCKS)[0] % 2
    for ref, high in ((edge_a_ref, 1 - odd), (edge_b_ref, odd)):
        at = pl.ds(pl.multiple_of(high * (own - edge_t), 16), edge_t)
        row = put_tiles(ref, 0, teacher_ref[at, :])
        at = high * (own - edge_x)
        ref[row:, :] = jnp.concatenate(
            [
                x_ref[pl.ds(pl.multiple_of(at, 16), half), :],
                x_ref[pl.ds(pl.multiple_of(at + edge_t, 16), half), :],
            ],
            1,
        )


def sides(edge_a_ref, edge_b_ref):
    a, b = edge_a_ref[...], edge_b_ref[...]
    odd = position(BLOCKS)[0] % 2 == 1
    return jnp.where(odd, a, b), jnp.where(odd, b, a)


def edge_x_cells(edge, edge_t, channels):
    packed = edge[edge_t * len(tiles(channels)) :, :]
    depth = LANES // 2
    overlap = packed.shape[0] - edge_t
    return jnp.concatenate([packed[:, :depth], packed[overlap:, depth:]], 0)


def early_kernel(
    own,
    rows,
    total,
    channels,
    edge_t,
    x_ref,
    edge_a_ref,
    edge_b_ref,
    h_ref,
    hy_ref,
    hc_ref,
    hyc_ref,
    tilt_first_ref,
    tilt_second_ref,
    patch_first_ref,
    patch_middle_ref,
    patch_last_ref,
    w_middle_ref,
    small_ref,
):
    group, _, place = position(BLOCKS)
    first_col = group * own
    r_small = small_ref.shape[1] // 2
    in_taps, taps = patch_first_ref.shape[1], patch_middle_ref.shape[1]
    for near, ref in enumerate((h_ref, hc_ref, hy_ref, hyc_ref)):
        for far in range(FAR):
            at = place ^ (4 * far + near)
            small = ref[far].astype(f32)
            row = 0
            for first, width in ((0, taps), (r_small, in_taps)):
                for start, size in tiles(width):
                    small_ref[at, first : first + r_small, start : start + size] = small[
                        row : row + r_small, :size
                    ]
                    row += r_small
    small = small_ref[...]
    w_middle_ref[...] = small[:, :r_small].reshape(-1, taps).astype(bf16)
    w_first = small[:, r_small:, :in_taps].reshape(-1, in_taps).astype(bf16)

    n_first, n_second, n_slope = (
        own + 2 * HALO_FIRST,
        own + 2 * HALO_SECOND,
        own + 2 * HALO_SLOPE,
    )
    before, after = sides(edge_a_ref, edge_b_ref)
    wide = jnp.concatenate(
        [
            edge_x_cells(before, edge_t, channels),
            x_ref[...],
            edge_x_cells(after, edge_t, channels),
        ],
        0,
    )
    put_patch(patch_first_ref, wide.astype(f32), 1, rows, n_first)
    pre = dot(patch_first_ref[...], w_first, ((1,), (1,)))
    sigma = 1.0 / (1.0 + jnp.exp(-pre))
    act = jnp.where(
        inside(n_first * rows, rows, first_col - HALO_FIRST, total), pre * sigma, 0.0
    )
    lo = HALO_FIRST * rows
    pre_own, sigma_own = pre[lo : lo + own * rows], sigma[lo : lo + own * rows]
    tilt_first_ref[...] = sigma_own * (1.0 + pre_own * (1.0 - sigma_own))
    put_patch(patch_middle_ref, act, 2, rows, n_second)

    pre = dot(patch_middle_ref[...], w_middle_ref[...], ((1,), (1,)))
    sigma = 1.0 / (1.0 + jnp.exp(-pre))
    act = jnp.where(
        inside(n_second * rows, rows, first_col - HALO_SECOND, total), pre * sigma, 0.0
    )
    lo, n_back = (HALO_SECOND - HALO_BACK) * rows, (own + 2 * HALO_BACK) * rows
    pre_back, sigma_back = pre[lo : lo + n_back], sigma[lo : lo + n_back]
    tilt_second_ref[...] = jnp.where(
        inside(n_back, rows, first_col - HALO_BACK, total),
        sigma_back * (1.0 + pre_back * (1.0 - sigma_back)),
        0.0,
    )
    put_patch(patch_last_ref, act, 4, rows, n_slope)


def front_kernel(
    own,
    rows,
    total,
    teacher_ref,
    edge_a_ref,
    edge_b_ref,
    patch_last_ref,
    h_ref,
    hy_ref,
    hc_ref,
    hyc_ref,
    keep_ref,
    send_ref,
    slope_ref,
    w_last_ref,
    student_ref,
    terms_ref,
):
    group, _, place = position(BLOCKS)
    first_col = group * own
    r_last, taps = w_last_ref.shape[1:]
    channels = slope_ref.shape[1]
    for near, ref in enumerate((h_ref, hc_ref, hy_ref, hyc_ref)):
        for far in range(FAR):
            at = place ^ (4 * far + near)
            for i, (start, size) in enumerate(tiles(taps)):
                w_last_ref[at, :, start : start + size] = ref[far, i * r_last : (i + 1) * r_last]

    w_last = w_last_ref[...].reshape(-1, taps)
    student_ref[...] = dot(patch_last_ref[...], w_last, ((1,), (1,)))

    def slopes(start, count, target, col):
        at = pl.ds(start, count)
        student = student_ref[at, :]
        s_inv = lax.rsqrt(jnp.sum(student * student, -1, keepdims=True) + epsilon)
        target = target.astype(f32)
        t_inv = lax.rsqrt(jnp.sum(target * target, -1, keepdims=True) + epsilon)
        s_unit = student * s_inv
        differ = s_unit - target * t_inv
        slope = (differ - s_unit * jnp.sum(s_unit * differ, -1, keepdims=True)) * s_inv
        slope_ref[at, :] = jnp.where(inside(count, rows, col, total), slope, 0.0).astype(bf16)

    edge, block = HALO_SLOPE * rows, 4 * rows
    lo, n_own = edge, own * rows
    before, after = sides(edge_a_ref, edge_b_ref)
    slopes(0, edge, take_tiles(before, 0, edge, channels), first_col - HALO_SLOPE)
    slopes(edge + n_own, edge, take_tiles(after, 0, edge, channels), first_col + own)

    def step(i, carry):
        at = pl.multiple_of(i * block, block)
        target = teacher_ref[pl.ds(at, block), :]
        slopes(pl.multiple_of(edge + at, rows), block, target, first_col + i * 4)
        return carry

    lax.fori_loop(0, own // 4, step, 0)
    terms = dot(
        slope_ref[lo : lo + n_own, :], patch_last_ref[lo : lo + n_own, :], ((0,), (0,))
    )
    terms_ref[...] = terms.reshape(terms_ref.shape)
    for ry in range(2):
        for far in range(FAR):
            at = place ^ (4 * far + 2 * ry)
            keep_ref[ry, far] = terms_ref[at]
            send_ref[ry, far] = terms_ref[at ^ 1].astype(bf16)


def back_kernel(
    own,
    rows,
    slope_ref,
    tilt_second_ref,
    w_last_ref,
    tilt_first_ref,
    patch_first_ref,
    patch_middle_ref,
    w_middle_ref,
    keep_ref,
    send_ref,
    parts_last_ref,
    parts_ref,
    terms_ref,
):
    place = position(BLOCKS)[2]
    n_own = own * rows
    w_last = w_last_ref[...].reshape(-1, w_last_ref.shape[2])
    parts_last_ref[...] = dot(slope_ref[...], w_last, ((1,), (0,)))
    back_second = spread_back(parts_last_ref, 4, rows, own + 2 * HALO_BACK)
    slope_second = (back_second * tilt_second_ref[...]).astype(bf16)
    lo, hi = HALO_BACK * rows, HALO_SECOND * rows
    r_small, middle = terms_ref.shape[1], patch_middle_ref.shape[1]
    grad_middle = dot(
        slope_second[lo : lo + n_own], patch_middle_ref[hi : hi + n_own, :], ((0,), (0,))
    )
    terms_ref[:, :, :middle] = grad_middle.reshape(-1, r_small, middle)
    parts_ref[...] = dot(slope_second, w_middle_ref[...], ((1,), (0,)))
    back_first = spread_back(parts_ref, 2, rows, own)
    slope_first = (back_first * tilt_first_ref[...]).astype(bf16)
    hi = HALO_FIRST * rows
    grad_first = dot(slope_first, patch_first_ref[hi : hi + n_own, :], ((0,), (0,)))
    terms_ref[:, :, middle:] = grad_first.reshape(-1, r_small, grad_first.shape[1])
    for ry in range(2):
        for far in range(FAR):
            at = place ^ (4 * far + 2 * ry)
            keep_ref[far, ry] = terms_ref[at]
            send_ref[far, ry] = terms_ref[at ^ 1].astype(bf16)


def split_kernel(keep_ref, got_ref, kept_ref, *send_refs):
    for i, ref in enumerate((kept_ref,) + send_refs):
        ref[...] = (keep_ref[i] + got_ref[i].astype(f32)).astype(ref.dtype)


def add_kernel(keep_ref, got1_ref, got2_ref, got3_ref, kept_ref, send_ref):
    total = keep_ref[...]
    for ref in (got1_ref, got2_ref, got3_ref):
        total = total + ref[...].astype(f32)
    kept_ref[...] = total[0]
    send_ref[...] = total[1].astype(bf16)


def finish_kernel(
    last_ref, got1_ref, got2_ref, got3_ref, small_ref, got_ref, first_ref, middle_ref, out_ref
):
    total = last_ref[...]
    for ref in (got1_ref, got2_ref, got3_ref):
        total = total + ref[...].astype(f32)
    out_ref[...] = total
    small = small_ref[...] + got_ref[...].astype(f32)
    middle_ref[...] = small[:, : middle_ref.shape[1]]
    first_ref[...] = small[:, middle_ref.shape[1] :]


def call(kernel, name, inputs, outs, scratch, flops, spaces=None, semaphores=(), vmem_mib=24, out_spaces=None, aliases=None):
    vmem = pl.BlockSpec(memory_space=pltpu.VMEM)
    spaces = spaces or {}
    return pl.pallas_call(
        kernel,
        in_specs=[spaces.get(i, vmem) for i in range(len(inputs))],
        out_specs=[(out_spaces or {}).get(i, vmem) for i in range(len(outs))],
        input_output_aliases=aliases or {},
        out_shape=[jax.ShapeDtypeStruct(shape, kind) for shape, kind in outs],
        scratch_shapes=[pltpu.VMEM(shape, kind) for shape, kind in scratch] + list(semaphores),
        compiler_params=pltpu.CompilerParams(vmem_limit_bytes=int(vmem_mib * MIB)),
        cost_estimate=pl.CostEstimate(flops=flops, bytes_accessed=1_000_000, transcendentals=0),
        name=name,
    )(*inputs)


def on_device(image_feats, teacher, w_first, w_middle, w_last):
    size = lax.axis_size("cols")
    fold = size // BLOCKS
    height, breadth, channels = teacher.shape
    in_depth = w_first.shape[1] // 9
    hidden = w_middle.shape[1] // 9
    rows, piece = height // 2, breadth // 2
    own = 4 * piece
    total = own * (size // 4)

    if fold > 1:
        w_first, w_middle, w_last = (
            lax.all_gather(w, "cols", axis_index_groups=neighbours(fold), axis=0, tiled=True)
            for w in (w_first, w_middle, w_last)
        )
    r_last, r_small = w_last.shape[0], w_first.shape[0]
    cells = piece * rows
    dealt = cells * len(tiles(channels)) + cells
    packed = r_last * len(tiles(9 * hidden))
    packed += r_small * (len(tiles(9 * hidden)) + len(tiles(9 * in_depth)))
    hbm = pl.BlockSpec(memory_space=pltpu.HBM)
    own_class, near, across, shard = call(
        deal_kernel,
        "deal",
        (image_feats, teacher, w_first, w_middle, w_last),
        [
            ((packed + dealt, LANES), bf16),
            ((dealt, LANES), bf16),
            ((2 * dealt - cells, LANES), bf16),
            ((packed, LANES), bf16),
        ],
        [(a.shape, a.dtype) for a in (image_feats, teacher, w_first, w_middle, w_last)]
        + [((2, cells, piece * height), bf16), ((2, 2, cells, height * breadth), bf16)],
        600_000_000,
        {i: hbm for i in range(5)},
        [pltpu.SemaphoreType.DMA((5,))],
        60,
    )
    across = swap(across, 2)
    far = {k: swap(shard, 4 * k * fold) for k in (3, 2, 1)}
    near = swap(near, 1)
    anywhere = pl.BlockSpec(memory_space=pl.ANY)
    held, across = call(
        hold_kernel,
        "hold",
        (own_class, across),
        [(own_class.shape, bf16), (across.shape, bf16)],
        [],
        1_000_000,
        {1: anywhere},
        out_spaces={1: anywhere},
        aliases={1: 1},
    )
    diagonal = swap(across, 1)
    edge_t, edge_x = HALO_SLOPE * rows, HALO_X * rows
    edge = edge_t * len(tiles(channels)) + edge_x - edge_t
    part_last = r_last * len(tiles(9 * hidden))
    held_last, held_small = call(
        stack_kernel,
        "stack",
        (held, far[1], far[2], far[3]),
        [((FAR, part_last, LANES), bf16), ((FAR, packed - part_last, LANES), bf16)],
        [],
        STACK_COST,
    )
    x_band, t_band, edge_a, edge_b, held_last, held_small = call(
        functools.partial(collect_kernel, cells, edge_t, edge_x),
        "collect",
        (held, near, across, diagonal, held_last, held_small),
        [
            ((own * rows, in_depth), bf16),
            ((own * rows, channels), bf16),
            ((edge, LANES), bf16),
            ((edge, LANES), bf16),
            (held_last.shape, bf16),
            (held_small.shape, bf16),
        ],
        [],
        1_000_000,
        {4: anywhere, 5: anywhere},
        out_spaces={4: anywhere, 5: anywhere},
        aliases={4: 4, 5: 5},
    )

    small_y = swap(held_small, 2 * fold)
    last_y = swap(held_last, 2 * fold)
    all_small = held_small, small_y, swap(held_small, fold), swap(small_y, fold)
    edge_a, edge_b = bands_beside(edge_a, edge_b)

    n_first, n_second, n_slope, n_back = (
        (own + 2 * halo) * rows for halo in (HALO_FIRST, HALO_SECOND, HALO_SLOPE, HALO_BACK)
    )
    tilt_first, tilt_second, patch_first, patch_middle, patch_last, all_middle = call(
        functools.partial(early_kernel, own, rows, total, channels, edge_t),
        "early",
        (x_band, edge_a, edge_b, *all_small),
        [
            ((own * rows, hidden), f32),
            ((n_back, hidden), f32),
            ((n_first, 9 * in_depth), bf16),
            ((n_second, 9 * hidden), bf16),
            ((n_slope, 9 * hidden), bf16),
            ((hidden, 9 * hidden), bf16),
        ],
        [((BLOCKS, 2 * r_small, 9 * hidden), f32)],
        EARLY_COST,
    )
    (last_y,) = call(
        after_kernel,
        "after",
        (last_y, patch_last),
        [(last_y.shape, bf16)],
        [],
        1_000_000,
        {0: anywhere, 1: anywhere},
        out_spaces={0: anywhere},
        aliases={0: 0},
    )
    all_last = held_last, last_y, swap(held_last, fold), swap(last_y, fold)
    keep, send, slope, all_last = call(
        functools.partial(front_kernel, own, rows, total),
        "front",
        (t_band, edge_a, edge_b, patch_last, *all_last),
        [
            ((2, FAR, r_last, 9 * hidden), f32),
            ((2, FAR, r_last, 9 * hidden), bf16),
            ((n_slope, channels), bf16),
            ((BLOCKS, r_last, 9 * hidden), bf16),
        ],
        [
            ((n_slope, channels), f32),
            ((BLOCKS, r_last, 9 * hidden), f32),
        ],
        6_000_000_000,
    )
    both = 9 * (hidden + in_depth)
    got = swap(send, fold)
    small_keep, small_send = call(
        functools.partial(back_kernel, own, rows),
        "back",
        (slope, tilt_second, all_last, tilt_first, patch_first, patch_middle, all_middle),
        [
            ((FAR, 2, r_small, both), f32),
            ((FAR, 2, r_small, both), bf16),
        ],
        [
            ((n_slope, 9 * hidden), f32),
            ((n_back, 9 * hidden), f32),
            ((BLOCKS, r_small, both), f32),
        ],
        4_000_000_000,
    )
    def split(keep, got, count):
        shape = keep.shape[1:]
        outs = [(shape, f32)] + [(shape, bf16)] * (count - 1)
        return call(split_kernel, "split", (keep, got), outs, [], 1_000_000)

    last_kept, last_sent = split(keep, got, 2)
    last_got = swap(last_sent, 2 * fold)
    parts = split(small_keep, swap(small_send, fold), FAR)
    small_got = {k: swap(parts[k], 4 * k * fold) for k in (3, 2, 1)}
    last = split(last_kept, last_got, FAR)
    last_got = {k: swap(last[k], 4 * k * fold) for k in (3, 2, 1)}
    small_kept, small_sent = call(
        add_kernel,
        "add",
        (parts[0], small_got[1], small_got[2], small_got[3]),
        [((r_small, both), f32), ((r_small, both), bf16)],
        [],
        1_000_000,
    )
    small_got = swap(small_sent, 2 * fold)
    out_first, out_middle, out_last = call(
        finish_kernel,
        "finish",
        (last[0], last_got[1], last_got[2], last_got[3], small_kept, small_got),
        [(w.shape, f32) for w in (w_first, w_middle, w_last)],
        [],
        1_000_000,
    )
    if fold > 1:
        out_first, out_middle, out_last = (
            lax.psum_scatter(
                out, "cols", scatter_dimension=0, axis_index_groups=neighbours(fold), tiled=True
            )
            for out in (out_first, out_middle, out_last)
        )
    return (out_first, out_middle, out_last)


def solution(mesh):
    placed = (
        P("groups", "cols"),
        P("groups", "cols", None),
        P("cols", None),
        P("cols", None),
        P("cols", None),
    )
    return jax.shard_map(
        on_device,
        mesh=mesh,
        in_specs=placed,
        out_specs=(
            P(("groups", "cols"), None),
            P(("groups", "cols"), None),
            P(("groups", "cols"), None),
        ),
        check_vma=False,
    )
```

```python
import functools

import jax
import jax.numpy as jnp
from jax import lax
from jax.experimental import pallas as pl
from jax.experimental.pallas import tpu as pltpu
from jax.sharding import PartitionSpec as P

epsilon = 1e-06
bf16, f32 = jnp.bfloat16, jnp.float32
MIB = 1024 * 1024
HALO_X, HALO_FIRST, HALO_SECOND, HALO_SLOPE, HALO_BACK = 13, 12, 10, 6, 2
BLOCKS, FAR = 16, 4
LANES = 128
STACK_COST = 3_000_000_000
EARLY_COST = 1_500_000_000
HALF_COST = 1_500_000_000


def swap(array, mask):
    size = lax.axis_size("cols")
    return lax.ppermute(array, "cols", [(i, i ^ mask) for i in range(size)])


def bands_beside(low_pairs, high_pairs):
    size = lax.axis_size("cols")
    pairs = [(i, i + 4) for i in range(4, size - 4) if (i // 4) % 2]
    across = lax.ppermute(high_pairs, "cols", pairs + [(j, i) for i, j in pairs])
    return swap(low_pairs, 4), across


def neighbours(fold):
    size = lax.axis_size("cols")
    return [list(range(i, i + fold)) for i in range(0, size, fold)]


def position(blocks):
    me = lax.axis_index("cols")
    return me // 4, me % 4, me // (lax.axis_size("cols") // blocks)


def dot(a, b, contract):
    return lax.dot_general(a, b, (contract, ((), ())), preferred_element_type=f32)


def iota(shape, axis):
    return lax.broadcasted_iota(jnp.int32, shape, axis)


def row_shifted(value, step, rows):
    count = value.shape[0]
    if step == 0:
        return value
    row = iota((count, 1), 0) % rows + step
    rolled = pltpu.roll(value, (-step) % count, 0)
    return jnp.where((row >= 0) & (row < rows), rolled, 0.0)


def inside(count, rows, first, total):
    col = iota((count, 1), 0) // rows + first
    return (col >= 0) & (col < total)


def put_patch(patch_ref, value, step, rows, out_cols):
    depth = value.shape[1]
    for ky in range(3):
        moved = row_shifted(value, (ky - 1) * step, rows).astype(bf16)
        for kx in range(3):
            tap = 3 * ky + kx
            start = kx * step * rows
            patch_ref[:, tap * depth : (tap + 1) * depth] = moved[start : start + out_cols * rows]


def spread_back(parts_ref, step, rows, out_cols):
    depth = parts_ref.shape[1] // 9
    total = None
    for ky in range(3):
        line = None
        for kx in range(3):
            tap = 3 * ky + kx
            start = (2 - kx) * step * rows
            piece = parts_ref[start : start + out_cols * rows, tap * depth : (tap + 1) * depth]
            line = piece if line is None else line + piece
        line = row_shifted(line, (1 - ky) * step, rows)
        total = line if total is None else total + line
    return total


def deal_kernel(
    x_hbm,
    teacher_hbm,
    w_first_hbm,
    w_middle_hbm,
    w_last_hbm,
    own_ref,
    near_ref,
    across_ref,
    shard_ref,
    x_ref,
    teacher_ref,
    w_first_ref,
    w_middle_ref,
    w_last_ref,
    pick_x_ref,
    pick_t_ref,
    arrived,
):
    copies = [
        pltpu.make_async_copy(source, target, arrived.at[i])
        for i, (source, target) in enumerate(
            (
                (teacher_hbm, teacher_ref),
                (x_hbm, x_ref),
                (w_last_hbm, w_last_ref),
                (w_middle_hbm, w_middle_ref),
                (w_first_hbm, w_first_ref),
            )
        )
    ]
    for copy in copies:
        copy.start()
    height, breadth, channels = teacher_ref.shape
    depth = x_ref.shape[1] // breadth
    rows, piece = height // 2, breadth // 2
    cells = rows * piece
    low = position(BLOCKS)[1]
    core, row = low % 2, low // 2
    out = iota((cells, 1), 0)
    col, line = out // rows, out % rows
    for rc in range(2):
        line_of = 2 * line + (core ^ rc)
        pick_x_ref[rc] = (iota((cells, piece * height), 1) == col * height + line_of).astype(f32).astype(bf16)
        for ry in range(2):
            source = line_of * breadth + 2 * col + (row ^ ry)
            pick_t_ref[rc, ry] = (iota((cells, height * breadth), 1) == source).astype(f32).astype(bf16)
    for copy in copies:
        copy.wait()
    at = put_tiles(shard_ref, 0, w_last_ref[...])
    at = put_tiles(shard_ref, at, w_middle_ref[...])
    put_tiles(shard_ref, at, w_first_ref[...])
    own_ref[: shard_ref.shape[0]] = shard_ref[...]
    field = teacher_ref[...].reshape(height * breadth, channels)
    pairs = jnp.concatenate(
        [x_ref[:, 2 * depth * i : 2 * depth * (i + 1)] for i in range(piece)], 0
    )
    x_parts = []
    for rc, out_ref in ((0, own_ref), (1, near_ref)):
        both = dot(pick_x_ref[rc], pairs, ((1,), (0,))).astype(bf16)
        low, high = both[:, :depth], both[:, depth:]
        x_parts.append(jnp.where(row == 0, high, low))
        across = dot(pick_t_ref[rc, 1], field, ((1,), (0,))).astype(bf16)
        put_tiles(across_ref, rc * cells * len(tiles(channels)), across)
        value = dot(pick_t_ref[rc, 0], field, ((1,), (0,))).astype(bf16)
        at = put_tiles(out_ref, out_ref.shape[0] - near_ref.shape[0], value)
        x = jnp.where(row == 0, low, high)
        out_ref[at:, :] = jnp.concatenate([x, jnp.zeros_like(x)], 1)
    across_ref[across_ref.shape[0] - cells :, :] = jnp.concatenate(x_parts, 1)


def tiles(width):
    return [(start, min(LANES, width - start)) for start in range(0, width, LANES)]


def put_tiles(ref, at, value):
    rows, width = value.shape
    for start, size in tiles(width):
        ref[at : at + rows, :size] = value[:, start : start + size]
        at += rows
    return at


def take_tiles(value, at, rows, width):
    return jnp.concatenate(
        [
            value[at + i * rows : at + (i + 1) * rows, :size]
            for i, (_, size) in enumerate(tiles(width))
        ],
        1,
    )


def hold_kernel(own_ref, across_ref, held_ref, same_ref):
    held_ref[...] = own_ref[...]


def stack_kernel(own_ref, far3_ref, far1_ref, far2_ref, last_ref, small_ref):
    cut, end = last_ref.shape[1], last_ref.shape[1] + small_ref.shape[1]
    for far, ref in enumerate((own_ref, far1_ref, far2_ref, far3_ref)):
        last_ref[far] = ref[:cut]
        small_ref[far] = ref[cut:end]


def after_kernel(value_ref, first_ref, same_ref):
    pass


def collect_kernel(
    cells,
    edge_t,
    edge_x,
    own_ref,
    near_ref,
    across_ref,
    diagonal_ref,
    last_ref,
    small_ref,
    x_ref,
    teacher_ref,
    edge_a_ref,
    edge_b_ref,
    same_last_ref,
    same_small_ref,
):
    depth, channels = x_ref.shape[1], teacher_ref.shape[1]
    low = position(BLOCKS)[1]
    part = cells * len(tiles(channels))
    skip = own_ref.shape[0] - near_ref.shape[0]
    pieces = ((own_ref, skip, 0), (near_ref, 0, 0), (across_ref, 0, 0), (diagonal_ref, part, depth))
    for k, (ref, row, lane) in enumerate(pieces):
        at = pl.ds(pl.multiple_of((low ^ k) * cells, cells), cells)
        x_ref[at, :] = ref[ref.shape[0] - cells :, lane : lane + depth]
        for lanes, size in tiles(channels):
            teacher_ref[at, lanes : lanes + size] = ref[row : row + cells, :]
            row += cells
    own = teacher_ref.shape[0]
    half = edge_x - edge_t
    odd = position(BLOCKS)[0] % 2
    for ref, high in ((edge_a_ref, 1 - odd), (edge_b_ref, odd)):
        at = pl.ds(pl.multiple_of(high * (own - edge_t), 16), edge_t)
        row = put_tiles(ref, 0, teacher_ref[at, :])
        at = high * (own - edge_x)
        ref[row:, :] = jnp.concatenate(
            [
                x_ref[pl.ds(pl.multiple_of(at, 16), half), :],
                x_ref[pl.ds(pl.multiple_of(at + edge_t, 16), half), :],
            ],
            1,
        )


def sides(edge_a_ref, edge_b_ref):
    a, b = edge_a_ref[...], edge_b_ref[...]
    odd = position(BLOCKS)[0] % 2 == 1
    return jnp.where(odd, a, b), jnp.where(odd, b, a)


def edge_x_cells(edge, edge_t, channels):
    packed = edge[edge_t * len(tiles(channels)) :, :]
    depth = LANES // 2
    overlap = packed.shape[0] - edge_t
    return jnp.concatenate([packed[:, :depth], packed[overlap:, depth:]], 0)


def early_kernel(
    own,
    rows,
    total,
    channels,
    edge_t,
    x_ref,
    edge_a_ref,
    edge_b_ref,
    h_ref,
    hy_ref,
    hc_ref,
    hyc_ref,
    tilt_first_ref,
    tilt_second_ref,
    patch_first_ref,
    patch_middle_ref,
    patch_last_ref,
    w_middle_ref,
    small_ref,
):
    group, _, place = position(BLOCKS)
    first_col = group * own
    r_small = small_ref.shape[1] // 2
    in_taps, taps = patch_first_ref.shape[1], patch_middle_ref.shape[1]
    for near, ref in enumerate((h_ref, hc_ref, hy_ref, hyc_ref)):
        for far in range(FAR):
            at = place ^ (4 * far + near)
            small = ref[far].astype(f32)
            row = 0
            for first, width in ((0, taps), (r_small, in_taps)):
                for start, size in tiles(width):
                    small_ref[at, first : first + r_small, start : start + size] = small[
                        row : row + r_small, :size
                    ]
                    row += r_small
    small = small_ref[...]
    w_middle_ref[...] = small[:, :r_small].reshape(-1, taps).astype(bf16)
    w_first = small[:, r_small:, :in_taps].reshape(-1, in_taps).astype(bf16)

    n_first, n_second, n_slope = (
        own + 2 * HALO_FIRST,
        own + 2 * HALO_SECOND,
        own + 2 * HALO_SLOPE,
    )
    before, after = sides(edge_a_ref, edge_b_ref)
    wide = jnp.concatenate(
        [
            edge_x_cells(before, edge_t, channels),
            x_ref[...],
            edge_x_cells(after, edge_t, channels),
        ],
        0,
    )
    put_patch(patch_first_ref, wide.astype(f32), 1, rows, n_first)
    pre = dot(patch_first_ref[...], w_first, ((1,), (1,)))
    sigma = 1.0 / (1.0 + jnp.exp(-pre))
    act = jnp.where(
        inside(n_first * rows, rows, first_col - HALO_FIRST, total), pre * sigma, 0.0
    )
    lo = HALO_FIRST * rows
    pre_own, sigma_own = pre[lo : lo + own * rows], sigma[lo : lo + own * rows]
    tilt_first_ref[...] = sigma_own * (1.0 + pre_own * (1.0 - sigma_own))
    put_patch(patch_middle_ref, act, 2, rows, n_second)

    pre = dot(patch_middle_ref[...], w_middle_ref[...], ((1,), (1,)))
    sigma = 1.0 / (1.0 + jnp.exp(-pre))
    act = jnp.where(
        inside(n_second * rows, rows, first_col - HALO_SECOND, total), pre * sigma, 0.0
    )
    lo, n_back = (HALO_SECOND - HALO_BACK) * rows, (own + 2 * HALO_BACK) * rows
    pre_back, sigma_back = pre[lo : lo + n_back], sigma[lo : lo + n_back]
    tilt_second_ref[...] = jnp.where(
        inside(n_back, rows, first_col - HALO_BACK, total),
        sigma_back * (1.0 + pre_back * (1.0 - sigma_back)),
        0.0,
    )
    put_patch(patch_last_ref, act, 4, rows, n_slope)


def put_blocks(w_ref, blocks, r_last):
    taps = w_ref.shape[1]
    for i, (ref, far) in enumerate(blocks):
        for j, (start, size) in enumerate(tiles(taps)):
            w_ref[i * r_last : (i + 1) * r_last, start : start + size] = ref[
                far, j * r_last : (j + 1) * r_last
            ]


def half_kernel(
    rows,
    edge_t,
    teacher_ref,
    edge_a_ref,
    edge_b_ref,
    patch_last_ref,
    h_ref,
    hy_ref,
    w_own_ref,
    student_ref,
    target_ref,
):
    place = position(BLOCKS)[2]
    channels = teacher_ref.shape[1]
    r_last = channels // BLOCKS
    put_blocks(w_own_ref, [(ref, far) for ref in (h_ref, hy_ref) for far in range(FAR)], r_last)
    student_ref[...] = dot(patch_last_ref[...], w_own_ref[...], ((1,), (1,)))
    before, after = sides(edge_a_ref, edge_b_ref)
    wide = jnp.concatenate(
        [
            take_tiles(before, 0, edge_t, channels),
            teacher_ref[...],
            take_tiles(after, 0, edge_t, channels),
        ],
        0,
    )
    out = iota((1, channels), 1)
    block = out // r_last
    key = 4 * (block % FAR) + 2 * (block // FAR % 2) + block // (2 * FAR)
    source = (key ^ place) * r_last + out % r_last
    pick = (iota((channels, channels), 0) == source).astype(f32).astype(bf16)
    target_ref[...] = dot(wide, pick, ((1,), (0,))).astype(bf16)


def front_kernel(
    own,
    rows,
    total,
    target_ref,
    patch_last_ref,
    student_own_ref,
    hc_ref,
    hyc_ref,
    send_ref,
    slope_ref,
    w_other_ref,
    student_ref,
):
    first_col = position(BLOCKS)[0] * own
    channels = slope_ref.shape[1]
    half = channels // 2
    put_blocks(
        w_other_ref, [(ref, far) for ref in (hc_ref, hyc_ref) for far in range(FAR)], channels // BLOCKS
    )
    student_ref[...] = dot(patch_last_ref[...], w_other_ref[...], ((1,), (1,)))
    block = 4 * rows
    for step in range(slope_ref.shape[0] // block):
        at = pl.ds(step * block, block)
        parts = [
            (student, target_ref[at, lane : lane + half].astype(f32), lane)
            for student, lane in ((student_own_ref[at, :], 0), (student_ref[at, :], half))
        ]

        def total_of(product):
            return sum(jnp.sum(product(s, t), -1, keepdims=True) for s, t, _ in parts)

        s_inv = lax.rsqrt(total_of(lambda s, t: s * s) + epsilon)
        t_inv = lax.rsqrt(total_of(lambda s, t: t * t) + epsilon)
        cosine = total_of(lambda s, t: s * t) * (s_inv * t_inv)
        ok = inside(block, rows, first_col - HALO_SLOPE + step * (block // rows), total)
        s_part = jnp.where(ok, s_inv * s_inv * (cosine + epsilon * (s_inv * s_inv)), 0.0)
        t_part = jnp.where(ok, s_inv * t_inv, 0.0)
        for student, target, lane in parts:
            slope_ref[at, lane : lane + half] = (student * s_part - target * t_part).astype(bf16)

    lo, n_own = HALO_SLOPE * rows, own * rows
    terms = dot(
        slope_ref[lo : lo + n_own, half:], patch_last_ref[lo : lo + n_own, :], ((0,), (0,))
    )
    send_ref[...] = terms.astype(bf16).reshape(send_ref.shape)


def back_kernel(
    own,
    rows,
    slope_ref,
    tilt_second_ref,
    w_own_ref,
    w_other_ref,
    patch_last_ref,
    keep_ref,
    slope_second_ref,
    parts_ref,
):
    half = w_own_ref.shape[0]
    lo, n_own = HALO_SLOPE * rows, own * rows
    terms = dot(
        slope_ref[lo : lo + n_own, :half], patch_last_ref[lo : lo + n_own, :], ((0,), (0,))
    )
    keep_ref[...] = terms.reshape(keep_ref.shape)
    parts_ref[...] = dot(slope_ref[:, :half], w_own_ref[...], ((1,), (0,))) + dot(
        slope_ref[:, half:], w_other_ref[...], ((1,), (0,))
    )
    back_second = spread_back(parts_ref, 4, rows, own + 2 * HALO_BACK)
    slope_second_ref[...] = (back_second * tilt_second_ref[...]).astype(bf16)


def first_kernel(
    own,
    rows,
    slope_second_ref,
    tilt_first_ref,
    patch_first_ref,
    patch_middle_ref,
    w_middle_ref,
    keep_ref,
    send_ref,
    parts_ref,
    terms_ref,
):
    place = position(BLOCKS)[2]
    n_own = own * rows
    slope_second = slope_second_ref[...]
    lo, hi = HALO_BACK * rows, HALO_SECOND * rows
    r_small, middle = terms_ref.shape[1], patch_middle_ref.shape[1]
    grad_middle = dot(
        slope_second[lo : lo + n_own], patch_middle_ref[hi : hi + n_own, :], ((0,), (0,))
    )
    terms_ref[:, :, :middle] = grad_middle.reshape(-1, r_small, middle)
    parts_ref[...] = dot(slope_second, w_middle_ref[...], ((1,), (0,)))
    back_first = spread_back(parts_ref, 2, rows, own)
    slope_first = (back_first * tilt_first_ref[...]).astype(bf16)
    hi = HALO_FIRST * rows
    grad_first = dot(slope_first, patch_first_ref[hi : hi + n_own, :], ((0,), (0,)))
    terms_ref[:, :, middle:] = grad_first.reshape(-1, r_small, grad_first.shape[1])
    for ry in range(2):
        for far in range(FAR):
            at = place ^ (4 * far + 2 * ry)
            keep_ref[far, ry] = terms_ref[at]
            send_ref[far, ry] = terms_ref[at ^ 1].astype(bf16)


def tied_split_kernel(keep_ref, got_ref, tie_ref, *out_refs):
    split_kernel(keep_ref, got_ref, *out_refs)


def split_kernel(keep_ref, got_ref, kept_ref, *send_refs):
    for i, ref in enumerate((kept_ref,) + send_refs):
        ref[...] = (keep_ref[i] + got_ref[i].astype(f32)).astype(ref.dtype)


def add_kernel(keep_ref, got1_ref, got2_ref, got3_ref, kept_ref, send_ref):
    total = keep_ref[...]
    for ref in (got1_ref, got2_ref, got3_ref):
        total = total + ref[...].astype(f32)
    kept_ref[...] = total[0]
    send_ref[...] = total[1].astype(bf16)


def finish_kernel(
    last_ref, got1_ref, got2_ref, got3_ref, small_ref, got_ref, first_ref, middle_ref, out_ref
):
    total = last_ref[...]
    for ref in (got1_ref, got2_ref, got3_ref):
        total = total + ref[...].astype(f32)
    out_ref[...] = total
    small = small_ref[...] + got_ref[...].astype(f32)
    middle_ref[...] = small[:, : middle_ref.shape[1]]
    first_ref[...] = small[:, middle_ref.shape[1] :]


def call(kernel, name, inputs, outs, scratch, flops, spaces=None, semaphores=(), vmem_mib=24, out_spaces=None, aliases=None):
    vmem = pl.BlockSpec(memory_space=pltpu.VMEM)
    spaces = spaces or {}
    return pl.pallas_call(
        kernel,
        in_specs=[spaces.get(i, vmem) for i in range(len(inputs))],
        out_specs=[(out_spaces or {}).get(i, vmem) for i in range(len(outs))],
        input_output_aliases=aliases or {},
        out_shape=[jax.ShapeDtypeStruct(shape, kind) for shape, kind in outs],
        scratch_shapes=[pltpu.VMEM(shape, kind) for shape, kind in scratch] + list(semaphores),
        compiler_params=pltpu.CompilerParams(vmem_limit_bytes=int(vmem_mib * MIB)),
        cost_estimate=pl.CostEstimate(flops=flops, bytes_accessed=1_000_000, transcendentals=0),
        name=name,
    )(*inputs)


def on_device(image_feats, teacher, w_first, w_middle, w_last):
    size = lax.axis_size("cols")
    fold = size // BLOCKS
    height, breadth, channels = teacher.shape
    in_depth = w_first.shape[1] // 9
    hidden = w_middle.shape[1] // 9
    rows, piece = height // 2, breadth // 2
    own = 4 * piece
    total = own * (size // 4)

    if fold > 1:
        w_first, w_middle, w_last = (
            lax.all_gather(w, "cols", axis_index_groups=neighbours(fold), axis=0, tiled=True)
            for w in (w_first, w_middle, w_last)
        )
    r_last, r_small = w_last.shape[0], w_first.shape[0]
    cells = piece * rows
    dealt = cells * len(tiles(channels)) + cells
    packed = r_last * len(tiles(9 * hidden))
    packed += r_small * (len(tiles(9 * hidden)) + len(tiles(9 * in_depth)))
    hbm = pl.BlockSpec(memory_space=pltpu.HBM)
    own_class, near, across, shard = call(
        deal_kernel,
        "deal",
        (image_feats, teacher, w_first, w_middle, w_last),
        [
            ((packed + dealt, LANES), bf16),
            ((dealt, LANES), bf16),
            ((2 * dealt - cells, LANES), bf16),
            ((packed, LANES), bf16),
        ],
        [(a.shape, a.dtype) for a in (image_feats, teacher, w_first, w_middle, w_last)]
        + [((2, cells, piece * height), bf16), ((2, 2, cells, height * breadth), bf16)],
        600_000_000,
        {i: hbm for i in range(5)},
        [pltpu.SemaphoreType.DMA((5,))],
        60,
    )
    across = swap(across, 2)
    far = {k: swap(shard, 4 * k * fold) for k in (1, 2, 3)}
    near = swap(near, 1)
    anywhere = pl.BlockSpec(memory_space=pl.ANY)
    held, across = call(
        hold_kernel,
        "hold",
        (own_class, across),
        [(own_class.shape, bf16), (across.shape, bf16)],
        [],
        1_000_000,
        {1: anywhere},
        out_spaces={1: anywhere},
        aliases={1: 1},
    )
    diagonal = swap(across, 1)
    edge_t, edge_x = HALO_SLOPE * rows, HALO_X * rows
    edge = edge_t * len(tiles(channels)) + edge_x - edge_t
    part_last = r_last * len(tiles(9 * hidden))
    held_last, held_small = call(
        stack_kernel,
        "stack",
        (held, far[3], far[1], far[2]),
        [((FAR, part_last, LANES), bf16), ((FAR, packed - part_last, LANES), bf16)],
        [],
        STACK_COST,
    )
    x_band, t_band, edge_a, edge_b, held_last, held_small = call(
        functools.partial(collect_kernel, cells, edge_t, edge_x),
        "collect",
        (held, near, across, diagonal, held_last, held_small),
        [
            ((own * rows, in_depth), bf16),
            ((own * rows, channels), bf16),
            ((edge, LANES), bf16),
            ((edge, LANES), bf16),
            (held_last.shape, bf16),
            (held_small.shape, bf16),
        ],
        [],
        1_000_000,
        {4: anywhere, 5: anywhere},
        out_spaces={4: anywhere, 5: anywhere},
        aliases={4: 4, 5: 5},
    )

    small_y = swap(held_small, 2 * fold)
    last_y = swap(held_last, 2 * fold)
    all_small = held_small, small_y, swap(held_small, fold), swap(small_y, fold)
    edge_a, edge_b = bands_beside(edge_a, edge_b)

    n_first, n_second, n_slope, n_back = (
        (own + 2 * halo) * rows for halo in (HALO_FIRST, HALO_SECOND, HALO_SLOPE, HALO_BACK)
    )
    tilt_first, tilt_second, patch_first, patch_middle, patch_last, all_middle = call(
        functools.partial(early_kernel, own, rows, total, channels, edge_t),
        "early",
        (x_band, edge_a, edge_b, *all_small),
        [
            ((own * rows, hidden), f32),
            ((n_back, hidden), f32),
            ((n_first, 9 * in_depth), bf16),
            ((n_second, 9 * hidden), bf16),
            ((n_slope, 9 * hidden), bf16),
            ((hidden, 9 * hidden), bf16),
        ],
        [((BLOCKS, 2 * r_small, 9 * hidden), f32)],
        EARLY_COST,
    )
    (last_y,) = call(
        after_kernel,
        "after",
        (last_y, patch_last),
        [(last_y.shape, bf16)],
        [],
        1_000_000,
        {0: anywhere, 1: anywhere},
        out_spaces={0: anywhere},
        aliases={0: 0},
    )
    half = channels // 2
    last_c, last_yc = swap(held_last, fold), swap(last_y, fold)
    w_own, student_own, target = call(
        functools.partial(half_kernel, rows, edge_t),
        "half",
        (t_band, edge_a, edge_b, patch_last, held_last, last_y),
        [
            ((half, 9 * hidden), bf16),
            ((n_slope, half), f32),
            ((n_slope, channels), bf16),
        ],
        [],
        HALF_COST,
    )
    send, slope, w_other = call(
        functools.partial(front_kernel, own, rows, total),
        "front",
        (target, patch_last, student_own, last_c, last_yc),
        [
            ((2, FAR, r_last, 9 * hidden), bf16),
            ((n_slope, channels), bf16),
            ((half, 9 * hidden), bf16),
        ],
        [((n_slope, half), f32)],
        6_000_000_000,
    )
    got = swap(send, fold)
    keep, slope_second = call(
        functools.partial(back_kernel, own, rows),
        "back",
        (slope, tilt_second, w_own, w_other, patch_last),
        [((2, FAR, r_last, 9 * hidden), f32), ((n_back, hidden), bf16)],
        [((n_slope, 9 * hidden), f32)],
        4_000_000_000,
    )
    both = 9 * (hidden + in_depth)
    small_keep, small_send = call(
        functools.partial(first_kernel, own, rows),
        "first",
        (slope_second, tilt_first, patch_first, patch_middle, all_middle),
        [((FAR, 2, r_small, both), f32), ((FAR, 2, r_small, both), bf16)],
        [((n_back, 9 * hidden), f32), ((BLOCKS, r_small, both), f32)],
        2_000_000_000,
    )

    def split(keep, got, count):
        shape = keep.shape[1:]
        outs = [(shape, f32)] + [(shape, bf16)] * (count - 1)
        return call(split_kernel, "split", (keep, got), outs, [], 1_000_000)

    last_kept, last_sent = call(
        tied_split_kernel,
        "split",
        (keep, got, slope_second),
        [(keep.shape[1:], f32), (keep.shape[1:], bf16)],
        [],
        1_000_000,
        {2: anywhere},
    )
    last_got = swap(last_sent, 2 * fold)
    parts = split(small_keep, swap(small_send, fold), FAR)
    small_got = {k: swap(parts[k], 4 * k * fold) for k in (1, 2, 3)}
    last = split(last_kept, last_got, FAR)
    last_got = {k: swap(last[k], 4 * k * fold) for k in (1, 2, 3)}
    small_kept, small_sent = call(
        add_kernel,
        "add",
        (parts[0], small_got[3], small_got[2], small_got[1]),
        [((r_small, both), f32), ((r_small, both), bf16)],
        [],
        1_000_000,
    )
    small_got = swap(small_sent, 2 * fold)
    out_first, out_middle, out_last = call(
        finish_kernel,
        "finish",
        (last[0], last_got[3], last_got[2], last_got[1], small_kept, small_got),
        [(w.shape, f32) for w in (w_first, w_middle, w_last)],
        [],
        1_000_000,
    )
    if fold > 1:
        out_first, out_middle, out_last = (
            lax.psum_scatter(
                out, "cols", scatter_dimension=0, axis_index_groups=neighbours(fold), tiled=True
            )
            for out in (out_first, out_middle, out_last)
        )
    return (out_first, out_middle, out_last)


def solution(mesh):
    placed = (
        P("groups", "cols"),
        P("groups", "cols", None),
        P("cols", None),
        P("cols", None),
        P("cols", None),
    )
    return jax.shard_map(
        on_device,
        mesh=mesh,
        in_specs=placed,
        out_specs=(
            P(("groups", "cols"), None),
            P(("groups", "cols"), None),
            P(("groups", "cols"), None),
        ),
        check_vma=False,
    )
```

```python
import functools

import jax
import jax.numpy as jnp
from jax import lax
from jax.experimental import pallas as pl
from jax.experimental.pallas import tpu as pltpu
from jax.sharding import PartitionSpec as P

epsilon = 1e-06
bf16, f32 = jnp.bfloat16, jnp.float32
MIB = 1024 * 1024
HALO_X, HALO_FIRST, HALO_SECOND, HALO_SLOPE, HALO_BACK = 13, 12, 10, 6, 2
BLOCKS, FAR = 16, 4
LANES = 128
STACK_COST = 3_000_000_000
EARLY_COST = 1_500_000_000
HALF_COST = 1_500_000_000


def swap(array, mask):
    size = lax.axis_size("cols")
    return lax.ppermute(array, "cols", [(i, i ^ mask) for i in range(size)])


def bands_beside(low_pairs, high_pairs):
    size = lax.axis_size("cols")
    bands = size // 4

    def other(i):
        band = i // 4 + (1 if i // 4 % 2 else -1)
        return i ^ 1 if band < 0 or band >= bands else 4 * band + i % 4

    return swap(low_pairs, 4), lax.ppermute(high_pairs, "cols", [(i, other(i)) for i in range(size)])


def neighbours(fold):
    size = lax.axis_size("cols")
    return [list(range(i, i + fold)) for i in range(0, size, fold)]


def position(blocks):
    me = lax.axis_index("cols")
    return me // 4, me % 4, me // (lax.axis_size("cols") // blocks)


def dot(a, b, contract):
    return lax.dot_general(a, b, (contract, ((), ())), preferred_element_type=f32)


def iota(shape, axis):
    return lax.broadcasted_iota(jnp.int32, shape, axis)


def row_shifted(value, step, rows):
    count = value.shape[0]
    if step == 0:
        return value
    row = iota((count, 1), 0) % rows + step
    rolled = pltpu.roll(value, (-step) % count, 0)
    return jnp.where((row >= 0) & (row < rows), rolled, 0.0)


def inside(count, rows, first, total):
    col = iota((count, 1), 0) // rows + first
    return (col >= 0) & (col < total)


def put_patch(patch_ref, value, step, rows, out_cols):
    depth = value.shape[1]
    for ky in range(3):
        moved = row_shifted(value, (ky - 1) * step, rows).astype(bf16)
        for kx in range(3):
            tap = 3 * ky + kx
            start = kx * step * rows
            patch_ref[:, tap * depth : (tap + 1) * depth] = moved[start : start + out_cols * rows]


def spread_back(parts_ref, step, rows, out_cols):
    depth = parts_ref.shape[1] // 9
    total = None
    for ky in range(3):
        line = None
        for kx in range(3):
            tap = 3 * ky + kx
            start = (2 - kx) * step * rows
            piece = parts_ref[start : start + out_cols * rows, tap * depth : (tap + 1) * depth]
            line = piece if line is None else line + piece
        line = row_shifted(line, (1 - ky) * step, rows)
        total = line if total is None else total + line
    return total


def deal_kernel(
    x_hbm,
    teacher_hbm,
    w_first_hbm,
    w_middle_hbm,
    w_last_hbm,
    own_ref,
    near_ref,
    across_ref,
    shard_ref,
    x_ref,
    teacher_ref,
    w_first_ref,
    w_middle_ref,
    w_last_ref,
    pick_x_ref,
    pick_t_ref,
    arrived,
):
    copies = [
        pltpu.make_async_copy(source, target, arrived.at[i])
        for i, (source, target) in enumerate(
            (
                (teacher_hbm, teacher_ref),
                (x_hbm, x_ref),
                (w_last_hbm, w_last_ref),
                (w_middle_hbm, w_middle_ref),
                (w_first_hbm, w_first_ref),
            )
        )
    ]
    for copy in copies:
        copy.start()
    height, breadth, channels = teacher_ref.shape
    depth = x_ref.shape[1] // breadth
    rows, piece = height // 2, breadth // 2
    cells = rows * piece
    low = position(BLOCKS)[1]
    core, row = low % 2, low // 2
    out = iota((cells, 1), 0)
    col, line = out // rows, out % rows
    for rc in range(2):
        line_of = 2 * line + (core ^ rc)
        pick_x_ref[rc] = (iota((cells, piece * height), 1) == col * height + line_of).astype(f32).astype(bf16)
        for ry in range(2):
            source = line_of * breadth + 2 * col + (row ^ ry)
            pick_t_ref[rc, ry] = (iota((cells, height * breadth), 1) == source).astype(f32).astype(bf16)
    for copy in copies:
        copy.wait()
    at = put_tiles(shard_ref, 0, w_last_ref[...])
    at = put_tiles(shard_ref, at, w_middle_ref[...])
    put_tiles(shard_ref, at, w_first_ref[...])
    own_ref[: shard_ref.shape[0]] = shard_ref[...]
    field = teacher_ref[...].reshape(height * breadth, channels)
    pairs = jnp.concatenate(
        [x_ref[:, 2 * depth * i : 2 * depth * (i + 1)] for i in range(piece)], 0
    )
    x_parts = []
    for rc, out_ref in ((0, own_ref), (1, near_ref)):
        both = dot(pick_x_ref[rc], pairs, ((1,), (0,))).astype(bf16)
        low, high = both[:, :depth], both[:, depth:]
        x_parts.append(jnp.where(row == 0, high, low))
        across = dot(pick_t_ref[rc, 1], field, ((1,), (0,))).astype(bf16)
        put_tiles(across_ref, rc * cells * len(tiles(channels)), across)
        value = dot(pick_t_ref[rc, 0], field, ((1,), (0,))).astype(bf16)
        at = put_tiles(out_ref, out_ref.shape[0] - near_ref.shape[0], value)
        x = jnp.where(row == 0, low, high)
        out_ref[at:, :] = jnp.concatenate([x, jnp.zeros_like(x)], 1)
    across_ref[across_ref.shape[0] - cells :, :] = jnp.concatenate(x_parts, 1)


def tiles(width):
    return [(start, min(LANES, width - start)) for start in range(0, width, LANES)]


def put_tiles(ref, at, value):
    rows, width = value.shape
    for start, size in tiles(width):
        ref[at : at + rows, :size] = value[:, start : start + size]
        at += rows
    return at


def take_tiles(value, at, rows, width):
    return jnp.concatenate(
        [
            value[at + i * rows : at + (i + 1) * rows, :size]
            for i, (_, size) in enumerate(tiles(width))
        ],
        1,
    )


def hold_kernel(own_ref, across_ref, held_ref, same_ref):
    held_ref[...] = own_ref[...]


def stack_kernel(own_ref, far3_ref, far1_ref, far2_ref, last_ref, small_ref):
    cut, end = last_ref.shape[1], last_ref.shape[1] + small_ref.shape[1]
    for far, ref in enumerate((own_ref, far1_ref, far2_ref, far3_ref)):
        last_ref[far] = ref[:cut]
        small_ref[far] = ref[cut:end]


def after_kernel(value_ref, first_ref, same_ref):
    pass


def collect_kernel(
    cells,
    edge_t,
    edge_x,
    own_ref,
    near_ref,
    across_ref,
    diagonal_ref,
    last_ref,
    small_ref,
    x_ref,
    teacher_ref,
    edge_a_ref,
    edge_b_ref,
    same_last_ref,
    same_small_ref,
):
    depth, channels = x_ref.shape[1], teacher_ref.shape[1]
    low = position(BLOCKS)[1]
    part = cells * len(tiles(channels))
    skip = own_ref.shape[0] - near_ref.shape[0]
    pieces = ((own_ref, skip, 0), (near_ref, 0, 0), (across_ref, 0, 0), (diagonal_ref, part, depth))
    for k, (ref, row, lane) in enumerate(pieces):
        at = pl.ds(pl.multiple_of((low ^ k) * cells, cells), cells)
        x_ref[at, :] = ref[ref.shape[0] - cells :, lane : lane + depth]
        for lanes, size in tiles(channels):
            teacher_ref[at, lanes : lanes + size] = ref[row : row + cells, :]
            row += cells
    own = teacher_ref.shape[0]
    half = edge_x - edge_t
    odd = position(BLOCKS)[0] % 2
    for ref, high in ((edge_a_ref, 1 - odd), (edge_b_ref, odd)):
        at = pl.ds(pl.multiple_of(high * (own - edge_t), 16), edge_t)
        row = put_tiles(ref, 0, teacher_ref[at, :])
        at = high * (own - edge_x)
        ref[row:, :] = jnp.concatenate(
            [
                x_ref[pl.ds(pl.multiple_of(at, 16), half), :],
                x_ref[pl.ds(pl.multiple_of(at + edge_t, 16), half), :],
            ],
            1,
        )


def sides(edge_a_ref, edge_b_ref):
    a, b = edge_a_ref[...], edge_b_ref[...]
    group, bands = position(BLOCKS)[0], lax.axis_size("cols") // 4
    odd = group % 2 == 1
    before, after = jnp.where(odd, a, b), jnp.where(odd, b, a)
    zero = jnp.zeros_like(a)
    return jnp.where(group == 0, zero, before), jnp.where(group == bands - 1, zero, after)


def edge_x_cells(edge, edge_t, channels):
    packed = edge[edge_t * len(tiles(channels)) :, :]
    depth = LANES // 2
    overlap = packed.shape[0] - edge_t
    return jnp.concatenate([packed[:, :depth], packed[overlap:, depth:]], 0)


def early_kernel(
    own,
    rows,
    total,
    channels,
    edge_t,
    x_ref,
    edge_a_ref,
    edge_b_ref,
    h_ref,
    hy_ref,
    hc_ref,
    hyc_ref,
    tilt_first_ref,
    tilt_second_ref,
    patch_first_ref,
    patch_middle_ref,
    patch_last_ref,
    w_middle_ref,
    small_ref,
):
    group, _, place = position(BLOCKS)
    first_col = group * own
    r_small = small_ref.shape[1] // 2
    in_taps, taps = patch_first_ref.shape[1], patch_middle_ref.shape[1]
    for near, ref in enumerate((h_ref, hc_ref, hy_ref, hyc_ref)):
        for far in range(FAR):
            at = place ^ (4 * far + near)
            small = ref[far].astype(f32)
            row = 0
            for first, width in ((0, taps), (r_small, in_taps)):
                for start, size in tiles(width):
                    small_ref[at, first : first + r_small, start : start + size] = small[
                        row : row + r_small, :size
                    ]
                    row += r_small
    small = small_ref[...]
    w_middle_ref[...] = small[:, :r_small].reshape(-1, taps).astype(bf16)
    w_first = small[:, r_small:, :in_taps].reshape(-1, in_taps).astype(bf16)

    n_first, n_second, n_slope = (
        own + 2 * HALO_FIRST,
        own + 2 * HALO_SECOND,
        own + 2 * HALO_SLOPE,
    )
    before, after = sides(edge_a_ref, edge_b_ref)
    wide = jnp.concatenate(
        [
            edge_x_cells(before, edge_t, channels),
            x_ref[...],
            edge_x_cells(after, edge_t, channels),
        ],
        0,
    )
    put_patch(patch_first_ref, wide.astype(f32), 1, rows, n_first)
    pre = dot(patch_first_ref[...], w_first, ((1,), (1,)))
    sigma = 1.0 / (1.0 + jnp.exp(-pre))
    act = jnp.where(
        inside(n_first * rows, rows, first_col - HALO_FIRST, total), pre * sigma, 0.0
    )
    lo = HALO_FIRST * rows
    pre_own, sigma_own = pre[lo : lo + own * rows], sigma[lo : lo + own * rows]
    tilt_first_ref[...] = sigma_own * (1.0 + pre_own * (1.0 - sigma_own))
    put_patch(patch_middle_ref, act, 2, rows, n_second)

    pre = dot(patch_middle_ref[...], w_middle_ref[...], ((1,), (1,)))
    sigma = 1.0 / (1.0 + jnp.exp(-pre))
    act = jnp.where(
        inside(n_second * rows, rows, first_col - HALO_SECOND, total), pre * sigma, 0.0
    )
    lo, n_back = (HALO_SECOND - HALO_BACK) * rows, (own + 2 * HALO_BACK) * rows
    pre_back, sigma_back = pre[lo : lo + n_back], sigma[lo : lo + n_back]
    tilt_second_ref[...] = jnp.where(
        inside(n_back, rows, first_col - HALO_BACK, total),
        sigma_back * (1.0 + pre_back * (1.0 - sigma_back)),
        0.0,
    )
    put_patch(patch_last_ref, act, 4, rows, n_slope)


def put_blocks(w_ref, blocks, r_last):
    taps = w_ref.shape[1]
    for i, (ref, far) in enumerate(blocks):
        for j, (start, size) in enumerate(tiles(taps)):
            w_ref[i * r_last : (i + 1) * r_last, start : start + size] = ref[
                far, j * r_last : (j + 1) * r_last
            ]


def half_kernel(
    rows,
    edge_t,
    teacher_ref,
    edge_a_ref,
    edge_b_ref,
    patch_last_ref,
    h_ref,
    hy_ref,
    w_own_ref,
    student_ref,
    target_ref,
):
    place = position(BLOCKS)[2]
    channels = teacher_ref.shape[1]
    r_last = channels // BLOCKS
    put_blocks(w_own_ref, [(ref, far) for ref in (h_ref, hy_ref) for far in range(FAR)], r_last)
    student_ref[...] = dot(patch_last_ref[...], w_own_ref[...], ((1,), (1,)))
    before, after = sides(edge_a_ref, edge_b_ref)
    wide = jnp.concatenate(
        [
            take_tiles(before, 0, edge_t, channels),
            teacher_ref[...],
            take_tiles(after, 0, edge_t, channels),
        ],
        0,
    )
    out = iota((1, channels), 1)
    block = out // r_last
    key = 4 * (block % FAR) + 2 * (block // FAR % 2) + block // (2 * FAR)
    source = (key ^ place) * r_last + out % r_last
    pick = (iota((channels, channels), 0) == source).astype(f32).astype(bf16)
    target_ref[...] = dot(wide, pick, ((1,), (0,))).astype(bf16)


def front_kernel(
    own,
    rows,
    total,
    target_ref,
    patch_last_ref,
    student_own_ref,
    hc_ref,
    hyc_ref,
    send_ref,
    slope_ref,
    w_other_ref,
    student_ref,
):
    first_col = position(BLOCKS)[0] * own
    channels = slope_ref.shape[1]
    half = channels // 2
    put_blocks(
        w_other_ref, [(ref, far) for ref in (hc_ref, hyc_ref) for far in range(FAR)], channels // BLOCKS
    )
    student_ref[...] = dot(patch_last_ref[...], w_other_ref[...], ((1,), (1,)))
    block = 4 * rows
    for step in range(slope_ref.shape[0] // block):
        at = pl.ds(step * block, block)
        parts = [
            (student, target_ref[at, lane : lane + half].astype(f32), lane)
            for student, lane in ((student_own_ref[at, :], 0), (student_ref[at, :], half))
        ]

        def total_of(product):
            return sum(jnp.sum(product(s, t), -1, keepdims=True) for s, t, _ in parts)

        s_inv = lax.rsqrt(total_of(lambda s, t: s * s) + epsilon)
        t_inv = lax.rsqrt(total_of(lambda s, t: t * t) + epsilon)
        cosine = total_of(lambda s, t: s * t) * (s_inv * t_inv)
        ok = inside(block, rows, first_col - HALO_SLOPE + step * (block // rows), total)
        s_part = jnp.where(ok, s_inv * s_inv * (cosine + epsilon * (s_inv * s_inv)), 0.0)
        t_part = jnp.where(ok, s_inv * t_inv, 0.0)
        for student, target, lane in parts:
            slope_ref[at, lane : lane + half] = (student * s_part - target * t_part).astype(bf16)

    lo, n_own = HALO_SLOPE * rows, own * rows
    terms = dot(
        slope_ref[lo : lo + n_own, half:], patch_last_ref[lo : lo + n_own, :], ((0,), (0,))
    )
    send_ref[...] = terms.astype(bf16).reshape(send_ref.shape)


def back_kernel(
    own,
    rows,
    slope_ref,
    tilt_second_ref,
    w_own_ref,
    w_other_ref,
    patch_last_ref,
    keep_ref,
    slope_second_ref,
    parts_ref,
):
    half = w_own_ref.shape[0]
    lo, n_own = HALO_SLOPE * rows, own * rows
    terms = dot(
        slope_ref[lo : lo + n_own, :half], patch_last_ref[lo : lo + n_own, :], ((0,), (0,))
    )
    keep_ref[...] = terms.reshape(keep_ref.shape)
    parts_ref[...] = dot(slope_ref[:, :half], w_own_ref[...], ((1,), (0,))) + dot(
        slope_ref[:, half:], w_other_ref[...], ((1,), (0,))
    )
    back_second = spread_back(parts_ref, 4, rows, own + 2 * HALO_BACK)
    slope_second_ref[...] = (back_second * tilt_second_ref[...]).astype(bf16)


def first_kernel(
    own,
    rows,
    slope_second_ref,
    tilt_first_ref,
    patch_first_ref,
    patch_middle_ref,
    w_middle_ref,
    keep_ref,
    send_ref,
    parts_ref,
    terms_ref,
):
    place = position(BLOCKS)[2]
    n_own = own * rows
    slope_second = slope_second_ref[...]
    lo, hi = HALO_BACK * rows, HALO_SECOND * rows
    r_small, middle = terms_ref.shape[1], patch_middle_ref.shape[1]
    grad_middle = dot(
        slope_second[lo : lo + n_own], patch_middle_ref[hi : hi + n_own, :], ((0,), (0,))
    )
    terms_ref[:, :, :middle] = grad_middle.reshape(-1, r_small, middle)
    parts_ref[...] = dot(slope_second, w_middle_ref[...], ((1,), (0,)))
    back_first = spread_back(parts_ref, 2, rows, own)
    slope_first = (back_first * tilt_first_ref[...]).astype(bf16)
    hi = HALO_FIRST * rows
    grad_first = dot(slope_first, patch_first_ref[hi : hi + n_own, :], ((0,), (0,)))
    terms_ref[:, :, middle:] = grad_first.reshape(-1, r_small, grad_first.shape[1])
    for ry in range(2):
        for far in range(FAR):
            at = place ^ (4 * far + 2 * ry)
            keep_ref[far, ry] = terms_ref[at]
            send_ref[far, ry] = terms_ref[at ^ 1].astype(bf16)


def tied_split_kernel(keep_ref, got_ref, tie_ref, *out_refs):
    split_kernel(keep_ref, got_ref, *out_refs)


def split_kernel(keep_ref, got_ref, kept_ref, *send_refs):
    for i, ref in enumerate((kept_ref,) + send_refs):
        ref[...] = (keep_ref[i] + got_ref[i].astype(f32)).astype(ref.dtype)


def add_kernel(keep_ref, got1_ref, got2_ref, got3_ref, kept_ref, send_ref):
    total = keep_ref[...]
    for ref in (got1_ref, got2_ref, got3_ref):
        total = total + ref[...].astype(f32)
    kept_ref[...] = total[0]
    send_ref[...] = total[1].astype(bf16)


def finish_kernel(
    last_ref, got1_ref, got2_ref, got3_ref, small_ref, got_ref, first_ref, middle_ref, out_ref
):
    total = last_ref[...]
    for ref in (got1_ref, got2_ref, got3_ref):
        total = total + ref[...].astype(f32)
    out_ref[...] = total
    small = small_ref[...] + got_ref[...].astype(f32)
    middle_ref[...] = small[:, : middle_ref.shape[1]]
    first_ref[...] = small[:, middle_ref.shape[1] :]


def call(kernel, name, inputs, outs, scratch, flops, spaces=None, semaphores=(), vmem_mib=24, out_spaces=None, aliases=None):
    vmem = pl.BlockSpec(memory_space=pltpu.VMEM)
    spaces = spaces or {}
    return pl.pallas_call(
        kernel,
        in_specs=[spaces.get(i, vmem) for i in range(len(inputs))],
        out_specs=[(out_spaces or {}).get(i, vmem) for i in range(len(outs))],
        input_output_aliases=aliases or {},
        out_shape=[jax.ShapeDtypeStruct(shape, kind) for shape, kind in outs],
        scratch_shapes=[pltpu.VMEM(shape, kind) for shape, kind in scratch] + list(semaphores),
        compiler_params=pltpu.CompilerParams(vmem_limit_bytes=int(vmem_mib * MIB)),
        cost_estimate=pl.CostEstimate(flops=flops, bytes_accessed=1_000_000, transcendentals=0),
        name=name,
    )(*inputs)


def on_device(image_feats, teacher, w_first, w_middle, w_last):
    size = lax.axis_size("cols")
    fold = size // BLOCKS
    height, breadth, channels = teacher.shape
    in_depth = w_first.shape[1] // 9
    hidden = w_middle.shape[1] // 9
    rows, piece = height // 2, breadth // 2
    own = 4 * piece
    total = own * (size // 4)

    if fold > 1:
        w_first, w_middle, w_last = (
            lax.all_gather(w, "cols", axis_index_groups=neighbours(fold), axis=0, tiled=True)
            for w in (w_first, w_middle, w_last)
        )
    r_last, r_small = w_last.shape[0], w_first.shape[0]
    cells = piece * rows
    dealt = cells * len(tiles(channels)) + cells
    packed = r_last * len(tiles(9 * hidden))
    packed += r_small * (len(tiles(9 * hidden)) + len(tiles(9 * in_depth)))
    hbm = pl.BlockSpec(memory_space=pltpu.HBM)
    own_class, near, across, shard = call(
        deal_kernel,
        "deal",
        (image_feats, teacher, w_first, w_middle, w_last),
        [
            ((packed + dealt, LANES), bf16),
            ((dealt, LANES), bf16),
            ((2 * dealt - cells, LANES), bf16),
            ((packed, LANES), bf16),
        ],
        [(a.shape, a.dtype) for a in (image_feats, teacher, w_first, w_middle, w_last)]
        + [((2, cells, piece * height), bf16), ((2, 2, cells, height * breadth), bf16)],
        600_000_000,
        {i: hbm for i in range(5)},
        [pltpu.SemaphoreType.DMA((5,))],
        60,
    )
    across = swap(across, 2)
    far = {k: swap(shard, 4 * k * fold) for k in (1, 2, 3)}
    near = swap(near, 1)
    anywhere = pl.BlockSpec(memory_space=pl.ANY)
    held, across = call(
        hold_kernel,
        "hold",
        (own_class, across),
        [(own_class.shape, bf16), (across.shape, bf16)],
        [],
        1_000_000,
        {1: anywhere},
        out_spaces={1: anywhere},
        aliases={1: 1},
    )
    diagonal = swap(across, 1)
    edge_t, edge_x = HALO_SLOPE * rows, HALO_X * rows
    edge = edge_t * len(tiles(channels)) + edge_x - edge_t
    part_last = r_last * len(tiles(9 * hidden))
    held_last, held_small = call(
        stack_kernel,
        "stack",
        (held, far[3], far[1], far[2]),
        [((FAR, part_last, LANES), bf16), ((FAR, packed - part_last, LANES), bf16)],
        [],
        STACK_COST,
    )
    x_band, t_band, edge_a, edge_b, held_last, held_small = call(
        functools.partial(collect_kernel, cells, edge_t, edge_x),
        "collect",
        (held, near, across, diagonal, held_last, held_small),
        [
            ((own * rows, in_depth), bf16),
            ((own * rows, channels), bf16),
            ((edge, LANES), bf16),
            ((edge, LANES), bf16),
            (held_last.shape, bf16),
            (held_small.shape, bf16),
        ],
        [],
        1_000_000,
        {4: anywhere, 5: anywhere},
        out_spaces={4: anywhere, 5: anywhere},
        aliases={4: 4, 5: 5},
    )

    small_y = swap(held_small, 2 * fold)
    last_y = swap(held_last, 2 * fold)
    all_small = held_small, small_y, swap(held_small, fold), swap(small_y, fold)
    edge_a, edge_b = bands_beside(edge_a, edge_b)

    n_first, n_second, n_slope, n_back = (
        (own + 2 * halo) * rows for halo in (HALO_FIRST, HALO_SECOND, HALO_SLOPE, HALO_BACK)
    )
    tilt_first, tilt_second, patch_first, patch_middle, patch_last, all_middle = call(
        functools.partial(early_kernel, own, rows, total, channels, edge_t),
        "early",
        (x_band, edge_a, edge_b, *all_small),
        [
            ((own * rows, hidden), f32),
            ((n_back, hidden), f32),
            ((n_first, 9 * in_depth), bf16),
            ((n_second, 9 * hidden), bf16),
            ((n_slope, 9 * hidden), bf16),
            ((hidden, 9 * hidden), bf16),
        ],
        [((BLOCKS, 2 * r_small, 9 * hidden), f32)],
        EARLY_COST,
    )
    (last_y,) = call(
        after_kernel,
        "after",
        (last_y, patch_last),
        [(last_y.shape, bf16)],
        [],
        1_000_000,
        {0: anywhere, 1: anywhere},
        out_spaces={0: anywhere},
        aliases={0: 0},
    )
    half = channels // 2
    last_c, last_yc = swap(held_last, fold), swap(last_y, fold)
    w_own, student_own, target = call(
        functools.partial(half_kernel, rows, edge_t),
        "half",
        (t_band, edge_a, edge_b, patch_last, held_last, last_y),
        [
            ((half, 9 * hidden), bf16),
            ((n_slope, half), f32),
            ((n_slope, channels), bf16),
        ],
        [],
        HALF_COST,
    )
    send, slope, w_other = call(
        functools.partial(front_kernel, own, rows, total),
        "front",
        (target, patch_last, student_own, last_c, last_yc),
        [
            ((2, FAR, r_last, 9 * hidden), bf16),
            ((n_slope, channels), bf16),
            ((half, 9 * hidden), bf16),
        ],
        [((n_slope, half), f32)],
        6_000_000_000,
    )
    got = swap(send, fold)
    keep, slope_second = call(
        functools.partial(back_kernel, own, rows),
        "back",
        (slope, tilt_second, w_own, w_other, patch_last),
        [((2, FAR, r_last, 9 * hidden), f32), ((n_back, hidden), bf16)],
        [((n_slope, 9 * hidden), f32)],
        4_000_000_000,
    )
    both = 9 * (hidden + in_depth)
    small_keep, small_send = call(
        functools.partial(first_kernel, own, rows),
        "first",
        (slope_second, tilt_first, patch_first, patch_middle, all_middle),
        [((FAR, 2, r_small, both), f32), ((FAR, 2, r_small, both), bf16)],
        [((n_back, 9 * hidden), f32), ((BLOCKS, r_small, both), f32)],
        2_000_000_000,
    )

    def split(keep, got, count):
        shape = keep.shape[1:]
        outs = [(shape, f32)] + [(shape, bf16)] * (count - 1)
        return call(split_kernel, "split", (keep, got), outs, [], 1_000_000)

    last_kept, last_sent = call(
        tied_split_kernel,
        "split",
        (keep, got, slope_second),
        [(keep.shape[1:], f32), (keep.shape[1:], bf16)],
        [],
        1_000_000,
        {2: anywhere},
    )
    last_got = swap(last_sent, 2 * fold)
    parts = split(small_keep, swap(small_send, fold), FAR)
    small_got = {k: swap(parts[k], 4 * k * fold) for k in (1, 2, 3)}
    last = split(last_kept, last_got, FAR)
    last_got = {k: swap(last[k], 4 * k * fold) for k in (1, 2, 3)}
    small_kept, small_sent = call(
        add_kernel,
        "add",
        (parts[0], small_got[3], small_got[2], small_got[1]),
        [((r_small, both), f32), ((r_small, both), bf16)],
        [],
        1_000_000,
    )
    small_got = swap(small_sent, 2 * fold)
    out_first, out_middle, out_last = call(
        finish_kernel,
        "finish",
        (last[0], last_got[3], last_got[2], last_got[1], small_kept, small_got),
        [(w.shape, f32) for w in (w_first, w_middle, w_last)],
        [],
        1_000_000,
    )
    if fold > 1:
        out_first, out_middle, out_last = (
            lax.psum_scatter(
                out, "cols", scatter_dimension=0, axis_index_groups=neighbours(fold), tiled=True
            )
            for out in (out_first, out_middle, out_last)
        )
    return (out_first, out_middle, out_last)


def solution(mesh):
    placed = (
        P("groups", "cols"),
        P("groups", "cols", None),
        P("cols", None),
        P("cols", None),
        P("cols", None),
    )
    return jax.shard_map(
        on_device,
        mesh=mesh,
        in_specs=placed,
        out_specs=(
            P(("groups", "cols"), None),
            P(("groups", "cols"), None),
            P(("groups", "cols"), None),
        ),
        check_vma=False,
    )
```

```python
import functools

import jax
import jax.numpy as jnp
from jax import lax
from jax.experimental import pallas as pl
from jax.experimental.pallas import tpu as pltpu
from jax.sharding import PartitionSpec as P

epsilon = 1e-06
bf16, f32 = jnp.bfloat16, jnp.float32
MIB = 1024 * 1024
HALO_X, HALO_FIRST, HALO_SECOND, HALO_SLOPE, HALO_BACK = 13, 12, 10, 6, 2
BLOCKS, FAR = 16, 4
LANES = 128
STACK_COST = 3_000_000_000
EARLY_COST = 1_500_000_000
HALF_COST = 1_500_000_000


def swap(array, mask):
    size = lax.axis_size("cols")
    return lax.ppermute(array, "cols", [(i, i ^ mask) for i in range(size)])


def bands_beside(low_pairs, high_pairs):
    size = lax.axis_size("cols")
    bands = size // 4

    def other(i):
        band = i // 4 + (1 if i // 4 % 2 else -1)
        return i ^ 1 if band < 0 or band >= bands else 4 * band + i % 4

    return swap(low_pairs, 4), lax.ppermute(high_pairs, "cols", [(i, other(i)) for i in range(size)])


def neighbours(fold):
    size = lax.axis_size("cols")
    return [list(range(i, i + fold)) for i in range(0, size, fold)]


def position(blocks):
    me = lax.axis_index("cols")
    return me // 4, me % 4, me // (lax.axis_size("cols") // blocks)


def dot(a, b, contract):
    return lax.dot_general(a, b, (contract, ((), ())), preferred_element_type=f32)


def iota(shape, axis):
    return lax.broadcasted_iota(jnp.int32, shape, axis)


def row_shifted(value, step, rows):
    count = value.shape[0]
    if step == 0:
        return value
    row = iota((count, 1), 0) % rows + step
    rolled = pltpu.roll(value, (-step) % count, 0)
    return jnp.where((row >= 0) & (row < rows), rolled, 0.0)


def inside(count, rows, first, total):
    col = iota((count, 1), 0) // rows + first
    return (col >= 0) & (col < total)


def put_patch(patch_ref, value, step, rows, out_cols):
    depth = value.shape[1]
    for ky in range(3):
        moved = row_shifted(value, (ky - 1) * step, rows).astype(bf16)
        for kx in range(3):
            tap = 3 * ky + kx
            start = kx * step * rows
            patch_ref[:, tap * depth : (tap + 1) * depth] = moved[start : start + out_cols * rows]


def spread_back(parts_ref, step, rows, out_cols):
    depth = parts_ref.shape[1] // 9
    total = None
    for ky in range(3):
        line = None
        for kx in range(3):
            tap = 3 * ky + kx
            start = (2 - kx) * step * rows
            piece = parts_ref[start : start + out_cols * rows, tap * depth : (tap + 1) * depth]
            line = piece if line is None else line + piece
        line = row_shifted(line, (1 - ky) * step, rows)
        total = line if total is None else total + line
    return total


def deal_kernel(
    x_hbm,
    teacher_hbm,
    w_first_hbm,
    w_middle_hbm,
    w_last_hbm,
    own_ref,
    near_ref,
    across_ref,
    shard_ref,
    x_ref,
    teacher_ref,
    w_first_ref,
    w_middle_ref,
    w_last_ref,
    pick_x_ref,
    pick_t_ref,
    arrived,
):
    copies = [
        pltpu.make_async_copy(source, target, arrived.at[i])
        for i, (source, target) in enumerate(
            (
                (teacher_hbm, teacher_ref),
                (x_hbm, x_ref),
                (w_last_hbm, w_last_ref),
                (w_middle_hbm, w_middle_ref),
                (w_first_hbm, w_first_ref),
            )
        )
    ]
    for copy in copies:
        copy.start()
    height, breadth, channels = teacher_ref.shape
    depth = x_ref.shape[1] // breadth
    rows, piece = height // 2, breadth // 2
    cells = rows * piece
    low = position(BLOCKS)[1]
    core, row = low % 2, low // 2
    out = iota((cells, 1), 0)
    col, line = out // rows, out % rows
    for rc in range(2):
        line_of = 2 * line + (core ^ rc)
        pick_x_ref[rc] = (iota((cells, piece * height), 1) == col * height + line_of).astype(f32).astype(bf16)
        for ry in range(2):
            source = line_of * breadth + 2 * col + (row ^ ry)
            pick_t_ref[rc, ry] = (iota((cells, height * breadth), 1) == source).astype(f32).astype(bf16)
    for copy in copies:
        copy.wait()
    at = put_tiles(shard_ref, 0, w_last_ref[...])
    at = put_tiles(shard_ref, at, w_middle_ref[...])
    put_tiles(shard_ref, at, w_first_ref[...])
    own_ref[: shard_ref.shape[0]] = shard_ref[...]
    field = teacher_ref[...].reshape(height * breadth, channels)
    pairs = jnp.concatenate(
        [x_ref[:, 2 * depth * i : 2 * depth * (i + 1)] for i in range(piece)], 0
    )
    x_parts = []
    for rc, out_ref in ((0, own_ref), (1, near_ref)):
        both = dot(pick_x_ref[rc], pairs, ((1,), (0,))).astype(bf16)
        low, high = both[:, :depth], both[:, depth:]
        x_parts.append(jnp.where(row == 0, high, low))
        across = dot(pick_t_ref[rc, 1], field, ((1,), (0,))).astype(bf16)
        put_tiles(across_ref, rc * cells * len(tiles(channels)), across)
        value = dot(pick_t_ref[rc, 0], field, ((1,), (0,))).astype(bf16)
        at = put_tiles(out_ref, out_ref.shape[0] - near_ref.shape[0], value)
        x = jnp.where(row == 0, low, high)
        out_ref[at:, :] = jnp.concatenate([x, jnp.zeros_like(x)], 1)
    across_ref[across_ref.shape[0] - cells :, :] = jnp.concatenate(x_parts, 1)


def tiles(width):
    return [(start, min(LANES, width - start)) for start in range(0, width, LANES)]


def put_tiles(ref, at, value):
    rows, width = value.shape
    for start, size in tiles(width):
        ref[at : at + rows, :size] = value[:, start : start + size]
        at += rows
    return at


def take_tiles(value, at, rows, width):
    return jnp.concatenate(
        [
            value[at + i * rows : at + (i + 1) * rows, :size]
            for i, (_, size) in enumerate(tiles(width))
        ],
        1,
    )


def hold_kernel(own_ref, far_ref, held_ref, same_ref):
    held_ref[...] = own_ref[...]


def stack_kernel(own_ref, far3_ref, far1_ref, far2_ref, last_ref, small_ref):
    cut, end = last_ref.shape[1], last_ref.shape[1] + small_ref.shape[1]
    for far, ref in enumerate((own_ref, far1_ref, far2_ref, far3_ref)):
        last_ref[far] = ref[:cut]
        small_ref[far] = ref[cut:end]


def after_kernel(value_ref, first_ref, same_ref):
    pass


def collect_kernel(
    cells,
    edge_t,
    edge_x,
    own_ref,
    near_ref,
    across_ref,
    diagonal_ref,
    x_ref,
    teacher_ref,
    edge_a_ref,
    edge_b_ref,
):
    depth, channels = x_ref.shape[1], teacher_ref.shape[1]
    low = position(BLOCKS)[1]
    part = cells * len(tiles(channels))
    skip = own_ref.shape[0] - near_ref.shape[0]
    pieces = ((own_ref, skip, 0), (near_ref, 0, 0), (across_ref, 0, 0), (diagonal_ref, part, depth))
    for k, (ref, row, lane) in enumerate(pieces):
        at = pl.ds(pl.multiple_of((low ^ k) * cells, cells), cells)
        x_ref[at, :] = ref[ref.shape[0] - cells :, lane : lane + depth]
        for lanes, size in tiles(channels):
            teacher_ref[at, lanes : lanes + size] = ref[row : row + cells, :]
            row += cells
    own = teacher_ref.shape[0]
    half = edge_x - edge_t
    odd = position(BLOCKS)[0] % 2
    for ref, high in ((edge_a_ref, 1 - odd), (edge_b_ref, odd)):
        at = pl.ds(pl.multiple_of(high * (own - edge_t), 16), edge_t)
        row = put_tiles(ref, 0, teacher_ref[at, :])
        at = high * (own - edge_x)
        ref[row:, :] = jnp.concatenate(
            [
                x_ref[pl.ds(pl.multiple_of(at, 16), half), :],
                x_ref[pl.ds(pl.multiple_of(at + edge_t, 16), half), :],
            ],
            1,
        )


def sides(edge_a_ref, edge_b_ref):
    a, b = edge_a_ref[...], edge_b_ref[...]
    group, bands = position(BLOCKS)[0], lax.axis_size("cols") // 4
    odd = group % 2 == 1
    before, after = jnp.where(odd, a, b), jnp.where(odd, b, a)
    zero = jnp.zeros_like(a)
    return jnp.where(group == 0, zero, before), jnp.where(group == bands - 1, zero, after)


def edge_x_cells(edge, edge_t, channels):
    packed = edge[edge_t * len(tiles(channels)) :, :]
    depth = LANES // 2
    overlap = packed.shape[0] - edge_t
    return jnp.concatenate([packed[:, :depth], packed[overlap:, depth:]], 0)


def early_kernel(
    own,
    rows,
    total,
    channels,
    edge_t,
    x_ref,
    edge_a_ref,
    edge_b_ref,
    h_ref,
    hy_ref,
    hc_ref,
    hyc_ref,
    tilt_first_ref,
    tilt_second_ref,
    patch_first_ref,
    patch_middle_ref,
    patch_last_ref,
    w_middle_ref,
    small_ref,
):
    group, _, place = position(BLOCKS)
    first_col = group * own
    r_small = small_ref.shape[1] // 2
    in_taps, taps = patch_first_ref.shape[1], patch_middle_ref.shape[1]
    for near, ref in enumerate((h_ref, hc_ref, hy_ref, hyc_ref)):
        for far in range(FAR):
            at = place ^ (4 * far + near)
            small = ref[far].astype(f32)
            row = 0
            for first, width in ((0, taps), (r_small, in_taps)):
                for start, size in tiles(width):
                    small_ref[at, first : first + r_small, start : start + size] = small[
                        row : row + r_small, :size
                    ]
                    row += r_small
    small = small_ref[...]
    w_middle_ref[...] = small[:, :r_small].reshape(-1, taps).astype(bf16)
    w_first = small[:, r_small:, :in_taps].reshape(-1, in_taps).astype(bf16)

    n_first, n_second, n_slope = (
        own + 2 * HALO_FIRST,
        own + 2 * HALO_SECOND,
        own + 2 * HALO_SLOPE,
    )
    before, after = sides(edge_a_ref, edge_b_ref)
    wide = jnp.concatenate(
        [
            edge_x_cells(before, edge_t, channels),
            x_ref[...],
            edge_x_cells(after, edge_t, channels),
        ],
        0,
    )
    put_patch(patch_first_ref, wide.astype(f32), 1, rows, n_first)
    pre = dot(patch_first_ref[...], w_first, ((1,), (1,)))
    sigma = 1.0 / (1.0 + jnp.exp(-pre))
    act = jnp.where(
        inside(n_first * rows, rows, first_col - HALO_FIRST, total), pre * sigma, 0.0
    )
    lo = HALO_FIRST * rows
    pre_own, sigma_own = pre[lo : lo + own * rows], sigma[lo : lo + own * rows]
    tilt_first_ref[...] = sigma_own * (1.0 + pre_own * (1.0 - sigma_own))
    put_patch(patch_middle_ref, act, 2, rows, n_second)

    pre = dot(patch_middle_ref[...], w_middle_ref[...], ((1,), (1,)))
    sigma = 1.0 / (1.0 + jnp.exp(-pre))
    act = jnp.where(
        inside(n_second * rows, rows, first_col - HALO_SECOND, total), pre * sigma, 0.0
    )
    lo, n_back = (HALO_SECOND - HALO_BACK) * rows, (own + 2 * HALO_BACK) * rows
    pre_back, sigma_back = pre[lo : lo + n_back], sigma[lo : lo + n_back]
    tilt_second_ref[...] = jnp.where(
        inside(n_back, rows, first_col - HALO_BACK, total),
        sigma_back * (1.0 + pre_back * (1.0 - sigma_back)),
        0.0,
    )
    put_patch(patch_last_ref, act, 4, rows, n_slope)


def put_blocks(w_ref, blocks, r_last):
    taps = w_ref.shape[1]
    for i, (ref, far) in enumerate(blocks):
        for j, (start, size) in enumerate(tiles(taps)):
            w_ref[i * r_last : (i + 1) * r_last, start : start + size] = ref[
                far, j * r_last : (j + 1) * r_last
            ]


def half_kernel(
    rows,
    edge_t,
    teacher_ref,
    edge_a_ref,
    edge_b_ref,
    patch_last_ref,
    h_ref,
    hy_ref,
    w_own_ref,
    student_ref,
    target_ref,
):
    place = position(BLOCKS)[2]
    channels = teacher_ref.shape[1]
    r_last = channels // BLOCKS
    put_blocks(w_own_ref, [(ref, far) for ref in (h_ref, hy_ref) for far in range(FAR)], r_last)
    student_ref[...] = dot(patch_last_ref[...], w_own_ref[...], ((1,), (1,)))
    before, after = sides(edge_a_ref, edge_b_ref)
    wide = jnp.concatenate(
        [
            take_tiles(before, 0, edge_t, channels),
            teacher_ref[...],
            take_tiles(after, 0, edge_t, channels),
        ],
        0,
    )
    out = iota((1, channels), 1)
    block = out // r_last
    key = 4 * (block % FAR) + 2 * (block // FAR % 2) + block // (2 * FAR)
    source = (key ^ place) * r_last + out % r_last
    pick = (iota((channels, channels), 0) == source).astype(f32).astype(bf16)
    target_ref[...] = dot(wide, pick, ((1,), (0,))).astype(bf16)


def front_kernel(
    own,
    rows,
    total,
    target_ref,
    patch_last_ref,
    student_own_ref,
    hc_ref,
    hyc_ref,
    send_ref,
    slope_ref,
    w_other_ref,
    student_ref,
):
    first_col = position(BLOCKS)[0] * own
    channels = slope_ref.shape[1]
    half = channels // 2
    put_blocks(
        w_other_ref, [(ref, far) for ref in (hc_ref, hyc_ref) for far in range(FAR)], channels // BLOCKS
    )
    student_ref[...] = dot(patch_last_ref[...], w_other_ref[...], ((1,), (1,)))
    block = 4 * rows
    for step in range(slope_ref.shape[0] // block):
        at = pl.ds(step * block, block)
        parts = [
            (student, target_ref[at, lane : lane + half].astype(f32), lane)
            for student, lane in ((student_own_ref[at, :], 0), (student_ref[at, :], half))
        ]

        def total_of(product):
            return sum(jnp.sum(product(s, t), -1, keepdims=True) for s, t, _ in parts)

        s_inv = lax.rsqrt(total_of(lambda s, t: s * s) + epsilon)
        t_inv = lax.rsqrt(total_of(lambda s, t: t * t) + epsilon)
        cosine = total_of(lambda s, t: s * t) * (s_inv * t_inv)
        ok = inside(block, rows, first_col - HALO_SLOPE + step * (block // rows), total)
        s_part = jnp.where(ok, s_inv * s_inv * (cosine + epsilon * (s_inv * s_inv)), 0.0)
        t_part = jnp.where(ok, s_inv * t_inv, 0.0)
        for student, target, lane in parts:
            slope_ref[at, lane : lane + half] = (student * s_part - target * t_part).astype(bf16)

    lo, n_own = HALO_SLOPE * rows, own * rows
    terms = dot(
        slope_ref[lo : lo + n_own, half:], patch_last_ref[lo : lo + n_own, :], ((0,), (0,))
    )
    send_ref[...] = terms.astype(bf16).reshape(send_ref.shape)


def back_kernel(
    own,
    rows,
    slope_ref,
    tilt_second_ref,
    w_own_ref,
    w_other_ref,
    patch_last_ref,
    keep_ref,
    slope_second_ref,
    parts_ref,
):
    half = w_own_ref.shape[0]
    lo, n_own = HALO_SLOPE * rows, own * rows
    terms = dot(
        slope_ref[lo : lo + n_own, :half], patch_last_ref[lo : lo + n_own, :], ((0,), (0,))
    )
    keep_ref[...] = terms.reshape(keep_ref.shape)
    parts_ref[...] = dot(slope_ref[:, :half], w_own_ref[...], ((1,), (0,))) + dot(
        slope_ref[:, half:], w_other_ref[...], ((1,), (0,))
    )
    back_second = spread_back(parts_ref, 4, rows, own + 2 * HALO_BACK)
    slope_second_ref[...] = (back_second * tilt_second_ref[...]).astype(bf16)


def first_kernel(
    own,
    rows,
    slope_second_ref,
    tilt_first_ref,
    patch_first_ref,
    patch_middle_ref,
    w_middle_ref,
    keep_ref,
    send_ref,
    parts_ref,
    terms_ref,
):
    place = position(BLOCKS)[2]
    n_own = own * rows
    slope_second = slope_second_ref[...]
    lo, hi = HALO_BACK * rows, HALO_SECOND * rows
    r_small, middle = terms_ref.shape[1], patch_middle_ref.shape[1]
    grad_middle = dot(
        slope_second[lo : lo + n_own], patch_middle_ref[hi : hi + n_own, :], ((0,), (0,))
    )
    terms_ref[:, :, :middle] = grad_middle.reshape(-1, r_small, middle)
    parts_ref[...] = dot(slope_second, w_middle_ref[...], ((1,), (0,)))
    back_first = spread_back(parts_ref, 2, rows, own)
    slope_first = (back_first * tilt_first_ref[...]).astype(bf16)
    hi = HALO_FIRST * rows
    grad_first = dot(slope_first, patch_first_ref[hi : hi + n_own, :], ((0,), (0,)))
    terms_ref[:, :, middle:] = grad_first.reshape(-1, r_small, grad_first.shape[1])
    for ry in range(2):
        for far in range(FAR):
            at = place ^ (4 * far + 2 * ry)
            keep_ref[far, ry] = terms_ref[at]
            send_ref[far, ry] = terms_ref[at ^ 1].astype(bf16)


def tied_split_kernel(keep_ref, got_ref, tie_ref, *out_refs):
    split_kernel(keep_ref, got_ref, *out_refs)


def split_kernel(keep_ref, got_ref, kept_ref, *send_refs):
    for i, ref in enumerate((kept_ref,) + send_refs):
        ref[...] = (keep_ref[i] + got_ref[i].astype(f32)).astype(ref.dtype)


def add_kernel(keep_ref, got1_ref, got2_ref, got3_ref, kept_ref, send_ref):
    total = keep_ref[...]
    for ref in (got1_ref, got2_ref, got3_ref):
        total = total + ref[...].astype(f32)
    kept_ref[...] = total[0]
    send_ref[...] = total[1].astype(bf16)


def finish_kernel(
    last_ref, got1_ref, got2_ref, got3_ref, small_ref, got_ref, first_ref, middle_ref, out_ref
):
    total = last_ref[...]
    for ref in (got1_ref, got2_ref, got3_ref):
        total = total + ref[...].astype(f32)
    out_ref[...] = total
    small = small_ref[...] + got_ref[...].astype(f32)
    middle_ref[...] = small[:, : middle_ref.shape[1]]
    first_ref[...] = small[:, middle_ref.shape[1] :]


def call(kernel, name, inputs, outs, scratch, flops, spaces=None, semaphores=(), vmem_mib=24, out_spaces=None, aliases=None):
    vmem = pl.BlockSpec(memory_space=pltpu.VMEM)
    spaces = spaces or {}
    return pl.pallas_call(
        kernel,
        in_specs=[spaces.get(i, vmem) for i in range(len(inputs))],
        out_specs=[(out_spaces or {}).get(i, vmem) for i in range(len(outs))],
        input_output_aliases=aliases or {},
        out_shape=[jax.ShapeDtypeStruct(shape, kind) for shape, kind in outs],
        scratch_shapes=[pltpu.VMEM(shape, kind) for shape, kind in scratch] + list(semaphores),
        compiler_params=pltpu.CompilerParams(vmem_limit_bytes=int(vmem_mib * MIB)),
        cost_estimate=pl.CostEstimate(flops=flops, bytes_accessed=1_000_000, transcendentals=0),
        name=name,
    )(*inputs)


def on_device(image_feats, teacher, w_first, w_middle, w_last):
    size = lax.axis_size("cols")
    fold = size // BLOCKS
    height, breadth, channels = teacher.shape
    in_depth = w_first.shape[1] // 9
    hidden = w_middle.shape[1] // 9
    rows, piece = height // 2, breadth // 2
    own = 4 * piece
    total = own * (size // 4)

    if fold > 1:
        w_first, w_middle, w_last = (
            lax.all_gather(w, "cols", axis_index_groups=neighbours(fold), axis=0, tiled=True)
            for w in (w_first, w_middle, w_last)
        )
    r_last, r_small = w_last.shape[0], w_first.shape[0]
    cells = piece * rows
    dealt = cells * len(tiles(channels)) + cells
    packed = r_last * len(tiles(9 * hidden))
    packed += r_small * (len(tiles(9 * hidden)) + len(tiles(9 * in_depth)))
    hbm = pl.BlockSpec(memory_space=pltpu.HBM)
    own_class, near, across, shard = call(
        deal_kernel,
        "deal",
        (image_feats, teacher, w_first, w_middle, w_last),
        [
            ((packed + dealt, LANES), bf16),
            ((dealt, LANES), bf16),
            ((2 * dealt - cells, LANES), bf16),
            ((packed, LANES), bf16),
        ],
        [(a.shape, a.dtype) for a in (image_feats, teacher, w_first, w_middle, w_last)]
        + [((2, cells, piece * height), bf16), ((2, 2, cells, height * breadth), bf16)],
        600_000_000,
        {i: hbm for i in range(5)},
        [pltpu.SemaphoreType.DMA((5,))],
        60,
    )
    across = swap(across, 2)
    far = {k: swap(shard, 4 * k * fold) for k in (1, 2, 3)}
    near = swap(near, 1)
    anywhere = pl.BlockSpec(memory_space=pl.ANY)

    def behind(value, first):
        return call(
            after_kernel,
            "after",
            (value, first),
            [(value.shape, value.dtype)],
            [],
            1_000_000,
            {0: anywhere, 1: anywhere},
            out_spaces={0: anywhere},
            aliases={0: 0},
        )[0]

    diagonal = swap(across, 1)
    held, far[1] = call(
        hold_kernel,
        "hold",
        (own_class, far[1]),
        [(own_class.shape, bf16), (shard.shape, bf16)],
        [],
        1_000_000,
        {1: anywhere},
        out_spaces={1: anywhere},
        aliases={1: 1},
    )
    edge_t, edge_x = HALO_SLOPE * rows, HALO_X * rows
    edge = edge_t * len(tiles(channels)) + edge_x - edge_t
    part_last = r_last * len(tiles(9 * hidden))
    held_last, held_small = call(
        stack_kernel,
        "stack",
        (held, far[3], far[1], far[2]),
        [((FAR, part_last, LANES), bf16), ((FAR, packed - part_last, LANES), bf16)],
        [],
        STACK_COST,
    )
    x_band, t_band, edge_a, edge_b = call(
        functools.partial(collect_kernel, cells, edge_t, edge_x),
        "collect",
        (held, near, across, diagonal),
        [
            ((own * rows, in_depth), bf16),
            ((own * rows, channels), bf16),
            ((edge, LANES), bf16),
            ((edge, LANES), bf16),
        ],
        [],
        1_000_000,
    )

    small_y = swap(held_small, 2 * fold)
    last_y = swap(held_last, 2 * fold)
    all_small = held_small, small_y, swap(held_small, fold), swap(small_y, fold)
    edge_a, edge_b = bands_beside(edge_a, edge_b)

    n_first, n_second, n_slope, n_back = (
        (own + 2 * halo) * rows for halo in (HALO_FIRST, HALO_SECOND, HALO_SLOPE, HALO_BACK)
    )
    tilt_first, tilt_second, patch_first, patch_middle, patch_last, all_middle = call(
        functools.partial(early_kernel, own, rows, total, channels, edge_t),
        "early",
        (x_band, edge_a, edge_b, *all_small),
        [
            ((own * rows, hidden), f32),
            ((n_back, hidden), f32),
            ((n_first, 9 * in_depth), bf16),
            ((n_second, 9 * hidden), bf16),
            ((n_slope, 9 * hidden), bf16),
            ((hidden, 9 * hidden), bf16),
        ],
        [((BLOCKS, 2 * r_small, 9 * hidden), f32)],
        EARLY_COST,
    )
    last_y = behind(last_y, patch_last)
    half = channels // 2
    last_c, last_yc = swap(held_last, fold), swap(last_y, fold)
    w_own, student_own, target = call(
        functools.partial(half_kernel, rows, edge_t),
        "half",
        (t_band, edge_a, edge_b, patch_last, held_last, last_y),
        [
            ((half, 9 * hidden), bf16),
            ((n_slope, half), f32),
            ((n_slope, channels), bf16),
        ],
        [],
        HALF_COST,
    )
    send, slope, w_other = call(
        functools.partial(front_kernel, own, rows, total),
        "front",
        (target, patch_last, student_own, last_c, last_yc),
        [
            ((2, FAR, r_last, 9 * hidden), bf16),
            ((n_slope, channels), bf16),
            ((half, 9 * hidden), bf16),
        ],
        [((n_slope, half), f32)],
        6_000_000_000,
    )
    got = swap(send, fold)
    keep, slope_second = call(
        functools.partial(back_kernel, own, rows),
        "back",
        (slope, tilt_second, w_own, w_other, patch_last),
        [((2, FAR, r_last, 9 * hidden), f32), ((n_back, hidden), bf16)],
        [((n_slope, 9 * hidden), f32)],
        4_000_000_000,
    )
    both = 9 * (hidden + in_depth)
    small_keep, small_send = call(
        functools.partial(first_kernel, own, rows),
        "first",
        (slope_second, tilt_first, patch_first, patch_middle, all_middle),
        [((FAR, 2, r_small, both), f32), ((FAR, 2, r_small, both), bf16)],
        [((n_back, 9 * hidden), f32), ((BLOCKS, r_small, both), f32)],
        2_000_000_000,
    )

    def split(keep, got, count):
        shape = keep.shape[1:]
        outs = [(shape, f32)] + [(shape, bf16)] * (count - 1)
        return call(split_kernel, "split", (keep, got), outs, [], 1_000_000)

    last_kept, last_sent = call(
        tied_split_kernel,
        "split",
        (keep, got, slope_second),
        [(keep.shape[1:], f32), (keep.shape[1:], bf16)],
        [],
        1_000_000,
        {2: anywhere},
    )
    last_got = swap(last_sent, 2 * fold)
    parts = split(small_keep, swap(small_send, fold), FAR)
    small_got = {k: swap(parts[k], 4 * k * fold) for k in (1, 2, 3)}
    last = split(last_kept, last_got, FAR)
    last_got = {k: swap(last[k], 4 * k * fold) for k in (1, 2, 3)}
    small_kept, small_sent = call(
        add_kernel,
        "add",
        (parts[0], small_got[3], small_got[2], small_got[1]),
        [((r_small, both), f32), ((r_small, both), bf16)],
        [],
        1_000_000,
    )
    small_got = swap(small_sent, 2 * fold)
    out_first, out_middle, out_last = call(
        finish_kernel,
        "finish",
        (last[0], last_got[2], last_got[3], last_got[1], small_kept, small_got),
        [(w.shape, f32) for w in (w_first, w_middle, w_last)],
        [],
        1_000_000,
    )
    if fold > 1:
        out_first, out_middle, out_last = (
            lax.psum_scatter(
                out, "cols", scatter_dimension=0, axis_index_groups=neighbours(fold), tiled=True
            )
            for out in (out_first, out_middle, out_last)
        )
    return (out_first, out_middle, out_last)


def solution(mesh):
    placed = (
        P("groups", "cols"),
        P("groups", "cols", None),
        P("cols", None),
        P("cols", None),
        P("cols", None),
    )
    return jax.shard_map(
        on_device,
        mesh=mesh,
        in_specs=placed,
        out_specs=(
            P(("groups", "cols"), None),
            P(("groups", "cols"), None),
            P(("groups", "cols"), None),
        ),
        check_vma=False,
    )
```

```python
import functools

import jax
import jax.numpy as jnp
from jax import lax
from jax.experimental import pallas as pl
from jax.experimental.pallas import tpu as pltpu
from jax.sharding import PartitionSpec as P

epsilon = 1e-06
bf16, f32 = jnp.bfloat16, jnp.float32
MIB = 1024 * 1024
HALO_X, HALO_FIRST, HALO_SECOND, HALO_SLOPE, HALO_BACK = 13, 12, 10, 6, 2
BLOCKS, FAR = 16, 4
LANES = 128
STACK_COST = 3_000_000_000
EARLY_COST = 1_500_000_000
HALF_COST = 1_500_000_000


def swap(array, mask):
    size = lax.axis_size("cols")
    return lax.ppermute(array, "cols", [(i, i ^ mask) for i in range(size)])


def bands_beside(low_pairs, high_pairs):
    size = lax.axis_size("cols")
    bands = size // 4

    def other(i):
        band = i // 4 + (1 if i // 4 % 2 else -1)
        return i ^ 1 if band < 0 or band >= bands else 4 * band + i % 4

    return swap(low_pairs, 4), lax.ppermute(high_pairs, "cols", [(i, other(i)) for i in range(size)])


def neighbours(fold):
    size = lax.axis_size("cols")
    return [list(range(i, i + fold)) for i in range(0, size, fold)]


def position(blocks):
    me = lax.axis_index("cols")
    return me // 4, me % 4, me // (lax.axis_size("cols") // blocks)


def dot(a, b, contract):
    return lax.dot_general(a, b, (contract, ((), ())), preferred_element_type=f32)


def iota(shape, axis):
    return lax.broadcasted_iota(jnp.int32, shape, axis)


def row_shifted(value, step, rows):
    count = value.shape[0]
    if step == 0:
        return value
    row = iota((count, 1), 0) % rows + step
    rolled = pltpu.roll(value, (-step) % count, 0)
    return jnp.where((row >= 0) & (row < rows), rolled, 0.0)


def inside(count, rows, first, total):
    col = iota((count, 1), 0) // rows + first
    return (col >= 0) & (col < total)


def put_patch(patch_ref, value, step, rows, out_cols):
    depth = value.shape[1]
    for ky in range(3):
        moved = row_shifted(value, (ky - 1) * step, rows).astype(bf16)
        for kx in range(3):
            tap = 3 * ky + kx
            start = kx * step * rows
            patch_ref[:, tap * depth : (tap + 1) * depth] = moved[start : start + out_cols * rows]


def spread_back(parts_ref, step, rows, out_cols):
    depth = parts_ref.shape[1] // 9
    total = None
    for ky in range(3):
        line = None
        for kx in range(3):
            tap = 3 * ky + kx
            start = (2 - kx) * step * rows
            piece = parts_ref[start : start + out_cols * rows, tap * depth : (tap + 1) * depth]
            line = piece if line is None else line + piece
        line = row_shifted(line, (1 - ky) * step, rows)
        total = line if total is None else total + line
    return total


def deal_kernel(
    x_hbm,
    teacher_hbm,
    w_first_hbm,
    w_middle_hbm,
    w_last_hbm,
    own_ref,
    near_ref,
    across_ref,
    shard_ref,
    x_ref,
    teacher_ref,
    w_first_ref,
    w_middle_ref,
    w_last_ref,
    pick_x_ref,
    pick_t_ref,
    arrived,
):
    copies = [
        pltpu.make_async_copy(source, target, arrived.at[i])
        for i, (source, target) in enumerate(
            (
                (teacher_hbm, teacher_ref),
                (x_hbm, x_ref),
                (w_last_hbm, w_last_ref),
                (w_middle_hbm, w_middle_ref),
                (w_first_hbm, w_first_ref),
            )
        )
    ]
    for copy in copies:
        copy.start()
    height, breadth, channels = teacher_ref.shape
    depth = x_ref.shape[1] // breadth
    rows, piece = height // 2, breadth // 2
    cells = rows * piece
    low = position(BLOCKS)[1]
    core, row = low % 2, low // 2
    out = iota((cells, 1), 0)
    col, line = out // rows, out % rows
    for rc in range(2):
        line_of = 2 * line + (core ^ rc)
        pick_x_ref[rc] = (iota((cells, piece * height), 1) == col * height + line_of).astype(f32).astype(bf16)
        for ry in range(2):
            source = line_of * breadth + 2 * col + (row ^ ry)
            pick_t_ref[rc, ry] = (iota((cells, height * breadth), 1) == source).astype(f32).astype(bf16)
    for copy in copies:
        copy.wait()
    at = put_tiles(shard_ref, 0, w_last_ref[...])
    at = put_tiles(shard_ref, at, w_middle_ref[...])
    put_tiles(shard_ref, at, w_first_ref[...])
    own_ref[: shard_ref.shape[0]] = shard_ref[...]
    field = teacher_ref[...].reshape(height * breadth, channels)
    pairs = jnp.concatenate(
        [x_ref[:, 2 * depth * i : 2 * depth * (i + 1)] for i in range(piece)], 0
    )
    x_parts = []
    for rc, out_ref in ((0, own_ref), (1, near_ref)):
        both = dot(pick_x_ref[rc], pairs, ((1,), (0,))).astype(bf16)
        low, high = both[:, :depth], both[:, depth:]
        x_parts.append(jnp.where(row == 0, high, low))
        across = dot(pick_t_ref[rc, 1], field, ((1,), (0,))).astype(bf16)
        put_tiles(across_ref, rc * cells * len(tiles(channels)), across)
        value = dot(pick_t_ref[rc, 0], field, ((1,), (0,))).astype(bf16)
        at = put_tiles(out_ref, out_ref.shape[0] - near_ref.shape[0], value)
        x = jnp.where(row == 0, low, high)
        out_ref[at:, :] = jnp.concatenate([x, jnp.zeros_like(x)], 1)
    across_ref[across_ref.shape[0] - cells :, :] = jnp.concatenate(x_parts, 1)


def tiles(width):
    return [(start, min(LANES, width - start)) for start in range(0, width, LANES)]


def put_tiles(ref, at, value):
    rows, width = value.shape
    for start, size in tiles(width):
        ref[at : at + rows, :size] = value[:, start : start + size]
        at += rows
    return at


def take_tiles(value, at, rows, width):
    return jnp.concatenate(
        [
            value[at + i * rows : at + (i + 1) * rows, :size]
            for i, (_, size) in enumerate(tiles(width))
        ],
        1,
    )


def hold_kernel(own_ref, far_ref, held_ref, same_ref):
    held_ref[...] = own_ref[...]


def stack_kernel(own_ref, far3_ref, far1_ref, far2_ref, last_ref, small_ref):
    cut, end = last_ref.shape[1], last_ref.shape[1] + small_ref.shape[1]
    for far, ref in enumerate((own_ref, far1_ref, far2_ref, far3_ref)):
        last_ref[far] = ref[:cut]
        small_ref[far] = ref[cut:end]


def after_kernel(value_ref, first_ref, same_ref):
    pass


def collect_kernel(
    cells,
    edge_t,
    edge_x,
    own_ref,
    near_ref,
    across_ref,
    diagonal_ref,
    x_ref,
    teacher_ref,
    edge_a_ref,
    edge_b_ref,
):
    depth, channels = x_ref.shape[1], teacher_ref.shape[1]
    low = position(BLOCKS)[1]
    part = cells * len(tiles(channels))
    skip = own_ref.shape[0] - near_ref.shape[0]
    pieces = ((own_ref, skip, 0), (near_ref, 0, 0), (across_ref, 0, 0), (diagonal_ref, part, depth))
    for k, (ref, row, lane) in enumerate(pieces):
        at = pl.ds(pl.multiple_of((low ^ k) * cells, cells), cells)
        x_ref[at, :] = ref[ref.shape[0] - cells :, lane : lane + depth]
        for lanes, size in tiles(channels):
            teacher_ref[at, lanes : lanes + size] = ref[row : row + cells, :]
            row += cells
    own = teacher_ref.shape[0]
    half = edge_x - edge_t
    odd = position(BLOCKS)[0] % 2
    for ref, high in ((edge_a_ref, 1 - odd), (edge_b_ref, odd)):
        at = pl.ds(pl.multiple_of(high * (own - edge_t), 16), edge_t)
        row = put_tiles(ref, 0, teacher_ref[at, :])
        at = high * (own - edge_x)
        ref[row:, :] = jnp.concatenate(
            [
                x_ref[pl.ds(pl.multiple_of(at, 16), half), :],
                x_ref[pl.ds(pl.multiple_of(at + edge_t, 16), half), :],
            ],
            1,
        )


def sides(edge_a_ref, edge_b_ref):
    a, b = edge_a_ref[...], edge_b_ref[...]
    group, bands = position(BLOCKS)[0], lax.axis_size("cols") // 4
    odd = group % 2 == 1
    before, after = jnp.where(odd, a, b), jnp.where(odd, b, a)
    zero = jnp.zeros_like(a)
    return jnp.where(group == 0, zero, before), jnp.where(group == bands - 1, zero, after)


def edge_x_cells(edge, edge_t, channels):
    packed = edge[edge_t * len(tiles(channels)) :, :]
    depth = LANES // 2
    overlap = packed.shape[0] - edge_t
    return jnp.concatenate([packed[:, :depth], packed[overlap:, depth:]], 0)


def early_kernel(
    own,
    rows,
    total,
    channels,
    edge_t,
    x_ref,
    edge_b_ref,
    edge_a_ref,
    h_ref,
    hy_ref,
    hc_ref,
    hyc_ref,
    tilt_first_ref,
    tilt_second_ref,
    patch_first_ref,
    patch_middle_ref,
    patch_last_ref,
    w_middle_ref,
    small_ref,
):
    group, _, place = position(BLOCKS)
    first_col = group * own
    r_small = small_ref.shape[1] // 2
    in_taps, taps = patch_first_ref.shape[1], patch_middle_ref.shape[1]
    for near, ref in enumerate((h_ref, hc_ref, hy_ref, hyc_ref)):
        for far in range(FAR):
            at = place ^ (4 * far + near)
            small = ref[far].astype(f32)
            row = 0
            for first, width in ((0, taps), (r_small, in_taps)):
                for start, size in tiles(width):
                    small_ref[at, first : first + r_small, start : start + size] = small[
                        row : row + r_small, :size
                    ]
                    row += r_small
    small = small_ref[...]
    w_middle_ref[...] = small[:, :r_small].reshape(-1, taps).astype(bf16)
    w_first = small[:, r_small:, :in_taps].reshape(-1, in_taps).astype(bf16)

    n_first, n_second, n_slope = (
        own + 2 * HALO_FIRST,
        own + 2 * HALO_SECOND,
        own + 2 * HALO_SLOPE,
    )
    before, after = sides(edge_a_ref, edge_b_ref)
    wide = jnp.concatenate(
        [
            edge_x_cells(before, edge_t, channels),
            x_ref[...],
            edge_x_cells(after, edge_t, channels),
        ],
        0,
    )
    put_patch(patch_first_ref, wide.astype(f32), 1, rows, n_first)
    pre = dot(patch_first_ref[...], w_first, ((1,), (1,)))
    sigma = 1.0 / (1.0 + jnp.exp(-pre))
    act = jnp.where(
        inside(n_first * rows, rows, first_col - HALO_FIRST, total), pre * sigma, 0.0
    )
    lo = HALO_FIRST * rows
    pre_own, sigma_own = pre[lo : lo + own * rows], sigma[lo : lo + own * rows]
    tilt_first_ref[...] = sigma_own * (1.0 + pre_own * (1.0 - sigma_own))
    put_patch(patch_middle_ref, act, 2, rows, n_second)

    pre = dot(patch_middle_ref[...], w_middle_ref[...], ((1,), (1,)))
    sigma = 1.0 / (1.0 + jnp.exp(-pre))
    act = jnp.where(
        inside(n_second * rows, rows, first_col - HALO_SECOND, total), pre * sigma, 0.0
    )
    lo, n_back = (HALO_SECOND - HALO_BACK) * rows, (own + 2 * HALO_BACK) * rows
    pre_back, sigma_back = pre[lo : lo + n_back], sigma[lo : lo + n_back]
    tilt_second_ref[...] = jnp.where(
        inside(n_back, rows, first_col - HALO_BACK, total),
        sigma_back * (1.0 + pre_back * (1.0 - sigma_back)),
        0.0,
    )
    put_patch(patch_last_ref, act, 4, rows, n_slope)


def put_blocks(w_ref, blocks, r_last):
    taps = w_ref.shape[1]
    for i, (ref, far) in enumerate(blocks):
        for j, (start, size) in enumerate(tiles(taps)):
            w_ref[i * r_last : (i + 1) * r_last, start : start + size] = ref[
                far, j * r_last : (j + 1) * r_last
            ]


def half_kernel(
    rows,
    edge_t,
    teacher_ref,
    edge_a_ref,
    edge_b_ref,
    patch_last_ref,
    h_ref,
    hy_ref,
    w_own_ref,
    student_ref,
    target_ref,
):
    place = position(BLOCKS)[2]
    channels = teacher_ref.shape[1]
    r_last = channels // BLOCKS
    put_blocks(w_own_ref, [(ref, far) for ref in (h_ref, hy_ref) for far in range(FAR)], r_last)
    student_ref[...] = dot(patch_last_ref[...], w_own_ref[...], ((1,), (1,)))
    before, after = sides(edge_a_ref, edge_b_ref)
    wide = jnp.concatenate(
        [
            take_tiles(before, 0, edge_t, channels),
            teacher_ref[...],
            take_tiles(after, 0, edge_t, channels),
        ],
        0,
    )
    out = iota((1, channels), 1)
    block = out // r_last
    key = 4 * (block % FAR) + 2 * (block // FAR % 2) + block // (2 * FAR)
    source = (key ^ place) * r_last + out % r_last
    pick = (iota((channels, channels), 0) == source).astype(f32).astype(bf16)
    target_ref[...] = dot(wide, pick, ((1,), (0,))).astype(bf16)


def front_kernel(
    own,
    rows,
    total,
    target_ref,
    patch_last_ref,
    student_own_ref,
    hc_ref,
    hyc_ref,
    send_ref,
    send_y_ref,
    slope_ref,
    w_other_ref,
    student_ref,
):
    first_col = position(BLOCKS)[0] * own
    channels = slope_ref.shape[1]
    half = channels // 2
    put_blocks(
        w_other_ref, [(ref, far) for ref in (hc_ref, hyc_ref) for far in range(FAR)], channels // BLOCKS
    )
    student_ref[...] = dot(patch_last_ref[...], w_other_ref[...], ((1,), (1,)))
    block = 4 * rows
    for step in range(slope_ref.shape[0] // block):
        at = pl.ds(step * block, block)
        parts = [
            (student, target_ref[at, lane : lane + half].astype(f32), lane)
            for student, lane in ((student_own_ref[at, :], 0), (student_ref[at, :], half))
        ]

        def total_of(product):
            return sum(jnp.sum(product(s, t), -1, keepdims=True) for s, t, _ in parts)

        s_inv = lax.rsqrt(total_of(lambda s, t: s * s) + epsilon)
        t_inv = lax.rsqrt(total_of(lambda s, t: t * t) + epsilon)
        cosine = total_of(lambda s, t: s * t) * (s_inv * t_inv)
        ok = inside(block, rows, first_col - HALO_SLOPE + step * (block // rows), total)
        s_part = jnp.where(ok, s_inv * s_inv * (cosine + epsilon * (s_inv * s_inv)), 0.0)
        t_part = jnp.where(ok, s_inv * t_inv, 0.0)
        for student, target, lane in parts:
            slope_ref[at, lane : lane + half] = (student * s_part - target * t_part).astype(bf16)

    lo, n_own = HALO_SLOPE * rows, own * rows
    terms = dot(
        slope_ref[lo : lo + n_own, half:], patch_last_ref[lo : lo + n_own, :], ((0,), (0,))
    )
    terms = terms.astype(bf16).reshape((2,) + send_ref.shape)
    send_ref[...] = terms[0]
    send_y_ref[...] = terms[1]


def back_kernel(
    own,
    rows,
    slope_ref,
    tilt_second_ref,
    w_own_ref,
    w_other_ref,
    patch_last_ref,
    keep_ref,
    keep_y_ref,
    slope_second_ref,
    parts_ref,
):
    half = w_own_ref.shape[0]
    lo, n_own = HALO_SLOPE * rows, own * rows
    terms = dot(
        slope_ref[lo : lo + n_own, :half], patch_last_ref[lo : lo + n_own, :], ((0,), (0,))
    )
    terms = terms.reshape((2,) + keep_ref.shape)
    keep_ref[...] = terms[0]
    keep_y_ref[...] = terms[1]
    parts_ref[...] = dot(slope_ref[:, :half], w_own_ref[...], ((1,), (0,))) + dot(
        slope_ref[:, half:], w_other_ref[...], ((1,), (0,))
    )
    back_second = spread_back(parts_ref, 4, rows, own + 2 * HALO_BACK)
    slope_second_ref[...] = (back_second * tilt_second_ref[...]).astype(bf16)


def first_kernel(
    own,
    rows,
    slope_second_ref,
    tilt_first_ref,
    patch_first_ref,
    patch_middle_ref,
    w_middle_ref,
    keep_ref,
    send_ref,
    parts_ref,
    terms_ref,
):
    place = position(BLOCKS)[2]
    n_own = own * rows
    slope_second = slope_second_ref[...]
    lo, hi = HALO_BACK * rows, HALO_SECOND * rows
    r_small, middle = terms_ref.shape[1], patch_middle_ref.shape[1]
    grad_middle = dot(
        slope_second[lo : lo + n_own], patch_middle_ref[hi : hi + n_own, :], ((0,), (0,))
    )
    terms_ref[:, :, :middle] = grad_middle.reshape(-1, r_small, middle)
    parts_ref[...] = dot(slope_second, w_middle_ref[...], ((1,), (0,)))
    back_first = spread_back(parts_ref, 2, rows, own)
    slope_first = (back_first * tilt_first_ref[...]).astype(bf16)
    hi = HALO_FIRST * rows
    grad_first = dot(slope_first, patch_first_ref[hi : hi + n_own, :], ((0,), (0,)))
    terms_ref[:, :, middle:] = grad_first.reshape(-1, r_small, grad_first.shape[1])
    for ry in range(2):
        for far in range(FAR):
            at = place ^ (4 * far + 2 * ry)
            keep_ref[far, ry] = terms_ref[at]
            send_ref[far, ry] = terms_ref[at ^ 1].astype(bf16)


def join_kernel(keep_ref, got_ref, sent_ref):
    sent_ref[...] = (keep_ref[...] + got_ref[...].astype(f32)).astype(sent_ref.dtype)


def split_kernel(keep_ref, *refs):
    got_refs, out_refs = refs[:-FAR], refs[-FAR:]
    for i, ref in enumerate(out_refs):
        total = keep_ref[i]
        for got_ref in got_refs:
            total = total + got_ref[i].astype(f32)
        ref[...] = total.astype(ref.dtype)


def add_kernel(keep_ref, got1_ref, got2_ref, got3_ref, kept_ref, send_ref):
    total = keep_ref[...]
    for ref in (got1_ref, got2_ref, got3_ref):
        total = total + ref[...].astype(f32)
    kept_ref[...] = total[0]
    send_ref[...] = total[1].astype(bf16)


def finish_kernel(
    last_ref, got1_ref, got2_ref, got3_ref, small_ref, got_ref, first_ref, middle_ref, out_ref
):
    total = last_ref[...]
    for ref in (got1_ref, got2_ref, got3_ref):
        total = total + ref[...].astype(f32)
    out_ref[...] = total
    small = small_ref[...] + got_ref[...].astype(f32)
    middle_ref[...] = small[:, : middle_ref.shape[1]]
    first_ref[...] = small[:, middle_ref.shape[1] :]


def call(kernel, name, inputs, outs, scratch, flops, spaces=None, semaphores=(), vmem_mib=24, out_spaces=None, aliases=None):
    vmem = pl.BlockSpec(memory_space=pltpu.VMEM)
    spaces = spaces or {}
    return pl.pallas_call(
        kernel,
        in_specs=[spaces.get(i, vmem) for i in range(len(inputs))],
        out_specs=[(out_spaces or {}).get(i, vmem) for i in range(len(outs))],
        input_output_aliases=aliases or {},
        out_shape=[jax.ShapeDtypeStruct(shape, kind) for shape, kind in outs],
        scratch_shapes=[pltpu.VMEM(shape, kind) for shape, kind in scratch] + list(semaphores),
        compiler_params=pltpu.CompilerParams(vmem_limit_bytes=int(vmem_mib * MIB)),
        cost_estimate=pl.CostEstimate(flops=flops, bytes_accessed=1_000_000, transcendentals=0),
        name=name,
    )(*inputs)


def on_device(image_feats, teacher, w_first, w_middle, w_last):
    size = lax.axis_size("cols")
    fold = size // BLOCKS
    height, breadth, channels = teacher.shape
    in_depth = w_first.shape[1] // 9
    hidden = w_middle.shape[1] // 9
    rows, piece = height // 2, breadth // 2
    own = 4 * piece
    total = own * (size // 4)

    if fold > 1:
        w_first, w_middle, w_last = (
            lax.all_gather(w, "cols", axis_index_groups=neighbours(fold), axis=0, tiled=True)
            for w in (w_first, w_middle, w_last)
        )
    r_last, r_small = w_last.shape[0], w_first.shape[0]
    cells = piece * rows
    dealt = cells * len(tiles(channels)) + cells
    packed = r_last * len(tiles(9 * hidden))
    packed += r_small * (len(tiles(9 * hidden)) + len(tiles(9 * in_depth)))
    hbm = pl.BlockSpec(memory_space=pltpu.HBM)
    own_class, near, across, shard = call(
        deal_kernel,
        "deal",
        (image_feats, teacher, w_first, w_middle, w_last),
        [
            ((packed + dealt, LANES), bf16),
            ((dealt, LANES), bf16),
            ((2 * dealt - cells, LANES), bf16),
            ((packed, LANES), bf16),
        ],
        [(a.shape, a.dtype) for a in (image_feats, teacher, w_first, w_middle, w_last)]
        + [((2, cells, piece * height), bf16), ((2, 2, cells, height * breadth), bf16)],
        600_000_000,
        {i: hbm for i in range(5)},
        [pltpu.SemaphoreType.DMA((5,))],
        60,
    )
    across = swap(across, 2)
    far = {k: swap(shard, 4 * k * fold) for k in (1, 2, 3)}
    near = swap(near, 1)
    anywhere = pl.BlockSpec(memory_space=pl.ANY)

    def behind(value, first):
        return call(
            after_kernel,
            "after",
            (value, first),
            [(value.shape, value.dtype)],
            [],
            1_000_000,
            {0: anywhere, 1: anywhere},
            out_spaces={0: anywhere},
            aliases={0: 0},
        )[0]

    diagonal = swap(across, 1)
    held, far[1] = call(
        hold_kernel,
        "hold",
        (own_class, far[1]),
        [(own_class.shape, bf16), (shard.shape, bf16)],
        [],
        1_000_000,
        {1: anywhere},
        out_spaces={1: anywhere},
        aliases={1: 1},
    )
    edge_t, edge_x = HALO_SLOPE * rows, HALO_X * rows
    edge = edge_t * len(tiles(channels)) + edge_x - edge_t
    part_last = r_last * len(tiles(9 * hidden))
    held_last, held_small = call(
        stack_kernel,
        "stack",
        (held, far[3], far[1], far[2]),
        [((FAR, part_last, LANES), bf16), ((FAR, packed - part_last, LANES), bf16)],
        [],
        STACK_COST,
    )
    x_band, t_band, edge_a, edge_b = call(
        functools.partial(collect_kernel, cells, edge_t, edge_x),
        "collect",
        (held, near, across, diagonal),
        [
            ((own * rows, in_depth), bf16),
            ((own * rows, channels), bf16),
            ((edge, LANES), bf16),
            ((edge, LANES), bf16),
        ],
        [],
        1_000_000,
    )

    small_y = swap(held_small, 2 * fold)
    last_y = swap(held_last, 2 * fold)
    all_small = held_small, small_y, swap(held_small, fold), swap(small_y, fold)
    edge_a, edge_b = bands_beside(edge_a, edge_b)

    n_first, n_second, n_slope, n_back = (
        (own + 2 * halo) * rows for halo in (HALO_FIRST, HALO_SECOND, HALO_SLOPE, HALO_BACK)
    )
    tilt_first, tilt_second, patch_first, patch_middle, patch_last, all_middle = call(
        functools.partial(early_kernel, own, rows, total, channels, edge_t),
        "early",
        (x_band, edge_b, edge_a, *all_small),
        [
            ((own * rows, hidden), f32),
            ((n_back, hidden), f32),
            ((n_first, 9 * in_depth), bf16),
            ((n_second, 9 * hidden), bf16),
            ((n_slope, 9 * hidden), bf16),
            ((hidden, 9 * hidden), bf16),
        ],
        [((BLOCKS, 2 * r_small, 9 * hidden), f32)],
        EARLY_COST,
    )
    last_y = behind(last_y, patch_last)
    half = channels // 2
    last_c, last_yc = swap(held_last, fold), swap(last_y, fold)
    w_own, student_own, target = call(
        functools.partial(half_kernel, rows, edge_t),
        "half",
        (t_band, edge_a, edge_b, patch_last, held_last, last_y),
        [
            ((half, 9 * hidden), bf16),
            ((n_slope, half), f32),
            ((n_slope, channels), bf16),
        ],
        [],
        HALF_COST,
    )
    send, send_y, slope, w_other = call(
        functools.partial(front_kernel, own, rows, total),
        "front",
        (target, patch_last, student_own, last_c, last_yc),
        [
            ((FAR, r_last, 9 * hidden), bf16),
            ((FAR, r_last, 9 * hidden), bf16),
            ((n_slope, channels), bf16),
            ((half, 9 * hidden), bf16),
        ],
        [((n_slope, half), f32)],
        6_000_000_000,
    )
    got_y, got = swap(send_y, fold), swap(send, fold)
    keep, keep_y, slope_second = call(
        functools.partial(back_kernel, own, rows),
        "back",
        (slope, tilt_second, w_own, w_other, patch_last),
        [((FAR, r_last, 9 * hidden), f32)] * 2 + [((n_back, hidden), bf16)],
        [((n_slope, 9 * hidden), f32)],
        4_000_000_000,
    )
    both = 9 * (hidden + in_depth)
    small_keep, small_send = call(
        functools.partial(first_kernel, own, rows),
        "first",
        (slope_second, tilt_first, patch_first, patch_middle, all_middle),
        [((FAR, 2, r_small, both), f32), ((FAR, 2, r_small, both), bf16)],
        [((n_back, 9 * hidden), f32), ((BLOCKS, r_small, both), f32)],
        2_000_000_000,
    )

    def split(keep, *got):
        shape = keep.shape[1:]
        outs = [(shape, f32)] + [(shape, bf16)] * (FAR - 1)
        return call(split_kernel, "split", (keep, *got), outs, [], 1_000_000)

    (last_sent,) = call(join_kernel, "join", (keep_y, got_y), [(keep.shape, bf16)], [], 1_000_000)
    last_got = swap(last_sent, 2 * fold)
    parts = split(small_keep, swap(small_send, fold))
    small_got = {k: swap(parts[k], 4 * k * fold) for k in (1, 2, 3)}
    last = split(keep, got, last_got)
    last_got = {k: swap(last[k], 4 * k * fold) for k in (1, 2, 3)}
    small_kept, small_sent = call(
        add_kernel,
        "add",
        (parts[0], small_got[3], small_got[2], small_got[1]),
        [((r_small, both), f32), ((r_small, both), bf16)],
        [],
        1_000_000,
    )
    small_got = swap(small_sent, 2 * fold)
    out_first, out_middle, out_last = call(
        finish_kernel,
        "finish",
        (last[0], last_got[2], last_got[1], last_got[3], small_kept, small_got),
        [(w.shape, f32) for w in (w_first, w_middle, w_last)],
        [],
        1_000_000,
    )
    if fold > 1:
        out_first, out_middle, out_last = (
            lax.psum_scatter(
                out, "cols", scatter_dimension=0, axis_index_groups=neighbours(fold), tiled=True
            )
            for out in (out_first, out_middle, out_last)
        )
    return (out_first, out_middle, out_last)


def solution(mesh):
    placed = (
        P("groups", "cols"),
        P("groups", "cols", None),
        P("cols", None),
        P("cols", None),
        P("cols", None),
    )
    return jax.shard_map(
        on_device,
        mesh=mesh,
        in_specs=placed,
        out_specs=(
            P(("groups", "cols"), None),
            P(("groups", "cols"), None),
            P(("groups", "cols"), None),
        ),
        check_vma=False,
    )
```

```python
import functools

import jax
import jax.numpy as jnp
from jax import lax
from jax.experimental import pallas as pl
from jax.experimental.pallas import tpu as pltpu
from jax.sharding import PartitionSpec as P

epsilon = 1e-06
bf16, f32 = jnp.bfloat16, jnp.float32
MIB = 1024 * 1024
HALO_X, HALO_FIRST, HALO_SECOND, HALO_SLOPE, HALO_BACK = 13, 12, 10, 6, 2
BLOCKS, FAR = 16, 4
LANES = 128
STACK_COST = 3_000_000_000
EARLY_COST = 1_500_000_000
HALF_COST = 1_500_000_000


def swap(array, mask):
    size = lax.axis_size("cols")
    return lax.ppermute(array, "cols", [(i, i ^ mask) for i in range(size)])


def bands_beside(low_pairs, high_pairs):
    size = lax.axis_size("cols")
    bands = size // 4

    def other(i):
        band = i // 4 + (1 if i // 4 % 2 else -1)
        return i ^ 1 if band < 0 or band >= bands else 4 * band + i % 4

    return swap(low_pairs, 4), lax.ppermute(high_pairs, "cols", [(i, other(i)) for i in range(size)])


def neighbours(fold):
    size = lax.axis_size("cols")
    return [list(range(i, i + fold)) for i in range(0, size, fold)]


def position(blocks):
    me = lax.axis_index("cols")
    return me // 4, me % 4, me // (lax.axis_size("cols") // blocks)


def dot(a, b, contract):
    return lax.dot_general(a, b, (contract, ((), ())), preferred_element_type=f32)


def iota(shape, axis):
    return lax.broadcasted_iota(jnp.int32, shape, axis)


def row_shifted(value, step, rows):
    count = value.shape[0]
    if step == 0:
        return value
    row = iota((count, 1), 0) % rows + step
    rolled = pltpu.roll(value, (-step) % count, 0)
    return jnp.where((row >= 0) & (row < rows), rolled, 0.0)


def inside(count, rows, first, total):
    col = iota((count, 1), 0) // rows + first
    return (col >= 0) & (col < total)


def put_patch(patch_ref, value, step, rows, out_cols):
    depth = value.shape[1]
    for ky in range(3):
        moved = row_shifted(value, (ky - 1) * step, rows).astype(bf16)
        for kx in range(3):
            tap = 3 * ky + kx
            start = kx * step * rows
            patch_ref[:, tap * depth : (tap + 1) * depth] = moved[start : start + out_cols * rows]


def spread_back(parts_ref, step, rows, out_cols):
    depth = parts_ref.shape[1] // 9
    total = None
    for ky in range(3):
        line = None
        for kx in range(3):
            tap = 3 * ky + kx
            start = (2 - kx) * step * rows
            piece = parts_ref[start : start + out_cols * rows, tap * depth : (tap + 1) * depth]
            line = piece if line is None else line + piece
        line = row_shifted(line, (1 - ky) * step, rows)
        total = line if total is None else total + line
    return total


def deal_kernel(
    x_hbm,
    teacher_hbm,
    w_first_hbm,
    w_middle_hbm,
    w_last_hbm,
    own_ref,
    near_ref,
    across_ref,
    shard_ref,
    x_ref,
    teacher_ref,
    w_first_ref,
    w_middle_ref,
    w_last_ref,
    pick_x_ref,
    pick_t_ref,
    arrived,
):
    copies = [
        pltpu.make_async_copy(source, target, arrived.at[i])
        for i, (source, target) in enumerate(
            (
                (teacher_hbm, teacher_ref),
                (x_hbm, x_ref),
                (w_last_hbm, w_last_ref),
                (w_middle_hbm, w_middle_ref),
                (w_first_hbm, w_first_ref),
            )
        )
    ]
    for copy in copies:
        copy.start()
    height, breadth, channels = teacher_ref.shape
    depth = x_ref.shape[1] // breadth
    rows, piece = height // 2, breadth // 2
    cells = rows * piece
    low = position(BLOCKS)[1]
    core, row = low % 2, low // 2
    out = iota((cells, 1), 0)
    col, line = out // rows, out % rows
    for rc in range(2):
        line_of = 2 * line + (core ^ rc)
        pick_x_ref[rc] = (iota((cells, piece * height), 1) == col * height + line_of).astype(f32).astype(bf16)
        for ry in range(2):
            source = line_of * breadth + 2 * col + (row ^ ry)
            pick_t_ref[rc, ry] = (iota((cells, height * breadth), 1) == source).astype(f32).astype(bf16)
    for copy in copies:
        copy.wait()
    at = put_tiles(shard_ref, 0, w_last_ref[...])
    at = put_tiles(shard_ref, at, w_middle_ref[...])
    put_tiles(shard_ref, at, w_first_ref[...])
    own_ref[: shard_ref.shape[0]] = shard_ref[...]
    field = teacher_ref[...].reshape(height * breadth, channels)
    pairs = jnp.concatenate(
        [x_ref[:, 2 * depth * i : 2 * depth * (i + 1)] for i in range(piece)], 0
    )
    x_parts = []
    for rc, out_ref in ((0, own_ref), (1, near_ref)):
        both = dot(pick_x_ref[rc], pairs, ((1,), (0,))).astype(bf16)
        low, high = both[:, :depth], both[:, depth:]
        x_parts.append(jnp.where(row == 0, high, low))
        across = dot(pick_t_ref[rc, 1], field, ((1,), (0,))).astype(bf16)
        put_tiles(across_ref, rc * cells * len(tiles(channels)), across)
        value = dot(pick_t_ref[rc, 0], field, ((1,), (0,))).astype(bf16)
        at = put_tiles(out_ref, out_ref.shape[0] - near_ref.shape[0], value)
        x = jnp.where(row == 0, low, high)
        out_ref[at:, :] = jnp.concatenate([x, jnp.zeros_like(x)], 1)
    across_ref[across_ref.shape[0] - cells :, :] = jnp.concatenate(x_parts, 1)


def tiles(width):
    return [(start, min(LANES, width - start)) for start in range(0, width, LANES)]


def put_tiles(ref, at, value):
    rows, width = value.shape
    for start, size in tiles(width):
        ref[at : at + rows, :size] = value[:, start : start + size]
        at += rows
    return at


def take_tiles(value, at, rows, width):
    return jnp.concatenate(
        [
            value[at + i * rows : at + (i + 1) * rows, :size]
            for i, (_, size) in enumerate(tiles(width))
        ],
        1,
    )


def hold_kernel(own_ref, far_ref, held_ref, same_ref):
    held_ref[...] = own_ref[...]


def stack_kernel(own_ref, far3_ref, far1_ref, far2_ref, last_ref, small_ref):
    cut, end = last_ref.shape[1], last_ref.shape[1] + small_ref.shape[1]
    for far, ref in enumerate((own_ref, far1_ref, far2_ref, far3_ref)):
        last_ref[far] = ref[:cut]
        small_ref[far] = ref[cut:end]


def after_kernel(value_ref, first_ref, same_ref):
    pass


def collect_kernel(
    cells,
    edge_t,
    edge_x,
    own_ref,
    near_ref,
    across_ref,
    diagonal_ref,
    x_ref,
    teacher_ref,
    edge_a_ref,
    edge_b_ref,
):
    depth, channels = x_ref.shape[1], teacher_ref.shape[1]
    low = position(BLOCKS)[1]
    part = cells * len(tiles(channels))
    skip = own_ref.shape[0] - near_ref.shape[0]
    pieces = ((own_ref, skip, 0), (near_ref, 0, 0), (across_ref, 0, 0), (diagonal_ref, part, depth))
    for k, (ref, row, lane) in enumerate(pieces):
        at = pl.ds(pl.multiple_of((low ^ k) * cells, cells), cells)
        x_ref[at, :] = ref[ref.shape[0] - cells :, lane : lane + depth]
        for lanes, size in tiles(channels):
            teacher_ref[at, lanes : lanes + size] = ref[row : row + cells, :]
            row += cells
    own = teacher_ref.shape[0]
    half = edge_x - edge_t
    odd = position(BLOCKS)[0] % 2
    for ref, high in ((edge_a_ref, 1 - odd), (edge_b_ref, odd)):
        at = pl.ds(pl.multiple_of(high * (own - edge_t), 16), edge_t)
        row = put_tiles(ref, 0, teacher_ref[at, :])
        at = high * (own - edge_x)
        ref[row:, :] = jnp.concatenate(
            [
                x_ref[pl.ds(pl.multiple_of(at, 16), half), :],
                x_ref[pl.ds(pl.multiple_of(at + edge_t, 16), half), :],
            ],
            1,
        )


def sides(edge_a_ref, edge_b_ref):
    a, b = edge_a_ref[...], edge_b_ref[...]
    group, bands = position(BLOCKS)[0], lax.axis_size("cols") // 4
    odd = group % 2 == 1
    before, after = jnp.where(odd, a, b), jnp.where(odd, b, a)
    zero = jnp.zeros_like(a)
    return jnp.where(group == 0, zero, before), jnp.where(group == bands - 1, zero, after)


def edge_x_cells(edge, edge_t, channels):
    packed = edge[edge_t * len(tiles(channels)) :, :]
    depth = LANES // 2
    overlap = packed.shape[0] - edge_t
    return jnp.concatenate([packed[:, :depth], packed[overlap:, depth:]], 0)


def early_kernel(
    own,
    rows,
    total,
    channels,
    edge_t,
    x_ref,
    edge_b_ref,
    edge_a_ref,
    h_ref,
    hy_ref,
    hc_ref,
    hyc_ref,
    tilt_first_ref,
    tilt_second_ref,
    patch_first_ref,
    patch_middle_ref,
    patch_last_ref,
    w_middle_ref,
    small_ref,
):
    group, _, place = position(BLOCKS)
    first_col = group * own
    r_small = small_ref.shape[1] // 2
    in_taps, taps = patch_first_ref.shape[1], patch_middle_ref.shape[1]
    for near, ref in enumerate((h_ref, hc_ref, hy_ref, hyc_ref)):
        for far in range(FAR):
            at = place ^ (4 * far + near)
            small = ref[far].astype(f32)
            row = 0
            for first, width in ((0, taps), (r_small, in_taps)):
                for start, size in tiles(width):
                    small_ref[at, first : first + r_small, start : start + size] = small[
                        row : row + r_small, :size
                    ]
                    row += r_small
    small = small_ref[...]
    w_middle_ref[...] = small[:, :r_small].reshape(-1, taps).astype(bf16)
    w_first = small[:, r_small:, :in_taps].reshape(-1, in_taps).astype(bf16)

    n_first, n_second, n_slope = (
        own + 2 * HALO_FIRST,
        own + 2 * HALO_SECOND,
        own + 2 * HALO_SLOPE,
    )
    before, after = sides(edge_a_ref, edge_b_ref)
    wide = jnp.concatenate(
        [
            edge_x_cells(before, edge_t, channels),
            x_ref[...],
            edge_x_cells(after, edge_t, channels),
        ],
        0,
    )
    put_patch(patch_first_ref, wide.astype(f32), 1, rows, n_first)
    pre = dot(patch_first_ref[...], w_first, ((1,), (1,)))
    sigma = 1.0 / (1.0 + jnp.exp(-pre))
    act = jnp.where(
        inside(n_first * rows, rows, first_col - HALO_FIRST, total), pre * sigma, 0.0
    )
    lo = HALO_FIRST * rows
    pre_own, sigma_own = pre[lo : lo + own * rows], sigma[lo : lo + own * rows]
    tilt_first_ref[...] = sigma_own * (1.0 + pre_own * (1.0 - sigma_own))
    put_patch(patch_middle_ref, act, 2, rows, n_second)

    pre = dot(patch_middle_ref[...], w_middle_ref[...], ((1,), (1,)))
    sigma = 1.0 / (1.0 + jnp.exp(-pre))
    act = jnp.where(
        inside(n_second * rows, rows, first_col - HALO_SECOND, total), pre * sigma, 0.0
    )
    lo, n_back = (HALO_SECOND - HALO_BACK) * rows, (own + 2 * HALO_BACK) * rows
    pre_back, sigma_back = pre[lo : lo + n_back], sigma[lo : lo + n_back]
    tilt_second_ref[...] = jnp.where(
        inside(n_back, rows, first_col - HALO_BACK, total),
        sigma_back * (1.0 + pre_back * (1.0 - sigma_back)),
        0.0,
    )
    put_patch(patch_last_ref, act, 4, rows, n_slope)


def put_blocks(w_ref, blocks, r_last):
    taps = w_ref.shape[1]
    for i, (ref, far) in enumerate(blocks):
        for j, (start, size) in enumerate(tiles(taps)):
            w_ref[i * r_last : (i + 1) * r_last, start : start + size] = ref[
                far, j * r_last : (j + 1) * r_last
            ]


def half_kernel(
    rows,
    edge_t,
    teacher_ref,
    edge_a_ref,
    edge_b_ref,
    patch_last_ref,
    h_ref,
    hy_ref,
    w_own_ref,
    student_ref,
    target_ref,
):
    place = position(BLOCKS)[2]
    channels = teacher_ref.shape[1]
    r_last = channels // BLOCKS
    put_blocks(w_own_ref, [(ref, far) for ref in (h_ref, hy_ref) for far in range(FAR)], r_last)
    student_ref[...] = dot(patch_last_ref[...], w_own_ref[...], ((1,), (1,)))
    before, after = sides(edge_a_ref, edge_b_ref)
    wide = jnp.concatenate(
        [
            take_tiles(before, 0, edge_t, channels),
            teacher_ref[...],
            take_tiles(after, 0, edge_t, channels),
        ],
        0,
    )
    out = iota((1, channels), 1)
    block = out // r_last
    key = 4 * (block % FAR) + 2 * (block // FAR % 2) + block // (2 * FAR)
    source = (key ^ place) * r_last + out % r_last
    pick = (iota((channels, channels), 0) == source).astype(f32).astype(bf16)
    target_ref[...] = dot(wide, pick, ((1,), (0,))).astype(bf16)


def front_kernel(
    own,
    rows,
    total,
    target_ref,
    patch_last_ref,
    student_own_ref,
    hc_ref,
    hyc_ref,
    send_y_ref,
    slope_ref,
    w_other_ref,
    student_ref,
):
    first_col = position(BLOCKS)[0] * own
    channels = slope_ref.shape[1]
    half = channels // 2
    put_blocks(
        w_other_ref, [(ref, far) for ref in (hc_ref, hyc_ref) for far in range(FAR)], channels // BLOCKS
    )
    student_ref[...] = dot(patch_last_ref[...], w_other_ref[...], ((1,), (1,)))
    block = 4 * rows
    for step in range(slope_ref.shape[0] // block):
        at = pl.ds(step * block, block)
        parts = [
            (student, target_ref[at, lane : lane + half].astype(f32), lane)
            for student, lane in ((student_own_ref[at, :], 0), (student_ref[at, :], half))
        ]

        def total_of(product):
            return sum(jnp.sum(product(s, t), -1, keepdims=True) for s, t, _ in parts)

        s_inv = lax.rsqrt(total_of(lambda s, t: s * s) + epsilon)
        t_inv = lax.rsqrt(total_of(lambda s, t: t * t) + epsilon)
        cosine = total_of(lambda s, t: s * t) * (s_inv * t_inv)
        ok = inside(block, rows, first_col - HALO_SLOPE + step * (block // rows), total)
        s_part = jnp.where(ok, s_inv * s_inv * (cosine + epsilon * (s_inv * s_inv)), 0.0)
        t_part = jnp.where(ok, s_inv * t_inv, 0.0)
        for student, target, lane in parts:
            slope_ref[at, lane : lane + half] = (student * s_part - target * t_part).astype(bf16)

    lo, n_own = HALO_SLOPE * rows, own * rows
    first = half + half // 2
    terms = dot(
        slope_ref[lo : lo + n_own, first:], patch_last_ref[lo : lo + n_own, :], ((0,), (0,))
    )
    send_y_ref[...] = terms.astype(bf16).reshape(send_y_ref.shape)


def beside_kernel(own, rows, slope_ref, patch_last_ref, keep_y_ref):
    half, lo, n_own = slope_ref.shape[1] // 2, HALO_SLOPE * rows, own * rows
    terms = dot(
        slope_ref[lo : lo + n_own, half // 2 : half],
        patch_last_ref[lo : lo + n_own, :],
        ((0,), (0,)),
    )
    keep_y_ref[...] = terms.reshape(keep_y_ref.shape)


def stay_kernel(own, rows, slope_ref, patch_last_ref, keep_ref, send_ref):
    half, lo, n_own = slope_ref.shape[1] // 2, HALO_SLOPE * rows, own * rows
    stays = jnp.concatenate(
        [slope_ref[lo : lo + n_own, first : first + half // 2] for first in (0, half)], 1
    )
    terms = dot(stays, patch_last_ref[lo : lo + n_own, :], ((0,), (0,)))
    terms = terms.reshape((2,) + keep_ref.shape)
    keep_ref[...] = terms[0]
    send_ref[...] = terms[1].astype(bf16)


def back_kernel(
    own,
    rows,
    slope_ref,
    tilt_second_ref,
    w_own_ref,
    w_other_ref,
    tie_ref,
    slope_second_ref,
    parts_ref,
):
    half = w_own_ref.shape[0]
    parts_ref[...] = dot(slope_ref[:, :half], w_own_ref[...], ((1,), (0,))) + dot(
        slope_ref[:, half:], w_other_ref[...], ((1,), (0,))
    )
    back_second = spread_back(parts_ref, 4, rows, own + 2 * HALO_BACK)
    slope_second_ref[...] = (back_second * tilt_second_ref[...]).astype(bf16)


def first_kernel(
    own,
    rows,
    slope_second_ref,
    tilt_first_ref,
    patch_first_ref,
    patch_middle_ref,
    w_middle_ref,
    keep_ref,
    send_ref,
    parts_ref,
    terms_ref,
):
    place = position(BLOCKS)[2]
    n_own = own * rows
    slope_second = slope_second_ref[...]
    lo, hi = HALO_BACK * rows, HALO_SECOND * rows
    r_small, middle = terms_ref.shape[1], patch_middle_ref.shape[1]
    grad_middle = dot(
        slope_second[lo : lo + n_own], patch_middle_ref[hi : hi + n_own, :], ((0,), (0,))
    )
    terms_ref[:, :, :middle] = grad_middle.reshape(-1, r_small, middle)
    parts_ref[...] = dot(slope_second, w_middle_ref[...], ((1,), (0,)))
    back_first = spread_back(parts_ref, 2, rows, own)
    slope_first = (back_first * tilt_first_ref[...]).astype(bf16)
    hi = HALO_FIRST * rows
    grad_first = dot(slope_first, patch_first_ref[hi : hi + n_own, :], ((0,), (0,)))
    terms_ref[:, :, middle:] = grad_first.reshape(-1, r_small, grad_first.shape[1])
    for ry in range(2):
        for far in range(FAR):
            at = place ^ (4 * far + 2 * ry)
            keep_ref[far, ry] = terms_ref[at]
            send_ref[far, ry] = terms_ref[at ^ 1].astype(bf16)


def join_kernel(keep_ref, got_ref, sent_ref):
    sent_ref[...] = (keep_ref[...] + got_ref[...].astype(f32)).astype(sent_ref.dtype)


def split_kernel(keep_ref, *refs):
    got_refs, out_refs = refs[:-FAR], refs[-FAR:]
    for i, ref in enumerate(out_refs):
        total = keep_ref[i]
        for got_ref in got_refs:
            total = total + got_ref[i].astype(f32)
        ref[...] = total.astype(ref.dtype)


def add_kernel(keep_ref, got1_ref, got2_ref, got3_ref, kept_ref, send_ref):
    total = keep_ref[...]
    for ref in (got1_ref, got2_ref, got3_ref):
        total = total + ref[...].astype(f32)
    kept_ref[...] = total[0]
    send_ref[...] = total[1].astype(bf16)


def finish_kernel(
    last_ref, got1_ref, got2_ref, got3_ref, small_ref, got_ref, first_ref, middle_ref, out_ref
):
    total = last_ref[...]
    for ref in (got1_ref, got2_ref, got3_ref):
        total = total + ref[...].astype(f32)
    out_ref[...] = total
    small = small_ref[...] + got_ref[...].astype(f32)
    middle_ref[...] = small[:, : middle_ref.shape[1]]
    first_ref[...] = small[:, middle_ref.shape[1] :]


def call(kernel, name, inputs, outs, scratch, flops, spaces=None, semaphores=(), vmem_mib=24, out_spaces=None, aliases=None):
    vmem = pl.BlockSpec(memory_space=pltpu.VMEM)
    spaces = spaces or {}
    return pl.pallas_call(
        kernel,
        in_specs=[spaces.get(i, vmem) for i in range(len(inputs))],
        out_specs=[(out_spaces or {}).get(i, vmem) for i in range(len(outs))],
        input_output_aliases=aliases or {},
        out_shape=[jax.ShapeDtypeStruct(shape, kind) for shape, kind in outs],
        scratch_shapes=[pltpu.VMEM(shape, kind) for shape, kind in scratch] + list(semaphores),
        compiler_params=pltpu.CompilerParams(vmem_limit_bytes=int(vmem_mib * MIB)),
        cost_estimate=pl.CostEstimate(flops=flops, bytes_accessed=1_000_000, transcendentals=0),
        name=name,
    )(*inputs)


def on_device(image_feats, teacher, w_first, w_middle, w_last):
    size = lax.axis_size("cols")
    fold = size // BLOCKS
    height, breadth, channels = teacher.shape
    in_depth = w_first.shape[1] // 9
    hidden = w_middle.shape[1] // 9
    rows, piece = height // 2, breadth // 2
    own = 4 * piece
    total = own * (size // 4)

    if fold > 1:
        w_first, w_middle, w_last = (
            lax.all_gather(w, "cols", axis_index_groups=neighbours(fold), axis=0, tiled=True)
            for w in (w_first, w_middle, w_last)
        )
    r_last, r_small = w_last.shape[0], w_first.shape[0]
    cells = piece * rows
    dealt = cells * len(tiles(channels)) + cells
    packed = r_last * len(tiles(9 * hidden))
    packed += r_small * (len(tiles(9 * hidden)) + len(tiles(9 * in_depth)))
    hbm = pl.BlockSpec(memory_space=pltpu.HBM)
    own_class, near, across, shard = call(
        deal_kernel,
        "deal",
        (image_feats, teacher, w_first, w_middle, w_last),
        [
            ((packed + dealt, LANES), bf16),
            ((dealt, LANES), bf16),
            ((2 * dealt - cells, LANES), bf16),
            ((packed, LANES), bf16),
        ],
        [(a.shape, a.dtype) for a in (image_feats, teacher, w_first, w_middle, w_last)]
        + [((2, cells, piece * height), bf16), ((2, 2, cells, height * breadth), bf16)],
        600_000_000,
        {i: hbm for i in range(5)},
        [pltpu.SemaphoreType.DMA((5,))],
        60,
    )
    across = swap(across, 2)
    far = {k: swap(shard, 4 * k * fold) for k in (1, 2, 3)}
    near = swap(near, 1)
    anywhere = pl.BlockSpec(memory_space=pl.ANY)

    def behind(value, first):
        return call(
            after_kernel,
            "after",
            (value, first),
            [(value.shape, value.dtype)],
            [],
            1_000_000,
            {0: anywhere, 1: anywhere},
            out_spaces={0: anywhere},
            aliases={0: 0},
        )[0]

    diagonal = swap(across, 1)
    held, far[1] = call(
        hold_kernel,
        "hold",
        (own_class, far[1]),
        [(own_class.shape, bf16), (shard.shape, bf16)],
        [],
        1_000_000,
        {1: anywhere},
        out_spaces={1: anywhere},
        aliases={1: 1},
    )
    edge_t, edge_x = HALO_SLOPE * rows, HALO_X * rows
    edge = edge_t * len(tiles(channels)) + edge_x - edge_t
    part_last = r_last * len(tiles(9 * hidden))
    held_last, held_small = call(
        stack_kernel,
        "stack",
        (held, far[3], far[1], far[2]),
        [((FAR, part_last, LANES), bf16), ((FAR, packed - part_last, LANES), bf16)],
        [],
        STACK_COST,
    )
    x_band, t_band, edge_a, edge_b = call(
        functools.partial(collect_kernel, cells, edge_t, edge_x),
        "collect",
        (held, near, across, diagonal),
        [
            ((own * rows, in_depth), bf16),
            ((own * rows, channels), bf16),
            ((edge, LANES), bf16),
            ((edge, LANES), bf16),
        ],
        [],
        1_000_000,
    )

    small_y = swap(held_small, 2 * fold)
    last_y = swap(held_last, 2 * fold)
    all_small = held_small, small_y, swap(held_small, fold), swap(small_y, fold)
    edge_a, edge_b = bands_beside(edge_a, edge_b)

    n_first, n_second, n_slope, n_back = (
        (own + 2 * halo) * rows for halo in (HALO_FIRST, HALO_SECOND, HALO_SLOPE, HALO_BACK)
    )
    tilt_first, tilt_second, patch_first, patch_middle, patch_last, all_middle = call(
        functools.partial(early_kernel, own, rows, total, channels, edge_t),
        "early",
        (x_band, edge_b, edge_a, *all_small),
        [
            ((own * rows, hidden), f32),
            ((n_back, hidden), f32),
            ((n_first, 9 * in_depth), bf16),
            ((n_second, 9 * hidden), bf16),
            ((n_slope, 9 * hidden), bf16),
            ((hidden, 9 * hidden), bf16),
        ],
        [((BLOCKS, 2 * r_small, 9 * hidden), f32)],
        EARLY_COST,
    )
    last_y = behind(last_y, patch_last)
    half = channels // 2
    last_c, last_yc = swap(held_last, fold), swap(last_y, fold)
    w_own, student_own, target = call(
        functools.partial(half_kernel, rows, edge_t),
        "half",
        (t_band, edge_a, edge_b, patch_last, held_last, last_y),
        [
            ((half, 9 * hidden), bf16),
            ((n_slope, half), f32),
            ((n_slope, channels), bf16),
        ],
        [],
        HALF_COST,
    )
    send_y, slope, w_other = call(
        functools.partial(front_kernel, own, rows, total),
        "front",
        (target, patch_last, student_own, last_c, last_yc),
        [
            ((FAR, r_last, 9 * hidden), bf16),
            ((n_slope, channels), bf16),
            ((half, 9 * hidden), bf16),
        ],
        [((n_slope, half), f32)],
        6_000_000_000,
    )
    got_y = swap(send_y, fold)
    quarter = (FAR, r_last, 9 * hidden)
    (keep_y,) = call(
        functools.partial(beside_kernel, own, rows),
        "beside",
        (slope, patch_last),
        [(quarter, f32)],
        [],
        1_000_000_000,
    )
    (last_sent,) = call(join_kernel, "join", (keep_y, got_y), [(quarter, bf16)], [], 1_000_000)
    last_got = swap(last_sent, 2 * fold)
    (slope_second,) = call(
        functools.partial(back_kernel, own, rows),
        "back",
        (slope, tilt_second, w_own, w_other, last_sent),
        [((n_back, hidden), bf16)],
        [((n_slope, 9 * hidden), f32)],
        4_000_000_000,
        {4: anywhere},
    )
    both = 9 * (hidden + in_depth)
    small_keep, small_send = call(
        functools.partial(first_kernel, own, rows),
        "first",
        (slope_second, tilt_first, patch_first, patch_middle, all_middle),
        [((FAR, 2, r_small, both), f32), ((FAR, 2, r_small, both), bf16)],
        [((n_back, 9 * hidden), f32), ((BLOCKS, r_small, both), f32)],
        2_000_000_000,
    )

    keep, send = call(
        functools.partial(stay_kernel, own, rows),
        "stay",
        (slope, patch_last),
        [(quarter, f32), (quarter, bf16)],
        [],
        1_000_000,
    )
    got = swap(send, fold)

    def split(keep, *got):
        shape = keep.shape[1:]
        outs = [(shape, f32)] + [(shape, bf16)] * (FAR - 1)
        return call(split_kernel, "split", (keep, *got), outs, [], 1_000_000)

    parts = split(small_keep, swap(small_send, fold))
    small_got = {k: swap(parts[k], 4 * k * fold) for k in (1, 2, 3)}
    last = split(keep, got, last_got)
    last_got = {k: swap(last[k], 4 * k * fold) for k in (1, 2, 3)}
    small_kept, small_sent = call(
        add_kernel,
        "add",
        (parts[0], small_got[3], small_got[2], small_got[1]),
        [((r_small, both), f32), ((r_small, both), bf16)],
        [],
        1_000_000,
    )
    small_got = swap(small_sent, 2 * fold)
    out_first, out_middle, out_last = call(
        finish_kernel,
        "finish",
        (last[0], last_got[2], last_got[1], last_got[3], small_kept, small_got),
        [(w.shape, f32) for w in (w_first, w_middle, w_last)],
        [],
        1_000_000,
    )
    if fold > 1:
        out_first, out_middle, out_last = (
            lax.psum_scatter(
                out, "cols", scatter_dimension=0, axis_index_groups=neighbours(fold), tiled=True
            )
            for out in (out_first, out_middle, out_last)
        )
    return (out_first, out_middle, out_last)


def solution(mesh):
    placed = (
        P("groups", "cols"),
        P("groups", "cols", None),
        P("cols", None),
        P("cols", None),
        P("cols", None),
    )
    return jax.shard_map(
        on_device,
        mesh=mesh,
        in_specs=placed,
        out_specs=(
            P(("groups", "cols"), None),
            P(("groups", "cols"), None),
            P(("groups", "cols"), None),
        ),
        check_vma=False,
    )
```

```python
import functools

import jax
import jax.numpy as jnp
from jax import lax
from jax.experimental import pallas as pl
from jax.experimental.pallas import tpu as pltpu
from jax.sharding import PartitionSpec as P

epsilon = 1e-06
bf16, f32 = jnp.bfloat16, jnp.float32
MIB = 1024 * 1024
HALO_X, HALO_FIRST, HALO_SECOND, HALO_SLOPE, HALO_BACK = 13, 12, 10, 6, 2
BLOCKS, FAR = 16, 4
LANES = 128
STACK_COST = 2_000_000_000
EARLY_COST = 1_500_000_000
HALF_COST = 1_500_000_000


def swap(array, mask):
    size = lax.axis_size("cols")
    return lax.ppermute(array, "cols", [(i, i ^ mask) for i in range(size)])


def bands_beside(low_pairs, high_pairs):
    size = lax.axis_size("cols")
    bands = size // 4

    def other(i):
        band = i // 4 + (1 if i // 4 % 2 else -1)
        return i ^ 1 if band < 0 or band >= bands else 4 * band + i % 4

    return swap(low_pairs, 4), lax.ppermute(high_pairs, "cols", [(i, other(i)) for i in range(size)])


def neighbours(fold):
    size = lax.axis_size("cols")
    return [list(range(i, i + fold)) for i in range(0, size, fold)]


def position(blocks):
    me = lax.axis_index("cols")
    return me // 4, me % 4, me // (lax.axis_size("cols") // blocks)


def dot(a, b, contract):
    return lax.dot_general(a, b, (contract, ((), ())), preferred_element_type=f32)


def iota(shape, axis):
    return lax.broadcasted_iota(jnp.int32, shape, axis)


def row_shifted(value, step, rows):
    count = value.shape[0]
    if step == 0:
        return value
    row = iota((count, 1), 0) % rows + step
    rolled = pltpu.roll(value, (-step) % count, 0)
    return jnp.where((row >= 0) & (row < rows), rolled, 0.0)


def inside(count, rows, first, total):
    col = iota((count, 1), 0) // rows + first
    return (col >= 0) & (col < total)


def put_patch(patch_ref, value, step, rows, out_cols):
    depth = value.shape[1]
    for ky in range(3):
        moved = row_shifted(value, (ky - 1) * step, rows).astype(bf16)
        for kx in range(3):
            tap = 3 * ky + kx
            start = kx * step * rows
            patch_ref[:, tap * depth : (tap + 1) * depth] = moved[start : start + out_cols * rows]


def spread_back(parts_ref, step, rows, out_cols):
    depth = parts_ref.shape[1] // 9
    total = None
    for ky in range(3):
        line = None
        for kx in range(3):
            tap = 3 * ky + kx
            start = (2 - kx) * step * rows
            piece = parts_ref[start : start + out_cols * rows, tap * depth : (tap + 1) * depth]
            line = piece if line is None else line + piece
        line = row_shifted(line, (1 - ky) * step, rows)
        total = line if total is None else total + line
    return total


def deal_kernel(
    x_hbm,
    teacher_hbm,
    w_first_hbm,
    w_middle_hbm,
    w_last_hbm,
    own_ref,
    near_ref,
    across_ref,
    shard_ref,
    x_ref,
    teacher_ref,
    w_first_ref,
    w_middle_ref,
    w_last_ref,
    pick_x_ref,
    pick_t_ref,
    arrived,
):
    copies = [
        pltpu.make_async_copy(source, target, arrived.at[i])
        for i, (source, target) in enumerate(
            (
                (teacher_hbm, teacher_ref),
                (x_hbm, x_ref),
                (w_last_hbm, w_last_ref),
                (w_middle_hbm, w_middle_ref),
                (w_first_hbm, w_first_ref),
            )
        )
    ]
    for copy in copies:
        copy.start()
    height, breadth, channels = teacher_ref.shape
    depth = x_ref.shape[1] // breadth
    rows, piece = height // 2, breadth // 2
    cells = rows * piece
    low = position(BLOCKS)[1]
    core, row = low % 2, low // 2
    out = iota((cells, 1), 0)
    col, line = out // rows, out % rows
    for rc in range(2):
        line_of = 2 * line + (core ^ rc)
        pick_x_ref[rc] = (iota((cells, piece * height), 1) == col * height + line_of).astype(f32).astype(bf16)
        for ry in range(2):
            source = line_of * breadth + 2 * col + (row ^ ry)
            pick_t_ref[rc, ry] = (iota((cells, height * breadth), 1) == source).astype(f32).astype(bf16)
    for copy in copies:
        copy.wait()
    at = put_tiles(shard_ref, 0, w_last_ref[...])
    at = put_tiles(shard_ref, at, w_middle_ref[...])
    put_tiles(shard_ref, at, w_first_ref[...])
    own_ref[: shard_ref.shape[0]] = shard_ref[...]
    field = teacher_ref[...].reshape(height * breadth, channels)
    pairs = jnp.concatenate(
        [x_ref[:, 2 * depth * i : 2 * depth * (i + 1)] for i in range(piece)], 0
    )
    x_parts = []
    for rc, out_ref in ((0, own_ref), (1, near_ref)):
        both = dot(pick_x_ref[rc], pairs, ((1,), (0,))).astype(bf16)
        low, high = both[:, :depth], both[:, depth:]
        x_parts.append(jnp.where(row == 0, high, low))
        across = dot(pick_t_ref[rc, 1], field, ((1,), (0,))).astype(bf16)
        put_tiles(across_ref, rc * cells * len(tiles(channels)), across)
        value = dot(pick_t_ref[rc, 0], field, ((1,), (0,))).astype(bf16)
        at = put_tiles(out_ref, out_ref.shape[0] - near_ref.shape[0], value)
        x = jnp.where(row == 0, low, high)
        out_ref[at:, :] = jnp.concatenate([x, jnp.zeros_like(x)], 1)
    across_ref[across_ref.shape[0] - cells :, :] = jnp.concatenate(x_parts, 1)


def tiles(width):
    return [(start, min(LANES, width - start)) for start in range(0, width, LANES)]


def put_tiles(ref, at, value):
    rows, width = value.shape
    for start, size in tiles(width):
        ref[at : at + rows, :size] = value[:, start : start + size]
        at += rows
    return at


def take_tiles(value, at, rows, width):
    return jnp.concatenate(
        [
            value[at + i * rows : at + (i + 1) * rows, :size]
            for i, (_, size) in enumerate(tiles(width))
        ],
        1,
    )


def hold_kernel(own_ref, far_ref, held_ref, same_ref):
    held_ref[...] = own_ref[...]


def stack_kernel(own_ref, far3_ref, far1_ref, far2_ref, last_ref, small_ref):
    cut, end = last_ref.shape[1], last_ref.shape[1] + small_ref.shape[1]
    for far, ref in enumerate((own_ref, far1_ref, far2_ref, far3_ref)):
        last_ref[far] = ref[:cut]
        small_ref[far] = ref[cut:end]


def after_kernel(value_ref, first_ref, same_ref):
    pass


def collect_kernel(
    cells,
    edge_t,
    edge_x,
    own_ref,
    near_ref,
    across_ref,
    diagonal_ref,
    x_ref,
    teacher_ref,
    edge_a_ref,
    edge_b_ref,
):
    depth, channels = x_ref.shape[1], teacher_ref.shape[1]
    low = position(BLOCKS)[1]
    part = cells * len(tiles(channels))
    skip = own_ref.shape[0] - near_ref.shape[0]
    pieces = ((own_ref, skip, 0), (near_ref, 0, 0), (across_ref, 0, 0), (diagonal_ref, part, depth))
    for k, (ref, row, lane) in enumerate(pieces):
        at = pl.ds(pl.multiple_of((low ^ k) * cells, cells), cells)
        x_ref[at, :] = ref[ref.shape[0] - cells :, lane : lane + depth]
        for lanes, size in tiles(channels):
            teacher_ref[at, lanes : lanes + size] = ref[row : row + cells, :]
            row += cells
    own = teacher_ref.shape[0]
    half = edge_x - edge_t
    odd = position(BLOCKS)[0] % 2
    for ref, high in ((edge_a_ref, 1 - odd), (edge_b_ref, odd)):
        at = pl.ds(pl.multiple_of(high * (own - edge_t), 16), edge_t)
        row = put_tiles(ref, 0, teacher_ref[at, :])
        at = high * (own - edge_x)
        ref[row:, :] = jnp.concatenate(
            [
                x_ref[pl.ds(pl.multiple_of(at, 16), half), :],
                x_ref[pl.ds(pl.multiple_of(at + edge_t, 16), half), :],
            ],
            1,
        )


def sides(edge_a_ref, edge_b_ref):
    a, b = edge_a_ref[...], edge_b_ref[...]
    group, bands = position(BLOCKS)[0], lax.axis_size("cols") // 4
    odd = group % 2 == 1
    before, after = jnp.where(odd, a, b), jnp.where(odd, b, a)
    zero = jnp.zeros_like(a)
    return jnp.where(group == 0, zero, before), jnp.where(group == bands - 1, zero, after)


def edge_x_cells(edge, edge_t, channels):
    packed = edge[edge_t * len(tiles(channels)) :, :]
    depth = LANES // 2
    overlap = packed.shape[0] - edge_t
    return jnp.concatenate([packed[:, :depth], packed[overlap:, depth:]], 0)


def early_kernel(
    own,
    rows,
    total,
    channels,
    edge_t,
    x_ref,
    edge_b_ref,
    edge_a_ref,
    h_ref,
    hy_ref,
    hc_ref,
    hyc_ref,
    tilt_first_ref,
    tilt_second_ref,
    patch_first_ref,
    patch_middle_ref,
    patch_last_ref,
    w_middle_ref,
    small_ref,
):
    group, _, place = position(BLOCKS)
    first_col = group * own
    r_small = small_ref.shape[1] // 2
    in_taps, taps = patch_first_ref.shape[1], patch_middle_ref.shape[1]
    for near, ref in enumerate((h_ref, hc_ref, hy_ref, hyc_ref)):
        for far in range(FAR):
            at = place ^ (4 * far + near)
            small = ref[far].astype(f32)
            row = 0
            for first, width in ((0, taps), (r_small, in_taps)):
                for start, size in tiles(width):
                    small_ref[at, first : first + r_small, start : start + size] = small[
                        row : row + r_small, :size
                    ]
                    row += r_small
    small = small_ref[...]
    w_middle_ref[...] = small[:, :r_small].reshape(-1, taps).astype(bf16)
    w_first = small[:, r_small:, :in_taps].reshape(-1, in_taps).astype(bf16)

    n_first, n_second, n_slope = (
        own + 2 * HALO_FIRST,
        own + 2 * HALO_SECOND,
        own + 2 * HALO_SLOPE,
    )
    before, after = sides(edge_a_ref, edge_b_ref)
    wide = jnp.concatenate(
        [
            edge_x_cells(before, edge_t, channels),
            x_ref[...],
            edge_x_cells(after, edge_t, channels),
        ],
        0,
    )
    put_patch(patch_first_ref, wide.astype(f32), 1, rows, n_first)
    pre = dot(patch_first_ref[...], w_first, ((1,), (1,)))
    sigma = 1.0 / (1.0 + jnp.exp(-pre))
    act = jnp.where(
        inside(n_first * rows, rows, first_col - HALO_FIRST, total), pre * sigma, 0.0
    )
    lo = HALO_FIRST * rows
    pre_own, sigma_own = pre[lo : lo + own * rows], sigma[lo : lo + own * rows]
    tilt_first_ref[...] = sigma_own * (1.0 + pre_own * (1.0 - sigma_own))
    put_patch(patch_middle_ref, act, 2, rows, n_second)

    pre = dot(patch_middle_ref[...], w_middle_ref[...], ((1,), (1,)))
    sigma = 1.0 / (1.0 + jnp.exp(-pre))
    act = jnp.where(
        inside(n_second * rows, rows, first_col - HALO_SECOND, total), pre * sigma, 0.0
    )
    lo, n_back = (HALO_SECOND - HALO_BACK) * rows, (own + 2 * HALO_BACK) * rows
    pre_back, sigma_back = pre[lo : lo + n_back], sigma[lo : lo + n_back]
    tilt_second_ref[...] = jnp.where(
        inside(n_back, rows, first_col - HALO_BACK, total),
        sigma_back * (1.0 + pre_back * (1.0 - sigma_back)),
        0.0,
    )
    put_patch(patch_last_ref, act, 4, rows, n_slope)


def put_blocks(w_ref, blocks, r_last):
    taps = w_ref.shape[1]
    for i, (ref, far) in enumerate(blocks):
        for j, (start, size) in enumerate(tiles(taps)):
            w_ref[i * r_last : (i + 1) * r_last, start : start + size] = ref[
                far, j * r_last : (j + 1) * r_last
            ]


def half_kernel(
    rows,
    edge_t,
    teacher_ref,
    edge_a_ref,
    edge_b_ref,
    patch_last_ref,
    h_ref,
    hy_ref,
    w_own_ref,
    student_ref,
    target_ref,
):
    place = position(BLOCKS)[2]
    channels = teacher_ref.shape[1]
    r_last = channels // BLOCKS
    put_blocks(w_own_ref, [(ref, far) for ref in (h_ref, hy_ref) for far in range(FAR)], r_last)
    student_ref[...] = dot(patch_last_ref[...], w_own_ref[...], ((1,), (1,)))
    before, after = sides(edge_a_ref, edge_b_ref)
    wide = jnp.concatenate(
        [
            take_tiles(before, 0, edge_t, channels),
            teacher_ref[...],
            take_tiles(after, 0, edge_t, channels),
        ],
        0,
    )
    out = iota((1, channels), 1)
    block = out // r_last
    key = 4 * (block % FAR) + 2 * (block // FAR % 2) + block // (2 * FAR)
    source = (key ^ place) * r_last + out % r_last
    pick = (iota((channels, channels), 0) == source).astype(f32).astype(bf16)
    target_ref[...] = dot(wide, pick, ((1,), (0,))).astype(bf16)


def front_kernel(
    own,
    rows,
    total,
    target_ref,
    patch_last_ref,
    student_own_ref,
    hc_ref,
    hyc_ref,
    send_y_ref,
    slope_ref,
    w_other_ref,
    student_ref,
):
    first_col = position(BLOCKS)[0] * own
    channels = slope_ref.shape[1]
    half = channels // 2
    put_blocks(
        w_other_ref, [(ref, far) for ref in (hc_ref, hyc_ref) for far in range(FAR)], channels // BLOCKS
    )
    student_ref[...] = dot(patch_last_ref[...], w_other_ref[...], ((1,), (1,)))
    block = 4 * rows
    for step in range(slope_ref.shape[0] // block):
        at = pl.ds(step * block, block)
        parts = [
            (student, target_ref[at, lane : lane + half].astype(f32), lane)
            for student, lane in ((student_own_ref[at, :], 0), (student_ref[at, :], half))
        ]

        def total_of(product):
            return sum(jnp.sum(product(s, t), -1, keepdims=True) for s, t, _ in parts)

        s_inv = lax.rsqrt(total_of(lambda s, t: s * s) + epsilon)
        t_inv = lax.rsqrt(total_of(lambda s, t: t * t) + epsilon)
        cosine = total_of(lambda s, t: s * t) * (s_inv * t_inv)
        ok = inside(block, rows, first_col - HALO_SLOPE + step * (block // rows), total)
        s_part = jnp.where(ok, s_inv * s_inv * (cosine + epsilon * (s_inv * s_inv)), 0.0)
        t_part = jnp.where(ok, s_inv * t_inv, 0.0)
        for student, target, lane in parts:
            slope_ref[at, lane : lane + half] = (student * s_part - target * t_part).astype(bf16)

    lo, n_own = HALO_SLOPE * rows, own * rows
    first = half + half // 2
    terms = dot(
        slope_ref[lo : lo + n_own, first:], patch_last_ref[lo : lo + n_own, :], ((0,), (0,))
    )
    send_y_ref[...] = terms.astype(bf16).reshape(send_y_ref.shape)


def beside_kernel(own, rows, slope_ref, patch_last_ref, keep_y_ref):
    half, lo, n_own = slope_ref.shape[1] // 2, HALO_SLOPE * rows, own * rows
    terms = dot(
        slope_ref[lo : lo + n_own, half // 2 : half],
        patch_last_ref[lo : lo + n_own, :],
        ((0,), (0,)),
    )
    keep_y_ref[...] = terms.reshape(keep_y_ref.shape)


def stay_kernel(own, rows, slope_ref, patch_last_ref, keep_ref, send_ref):
    half, lo, n_own = slope_ref.shape[1] // 2, HALO_SLOPE * rows, own * rows
    stays = jnp.concatenate(
        [slope_ref[lo : lo + n_own, first : first + half // 2] for first in (0, half)], 1
    )
    terms = dot(stays, patch_last_ref[lo : lo + n_own, :], ((0,), (0,)))
    terms = terms.reshape((2,) + keep_ref.shape)
    keep_ref[...] = terms[0]
    send_ref[...] = terms[1].astype(bf16)


def back_kernel(
    own,
    rows,
    slope_ref,
    tilt_second_ref,
    w_own_ref,
    w_other_ref,
    tie_ref,
    slope_second_ref,
    parts_ref,
):
    half = w_own_ref.shape[0]
    parts_ref[...] = dot(slope_ref[:, :half], w_own_ref[...], ((1,), (0,))) + dot(
        slope_ref[:, half:], w_other_ref[...], ((1,), (0,))
    )
    back_second = spread_back(parts_ref, 4, rows, own + 2 * HALO_BACK)
    slope_second_ref[...] = (back_second * tilt_second_ref[...]).astype(bf16)


def first_kernel(
    own,
    rows,
    slope_second_ref,
    tilt_first_ref,
    patch_first_ref,
    patch_middle_ref,
    w_middle_ref,
    keep_ref,
    send_ref,
    parts_ref,
    terms_ref,
):
    place = position(BLOCKS)[2]
    n_own = own * rows
    slope_second = slope_second_ref[...]
    lo, hi = HALO_BACK * rows, HALO_SECOND * rows
    r_small, middle = terms_ref.shape[1], patch_middle_ref.shape[1]
    grad_middle = dot(
        slope_second[lo : lo + n_own], patch_middle_ref[hi : hi + n_own, :], ((0,), (0,))
    )
    terms_ref[:, :, :middle] = grad_middle.reshape(-1, r_small, middle)
    parts_ref[...] = dot(slope_second, w_middle_ref[...], ((1,), (0,)))
    back_first = spread_back(parts_ref, 2, rows, own)
    slope_first = (back_first * tilt_first_ref[...]).astype(bf16)
    hi = HALO_FIRST * rows
    grad_first = dot(slope_first, patch_first_ref[hi : hi + n_own, :], ((0,), (0,)))
    terms_ref[:, :, middle:] = grad_first.reshape(-1, r_small, grad_first.shape[1])
    for ry in range(2):
        for far in range(FAR):
            at = place ^ (4 * far + 2 * ry)
            keep_ref[far, ry] = terms_ref[at]
            send_ref[far, ry] = terms_ref[at ^ 1].astype(bf16)


def join_kernel(keep_ref, got_ref, sent_ref):
    sent_ref[...] = (keep_ref[...] + got_ref[...].astype(f32)).astype(sent_ref.dtype)


def split_kernel(keep_ref, *refs):
    got_refs, out_refs = refs[:-FAR], refs[-FAR:]
    for i, ref in enumerate(out_refs):
        total = keep_ref[i]
        for got_ref in got_refs:
            total = total + got_ref[i].astype(f32)
        ref[...] = total.astype(ref.dtype)


def add_kernel(keep_ref, got1_ref, got2_ref, got3_ref, kept_ref, send_ref):
    total = keep_ref[...]
    for ref in (got1_ref, got2_ref, got3_ref):
        total = total + ref[...].astype(f32)
    kept_ref[...] = total[0]
    send_ref[...] = total[1].astype(bf16)


def finish_kernel(
    last_ref, got1_ref, got2_ref, got3_ref, small_ref, got_ref, first_ref, middle_ref, out_ref
):
    total = last_ref[...]
    for ref in (got1_ref, got2_ref, got3_ref):
        total = total + ref[...].astype(f32)
    out_ref[...] = total
    small = small_ref[...] + got_ref[...].astype(f32)
    middle_ref[...] = small[:, : middle_ref.shape[1]]
    first_ref[...] = small[:, middle_ref.shape[1] :]


def call(kernel, name, inputs, outs, scratch, flops, spaces=None, semaphores=(), vmem_mib=24, out_spaces=None, aliases=None):
    vmem = pl.BlockSpec(memory_space=pltpu.VMEM)
    spaces = spaces or {}
    return pl.pallas_call(
        kernel,
        in_specs=[spaces.get(i, vmem) for i in range(len(inputs))],
        out_specs=[(out_spaces or {}).get(i, vmem) for i in range(len(outs))],
        input_output_aliases=aliases or {},
        out_shape=[jax.ShapeDtypeStruct(shape, kind) for shape, kind in outs],
        scratch_shapes=[pltpu.VMEM(shape, kind) for shape, kind in scratch] + list(semaphores),
        compiler_params=pltpu.CompilerParams(vmem_limit_bytes=int(vmem_mib * MIB)),
        cost_estimate=pl.CostEstimate(flops=flops, bytes_accessed=1_000_000, transcendentals=0),
        name=name,
    )(*inputs)


def on_device(image_feats, teacher, w_first, w_middle, w_last):
    size = lax.axis_size("cols")
    fold = size // BLOCKS
    height, breadth, channels = teacher.shape
    in_depth = w_first.shape[1] // 9
    hidden = w_middle.shape[1] // 9
    rows, piece = height // 2, breadth // 2
    own = 4 * piece
    total = own * (size // 4)

    if fold > 1:
        w_first, w_middle, w_last = (
            lax.all_gather(w, "cols", axis_index_groups=neighbours(fold), axis=0, tiled=True)
            for w in (w_first, w_middle, w_last)
        )
    r_last, r_small = w_last.shape[0], w_first.shape[0]
    cells = piece * rows
    dealt = cells * len(tiles(channels)) + cells
    packed = r_last * len(tiles(9 * hidden))
    packed += r_small * (len(tiles(9 * hidden)) + len(tiles(9 * in_depth)))
    hbm = pl.BlockSpec(memory_space=pltpu.HBM)
    own_class, near, across, shard = call(
        deal_kernel,
        "deal",
        (image_feats, teacher, w_first, w_middle, w_last),
        [
            ((packed + dealt, LANES), bf16),
            ((dealt, LANES), bf16),
            ((2 * dealt - cells, LANES), bf16),
            ((packed, LANES), bf16),
        ],
        [(a.shape, a.dtype) for a in (image_feats, teacher, w_first, w_middle, w_last)]
        + [((2, cells, piece * height), bf16), ((2, 2, cells, height * breadth), bf16)],
        600_000_000,
        {i: hbm for i in range(5)},
        [pltpu.SemaphoreType.DMA((5,))],
        60,
    )
    across = swap(across, 2)
    far = {k: swap(shard, 4 * k * fold) for k in (1, 2, 3)}
    near = swap(near, 1)
    anywhere = pl.BlockSpec(memory_space=pl.ANY)

    def behind(value, first):
        return call(
            after_kernel,
            "after",
            (value, first),
            [(value.shape, value.dtype)],
            [],
            1_000_000,
            {0: anywhere, 1: anywhere},
            out_spaces={0: anywhere},
            aliases={0: 0},
        )[0]

    diagonal = swap(across, 1)
    held, far[1] = call(
        hold_kernel,
        "hold",
        (own_class, far[1]),
        [(own_class.shape, bf16), (shard.shape, bf16)],
        [],
        1_000_000,
        {1: anywhere},
        out_spaces={1: anywhere},
        aliases={1: 1},
    )
    edge_t, edge_x = HALO_SLOPE * rows, HALO_X * rows
    edge = edge_t * len(tiles(channels)) + edge_x - edge_t
    part_last = r_last * len(tiles(9 * hidden))
    held_last, held_small = call(
        stack_kernel,
        "stack",
        (held, far[3], far[1], far[2]),
        [((FAR, part_last, LANES), bf16), ((FAR, packed - part_last, LANES), bf16)],
        [],
        STACK_COST,
    )
    x_band, t_band, edge_a, edge_b = call(
        functools.partial(collect_kernel, cells, edge_t, edge_x),
        "collect",
        (held, near, across, diagonal),
        [
            ((own * rows, in_depth), bf16),
            ((own * rows, channels), bf16),
            ((edge, LANES), bf16),
            ((edge, LANES), bf16),
        ],
        [],
        1_000_000,
    )

    small_y = swap(held_small, 2 * fold)
    last_y = swap(held_last, 2 * fold)
    all_small = held_small, small_y, swap(held_small, fold), swap(small_y, fold)
    edge_a, edge_b = bands_beside(edge_a, edge_b)

    n_first, n_second, n_slope, n_back = (
        (own + 2 * halo) * rows for halo in (HALO_FIRST, HALO_SECOND, HALO_SLOPE, HALO_BACK)
    )
    tilt_first, tilt_second, patch_first, patch_middle, patch_last, all_middle = call(
        functools.partial(early_kernel, own, rows, total, channels, edge_t),
        "early",
        (x_band, edge_b, edge_a, *all_small),
        [
            ((own * rows, hidden), f32),
            ((n_back, hidden), f32),
            ((n_first, 9 * in_depth), bf16),
            ((n_second, 9 * hidden), bf16),
            ((n_slope, 9 * hidden), bf16),
            ((hidden, 9 * hidden), bf16),
        ],
        [((BLOCKS, 2 * r_small, 9 * hidden), f32)],
        EARLY_COST,
    )
    last_y = behind(last_y, patch_last)
    half = channels // 2
    last_c, last_yc = swap(held_last, fold), swap(last_y, fold)
    w_own, student_own, target = call(
        functools.partial(half_kernel, rows, edge_t),
        "half",
        (t_band, edge_a, edge_b, patch_last, held_last, last_y),
        [
            ((half, 9 * hidden), bf16),
            ((n_slope, half), f32),
            ((n_slope, channels), bf16),
        ],
        [],
        HALF_COST,
    )
    send_y, slope, w_other = call(
        functools.partial(front_kernel, own, rows, total),
        "front",
        (target, patch_last, student_own, last_c, last_yc),
        [
            ((FAR, r_last, 9 * hidden), bf16),
            ((n_slope, channels), bf16),
            ((half, 9 * hidden), bf16),
        ],
        [((n_slope, half), f32)],
        6_000_000_000,
    )
    got_y = swap(send_y, fold)
    quarter = (FAR, r_last, 9 * hidden)
    (keep_y,) = call(
        functools.partial(beside_kernel, own, rows),
        "beside",
        (slope, patch_last),
        [(quarter, f32)],
        [],
        1_000_000_000,
    )
    (last_sent,) = call(join_kernel, "join", (keep_y, got_y), [(quarter, bf16)], [], 1_000_000)
    last_got = swap(last_sent, 2 * fold)
    (slope_second,) = call(
        functools.partial(back_kernel, own, rows),
        "back",
        (slope, tilt_second, w_own, w_other, last_sent),
        [((n_back, hidden), bf16)],
        [((n_slope, 9 * hidden), f32)],
        4_000_000_000,
        {4: anywhere},
    )
    both = 9 * (hidden + in_depth)
    small_keep, small_send = call(
        functools.partial(first_kernel, own, rows),
        "first",
        (slope_second, tilt_first, patch_first, patch_middle, all_middle),
        [((FAR, 2, r_small, both), f32), ((FAR, 2, r_small, both), bf16)],
        [((n_back, 9 * hidden), f32), ((BLOCKS, r_small, both), f32)],
        2_000_000_000,
    )

    keep, send = call(
        functools.partial(stay_kernel, own, rows),
        "stay",
        (slope, patch_last),
        [(quarter, f32), (quarter, bf16)],
        [],
        1_000_000,
    )
    got = swap(send, fold)

    def split(keep, *got):
        shape = keep.shape[1:]
        outs = [(shape, f32)] + [(shape, bf16)] * (FAR - 1)
        return call(split_kernel, "split", (keep, *got), outs, [], 1_000_000)

    parts = split(small_keep, swap(small_send, fold))
    small_got = {k: swap(parts[k], 4 * k * fold) for k in (1, 2, 3)}
    last = split(keep, got, last_got)
    last_got = {k: swap(last[k], 4 * k * fold) for k in (1, 2, 3)}
    small_kept, small_sent = call(
        add_kernel,
        "add",
        (parts[0], small_got[3], small_got[2], small_got[1]),
        [((r_small, both), f32), ((r_small, both), bf16)],
        [],
        1_000_000,
    )
    small_got = swap(small_sent, 2 * fold)
    out_first, out_middle, out_last = call(
        finish_kernel,
        "finish",
        (last[0], last_got[2], last_got[1], last_got[3], small_kept, small_got),
        [(w.shape, f32) for w in (w_first, w_middle, w_last)],
        [],
        1_000_000,
    )
    if fold > 1:
        out_first, out_middle, out_last = (
            lax.psum_scatter(
                out, "cols", scatter_dimension=0, axis_index_groups=neighbours(fold), tiled=True
            )
            for out in (out_first, out_middle, out_last)
        )
    return (out_first, out_middle, out_last)


def solution(mesh):
    placed = (
        P("groups", "cols"),
        P("groups", "cols", None),
        P("cols", None),
        P("cols", None),
        P("cols", None),
    )
    return jax.shard_map(
        on_device,
        mesh=mesh,
        in_specs=placed,
        out_specs=(
            P(("groups", "cols"), None),
            P(("groups", "cols"), None),
            P(("groups", "cols"), None),
        ),
        check_vma=False,
    )
```
